256 devices in a mesh: tm: 16 (over z_hi, y), space: 16 (over z_lo, x, core).
Axes of the slice: x: 4, y: 4, z: 8 (z_hi: 4, z_lo: 2; z = z_hi * 2 + z_lo), core: 2. Of those that a mesh axis runs over, the one named last changes fastest.
Arguments:
- tokens: bfloat16 [384, 256, 1024], P('tm', 'space'), may hold values from -60 to 60
- cotangent: bfloat16 [384, 256, 1024], P('tm', 'space'), may hold values from -6 to 6
- norm_gain: float32 [1024], replicated, may hold values from 0.1 to 1.9
- query_weight: bfloat16 [1024, 1024], replicated, may hold values from -5.25 to 5.25
- key_weight: bfloat16 [1024, 1024], replicated, may hold values from -1 to 1
- value_weight: bfloat16 [1024, 1024], replicated, may hold values from -0.1875 to 0.1875
- out_weight: bfloat16 [1024, 1024], replicated, may hold values from -0.1875 to 0.1875
Outputs:
- grad_tokens: bfloat16 [384, 256, 1024], P('tm', 'space')
- weight_grads: float32 [1024, 4096], P(None, ('tm', 'space'))
The draws below stay inside these ranges and needn't reach their ends.
All inputs are finite; a program needn't handle non-finite values.
Results may differ from the reference program's by a relative error of at most 0.014.
The reference program's roundings to bfloat16 on the way (of `normed`, `weights_low`, `mixed`, `grad_mixed`, `grad_value` and `grad_scores`) count: a program that leaves them out, or rounds other values in their place, can miss the bound.
Values may be sent and summed in bfloat16 or wider, within the bound.
A program may use at most 128 MiB of HBM per device.

```python
import math
import jax
import jax.numpy as jnp
from jax import lax

D = 1024
H = 16
FRAMES = 384
POS = 256
ROWS = 98304


def shared_keys(key):
    return jax.random.truncated_normal(key, -4.0, 4.0, (D, D), jnp.float32) * D ** (-0.5)


def draw_key_weight(key, part):
    base = shared_keys(key)
    return base.astype(jnp.bfloat16)


def draw_query_weight(key, part):
    key = jax.random.fold_in(key, 12)
    own = jax.random.truncated_normal(key, -4.0, 4.0, (D, D), jnp.float32) * D ** (-0.5)
    return own.astype(jnp.bfloat16)


def draw_tokens(key, part):
    key = jax.random.fold_in(key, 13)
    return jnp.clip(jax.random.normal(key, (FRAMES, POS, D), jnp.float32), -6.0, 6.0).astype(jnp.bfloat16)


def raised(array, own_key, source, target, parts, factor):
    def block_of(dim):
        return (jnp.arange(array.shape[dim]) // (array.shape[dim] // parts)).reshape((-1,) + (1,) * (array.ndim - 1 - dim))

    one_side = jax.random.permutation(own_key, parts)[block_of(target)]
    far = (block_of(target) + parts // 2) % parts
    return jnp.where((block_of(source) == one_side) | (block_of(source) == far), factor * array, array)


def steps_of(stream_key, dims, cuts, least, high):
    def one(dim, blocks):
        steps = jax.random.uniform(jax.random.fold_in(jax.random.fold_in(stream_key, 6), dim), (blocks,), jnp.float32, least / len(cuts), high / len(cuts))
        return jnp.repeat(jnp.exp(steps), dims[dim] // blocks).reshape((-1,) + (1,) * (len(dims) - dim - 1))

    loudness = one(*cuts[0])
    for cut in cuts[1:]:
        loudness = loudness * one(*cut)
    return loudness


def normal_values(key, shape, width, reach, pieces=(), held_as=jnp.bfloat16):
    values = width * jax.random.normal(key, shape, jnp.float32)
    if pieces:
        values = values * steps_of(key, shape, pieces, -0.22, 0.18)
    return jnp.clip(values, -reach, reach).astype(held_as)


def bell_draw_with(stream_key, extent, deviation, reach, cuts, heavy, held_as=jnp.bfloat16):
    result = deviation * jax.random.normal(stream_key, extent, jnp.float32)
    if cuts:
        result = result * steps_of(stream_key, extent, cuts, -0.22, 0.18)
    return jnp.clip(raised(result, jax.random.fold_in(stream_key, 3), *heavy), -reach, reach).astype(held_as)


def setup_inputs(seed: int = 0) -> dict:
    arg_keys = jax.random.split(jax.random.key(seed), 8)
    return {
        "tokens": draw_tokens(jax.random.fold_in(arg_keys[7], 71), 0),
        "cotangent": bell_draw_with(arg_keys[1], (FRAMES, POS, D), 1.0, 6.0, ((0, 16), (1, 16)), (0, 2, 16, 2.0)),
        "norm_gain": jnp.clip(1.0 + 0.18 * jax.random.normal(arg_keys[2], (D,), jnp.float32), 0.1, 1.9),
        "query_weight": draw_query_weight(jax.random.fold_in(arg_keys[7], 71), 0),
        "key_weight": draw_key_weight(jax.random.fold_in(arg_keys[7], 71), 0),
        "value_weight": normal_values(arg_keys[5], (D, D), D ** -0.5, 0.1875),
        "out_weight": normal_values(arg_keys[6], (D, D), D ** -0.5, 0.1875),
    }


EPS = 1e-06

def heads_of(matrix):
    held = lax.optimization_barrier(matrix)
    return held.reshape(held.shape[0], H, -1).astype(jnp.float32)

def lowered(values):
    return lax.optimization_barrier(values.astype(jnp.bfloat16)).astype(jnp.float32)

def times_transposed(left, right):
    return lax.dot_general(left, right, (((1,), (1,)), ((), ())), preferred_element_type=jnp.float32)

def transposed_times(left, right):
    return lax.dot_general(left, right, (((0,), (0,)), ((), ())), preferred_element_type=jnp.float32)

def position_grads(x_rows, dy_rows, norm_gain, query_weight, key_weight, value_weight, out_weight):
    floated = x_rows.astype(jnp.float32)
    centred = floated - lax.optimization_barrier(jnp.mean(floated, -1, keepdims=True))
    variance = lax.optimization_barrier(jnp.mean(centred * centred, -1, keepdims=True))
    inv_scale = lax.rsqrt(variance + EPS)
    standard = centred * inv_scale
    normed = (standard * norm_gain).astype(jnp.bfloat16)
    query = jnp.dot(normed, query_weight, preferred_element_type=jnp.float32).astype(jnp.bfloat16)
    key_rows = jnp.dot(normed, key_weight, preferred_element_type=jnp.float32).astype(jnp.bfloat16)
    value = jnp.dot(normed, value_weight, preferred_element_type=jnp.float32).astype(jnp.bfloat16)
    head_size = query.shape[1] // H
    query_heads = heads_of(query)
    key_heads = heads_of(key_rows)
    value_heads = heads_of(value)
    scores = jnp.einsum('fhe,ghe->hfg', query_heads, key_heads) / math.sqrt(head_size)
    weights = jax.nn.softmax(scores, axis=-1)
    weights_low = lowered(weights)
    mixed = jnp.einsum('hfg,ghe->fhe', weights_low, value_heads).reshape(query.shape).astype(jnp.bfloat16)
    grad_mixed = times_transposed(dy_rows, out_weight).astype(jnp.bfloat16)
    mixed_heads = heads_of(grad_mixed)
    grad_weights = jnp.einsum('fhe,ghe->hfg', mixed_heads, value_heads)
    grad_value = jnp.einsum('hfg,fhe->ghe', weights_low, mixed_heads).reshape(query.shape).astype(jnp.bfloat16)
    delta_row = lax.optimization_barrier(jnp.sum(weights * grad_weights, -1, keepdims=True))
    grad_scores = lowered(weights * (grad_weights - delta_row) / math.sqrt(head_size))
    grad_query = jnp.einsum('hfg,ghe->fhe', grad_scores, key_heads).reshape(query.shape).astype(jnp.bfloat16)
    grad_key = jnp.einsum('hfg,fhe->ghe', grad_scores, query_heads).reshape(query.shape).astype(jnp.bfloat16)
    grads = jnp.concatenate([transposed_times(normed, grad_query), transposed_times(normed, grad_key), transposed_times(normed, grad_value), transposed_times(mixed, dy_rows)], axis=1)
    grad_normed = times_transposed(grad_query, query_weight) + times_transposed(grad_key, key_weight) + times_transposed(grad_value, value_weight)
    grad_standard = grad_normed * norm_gain
    grad_x = dy_rows.astype(jnp.float32) + inv_scale * (grad_standard - lax.optimization_barrier(jnp.mean(grad_standard, -1, keepdims=True)) - standard * lax.optimization_barrier(jnp.mean(grad_standard * standard, -1, keepdims=True)))
    return (grad_x.astype(jnp.bfloat16), grads)

def reference(tokens, cotangent, norm_gain, query_weight, key_weight, value_weight, out_weight):

    def advance(total, pair):
        grad_rows, grads = position_grads(pair[0], pair[1], norm_gain, query_weight, key_weight, value_weight, out_weight)
        return (total + grads, grad_rows)
    start = jnp.zeros((D, 4 * D), jnp.float32)
    total, grad_rows = lax.scan(advance, start, (jnp.transpose(tokens, (1, 0, 2)), jnp.transpose(cotangent, (1, 0, 2))))
    return (jnp.transpose(grad_rows, (1, 0, 2)), total * (1.0 / math.sqrt(ROWS)))
```

```python
import functools
import math

import jax
import jax.numpy as jnp
from jax import lax
from jax.experimental import pallas as pl
from jax.experimental.pallas import tpu as pltpu
from jax.sharding import PartitionSpec as P

H = 16
D = 1024
EPS = 1e-06
MESH = pl.DeviceIdType.MESH
BF16 = jnp.bfloat16
F32 = jnp.float32


def times_transposed(left, right):
    return lax.dot_general(
        left, right, (((1,), (1,)), ((), ())), preferred_element_type=jnp.float32
    )


def place():
    tm = lax.axis_index("tm")
    space = lax.axis_index("space")
    return (
        (tm // 4) * 2 + space // 8,
        tm % 4,
        (space // 2) % 4,
        space % 2,
    )


def device(z, y, x, core):
    return ((z // 2) * 4 + y, ((z % 2) * 4 + x) * 2 + core)


def remote(src, dst, send, recv, to):
    return pltpu.make_async_remote_copy(
        src_ref=src, dst_ref=dst, send_sem=send, recv_sem=recv, device_id=to, device_id_type=MESH
    )


def add_into(dst, count, *sources):
    def one(i, carry):
        total = sources[0](i).astype(F32)
        for source in sources[1:]:
            total = total + source(i).astype(F32)
        dst(i, total)
        return carry

    lax.fori_loop(0, count, one, 0, unroll=False)


def sum_kernel(
    scale,
    q_ref, k_ref, v_ref, dy_ref, normed_ref, mixed_ref,
    out_ref,
    part, pair, held, first_in, first_fwd, mid, second_in, second_fwd, last, last_in,
    core_send, core_recv, first_send, first_recv, second_send, second_recv, z_send, z_recv,
):
    z, y, x, core = place()
    other = 1 - core
    partner = device(z, y, x, other)
    x_next, x_prev = device(z, y, (x + 1) % 4, core), device(z, y, (x + 3) % 4, core)
    y_next, y_prev = device(z, (y + 1) % 4, x, core), device(z, (y + 3) % 4, x, core)
    z_others = [device((z + o) % 8, y, x, core) for o in range(1, 8)]

    barrier = pltpu.get_barrier_semaphore()
    peers = [partner, x_next, x_prev, y_next, y_prev] + z_others
    for peer in peers:
        pl.semaphore_signal(barrier, inc=1, device_id=peer, device_id_type=MESH)
    pl.semaphore_wait(barrier, len(peers))

    lefts = [q_ref, k_ref, v_ref, dy_ref]
    rights = [normed_ref, normed_ref, normed_ref, mixed_ref]
    pending = []

    def product(w):
        for r in range(4):
            total = lax.dot_general(
                lefts[w][:, r * 256:(r + 1) * 256], rights[w][...],
                (((0,), (0,)), ((), ())), preferred_element_type=F32,
            )
            part[w, r] = total.astype(BF16).reshape(2, 4, 2, 16, D)
            copy = remote(
                part.at[w, r, :, :, other], pair.at[w, r], core_send.at[w, r], core_recv.at[w, r], partner
            )
            copy.start()
            pending.append(copy)

    def ring_starts(w, stage, source, inbox, send, recv, me, after, before):
        across, ahead, behind = (me + 2) % 4, (me + 1) % 4, (me + 3) % 4
        copies = [
            remote(source(across, 0), inbox.at[w, 0, 0], send.at[w, 0, 0], recv.at[w, 0, 0], after),
            remote(source(across, 1), inbox.at[w, 1, 0], send.at[w, 1, 0], recv.at[w, 1, 0], before),
            remote(source(ahead, 1), inbox.at[w, 0, 1], send.at[w, 0, 1], recv.at[w, 0, 1], after),
            remote(source(behind, 0), inbox.at[w, 1, 1], send.at[w, 1, 1], recv.at[w, 1, 1], before),
        ]
        for copy in copies:
            copy.start()
        return copies

    def x_first(w):
        return w % 2 == 1

    def gather_pair(w):
        for r in range(4):
            pending[(order.index(w)) * 4 + r].wait_recv()

            for h in range(2):
                for c in range(4):
                    total = part[w, r, h, c, core].astype(F32) + pair[w, r, h, c].astype(F32)
                    if x_first(w):
                        held[w, c, r, h] = total.astype(BF16)
                    else:
                        held[w, r, c, h] = total.astype(BF16)

    def first_ring(w):
        me, after, before = (x, x_next, x_prev) if x_first(w) else (y, y_next, y_prev)
        return ring_starts(
            w, 0, lambda i, h: held.at[w, i, :, h], first_in, first_send, first_recv, me, after, before
        )

    def first_forward(w, copies):
        me, after, before = (x, x_next, x_prev) if x_first(w) else (y, y_next, y_prev)
        ahead, behind = (me + 1) % 4, (me + 3) % 4
        copies[0].wait_recv()
        for c in range(4):
            first_fwd[w, 0, c] = (first_in[w, 0, 0, c].astype(F32) + held[w, ahead, c, 0].astype(F32)).astype(BF16)
        one = remote(first_fwd.at[w, 0], first_in.at[w, 0, 2], first_send.at[w, 0, 2], first_recv.at[w, 0, 2], after)
        one.start()
        copies[1].wait_recv()
        for c in range(4):
            first_fwd[w, 1, c] = (first_in[w, 1, 0, c].astype(F32) + held[w, behind, c, 1].astype(F32)).astype(BF16)
        two = remote(first_fwd.at[w, 1], first_in.at[w, 1, 2], first_send.at[w, 1, 2], first_recv.at[w, 1, 2], before)
        two.start()
        return copies + [one, two]

    def first_finish(w, copies):
        me = x if x_first(w) else y
        for copy in copies[2:]:
            copy.wait_recv()
        for c in range(4):
            mid[w, c, 0] = (
                held[w, me, c, 0].astype(F32) + first_in[w, 0, 2, c].astype(F32) + first_in[w, 1, 1, c].astype(F32)
            ).astype(BF16)
            mid[w, c, 1] = (
                held[w, me, c, 1].astype(F32) + first_in[w, 1, 2, c].astype(F32) + first_in[w, 0, 1, c].astype(F32)
            ).astype(BF16)

    def second_ring(w):
        me, after, before = (y, y_next, y_prev) if x_first(w) else (x, x_next, x_prev)
        return ring_starts(
            w, 1, lambda i, h: mid.at[w, i, h], second_in, second_send, second_recv, me, after, before
        )

    def second_forward(w, copies):
        me, after, before = (y, y_next, y_prev) if x_first(w) else (x, x_next, x_prev)
        ahead, behind = (me + 1) % 4, (me + 3) % 4
        copies[0].wait_recv()
        second_fwd[w, 0] = (second_in[w, 0, 0].astype(F32) + mid[w, ahead, 0].astype(F32)).astype(BF16)
        one = remote(second_fwd.at[w, 0], second_in.at[w, 0, 2], second_send.at[w, 0, 2], second_recv.at[w, 0, 2], after)
        one.start()
        copies[1].wait_recv()
        second_fwd[w, 1] = (second_in[w, 1, 0].astype(F32) + mid[w, behind, 1].astype(F32)).astype(BF16)
        two = remote(second_fwd.at[w, 1], second_in.at[w, 1, 2], second_send.at[w, 1, 2], second_recv.at[w, 1, 2], before)
        two.start()
        return copies + [one, two]

    def second_finish(w, copies):
        me = y if x_first(w) else x
        for copy in copies[2:]:
            copy.wait_recv()
        last[2 * w] = (
            mid[w, me, 0].astype(F32) + second_in[w, 0, 2].astype(F32) + second_in[w, 1, 1].astype(F32)
        ).astype(BF16)
        last[2 * w + 1] = (
            mid[w, me, 1].astype(F32) + second_in[w, 1, 2].astype(F32) + second_in[w, 0, 1].astype(F32)
        ).astype(BF16)

    order = [3, 2, 1, 0]
    rings = {}
    seconds = {}
    for w in order:
        product(w)
    for w in order:
        gather_pair(w)
        rings[w] = first_ring(w)
    for w in order:
        rings[w] = first_forward(w, rings[w])
    for w in order:
        first_finish(w, rings[w])
        seconds[w] = second_ring(w)
    for w in order:
        seconds[w] = second_forward(w, seconds[w])
    for w in order:
        second_finish(w, seconds[w])
    copies = []
    for o in range(1, 8):
        copy = remote(
            last.at[(z + o) % 8], last_in.at[o - 1], z_send.at[o - 1], z_recv.at[o - 1], z_others[o - 1]
        )
        copy.start()
        copies.append(copy)
    total = last[z].astype(F32)
    for o in range(1, 8):
        copies[o - 1].wait_recv()
        total = total + last_in[o - 1].astype(F32)
    out_ref[...] = total * scale
    for copy in pending + copies:
        copy.wait_send()
    for w in order:
        for copy in rings[w] + seconds[w]:
            copy.wait_send()


def weight_sums(q, k, v, dy, normed, mixed, scale):
    vmem = pl.BlockSpec(memory_space=pltpu.VMEM)
    dma = pltpu.SemaphoreType.DMA
    return pl.pallas_call(
        functools.partial(sum_kernel, scale),
        out_shape=jax.ShapeDtypeStruct((16, D), F32),
        in_specs=[vmem] * 6,
        out_specs=vmem,
        scratch_shapes=[
            pltpu.VMEM((4, 4, 2, 4, 2, 16, D), BF16),
            pltpu.VMEM((4, 4, 2, 4, 16, D), BF16),
            pltpu.VMEM((4, 4, 4, 2, 16, D), BF16),
            pltpu.VMEM((4, 2, 3, 4, 16, D), BF16),
            pltpu.VMEM((4, 2, 4, 16, D), BF16),
            pltpu.VMEM((4, 4, 2, 16, D), BF16),
            pltpu.VMEM((4, 2, 3, 16, D), BF16),
            pltpu.VMEM((4, 2, 16, D), BF16),
            pltpu.VMEM((8, 16, D), BF16),
            pltpu.VMEM((7, 16, D), BF16),
            dma((4, 4)), dma((4, 4)),
            dma((4, 2, 3)), dma((4, 2, 3)),
            dma((4, 2, 3)), dma((4, 2, 3)),
            dma((7,)), dma((7,)),
        ],
        compiler_params=pltpu.CompilerParams(
            collective_id=0, has_side_effects=True, vmem_limit_bytes=56 * 1024 * 1024
        ),
        cost_estimate=pl.CostEstimate(flops=8 * 384 * D * D, bytes_accessed=6 * 384 * D * 2, transcendentals=0),
    )(q, k, v, dy, normed, mixed)


def shards(tokens, cotangent, norm_gain, query_weight, key_weight, value_weight, out_weight):
    x_rows, dy_rows = (
        lax.all_to_all(tokens, "tm", split_axis=1, concat_axis=0, tiled=True),
        lax.all_to_all(cotangent, "tm", split_axis=1, concat_axis=0, tiled=True),
    )
    frames, places, features = x_rows.shape
    head_size = features // H
    count = frames * places

    def split_heads(matrix):
        return matrix.reshape(frames, places, H, head_size)

    floated = x_rows.reshape(count, features).astype(jnp.float32)
    centred = floated - jnp.mean(floated, -1, keepdims=True)
    variance = jnp.mean(centred * centred, -1, keepdims=True)
    inv_scale = lax.rsqrt(variance + EPS)
    standard = centred * inv_scale
    normed = (standard * norm_gain).astype(jnp.bfloat16)
    query = jnp.dot(normed, query_weight, preferred_element_type=jnp.float32).astype(jnp.bfloat16)
    key_rows = jnp.dot(normed, key_weight, preferred_element_type=jnp.float32).astype(jnp.bfloat16)
    value = jnp.dot(normed, value_weight, preferred_element_type=jnp.float32).astype(jnp.bfloat16)
    query_heads = split_heads(query)
    key_heads = split_heads(key_rows)
    value_heads = split_heads(value)
    scores = jnp.einsum(
        "fphe,gphe->phfg", query_heads, key_heads, preferred_element_type=jnp.float32
    ) / math.sqrt(head_size)
    weights = jax.nn.softmax(scores, axis=-1)
    weights_low = weights.astype(jnp.bfloat16)
    mixed = (
        jnp.einsum("phfg,gphe->fphe", weights_low, value_heads, preferred_element_type=jnp.float32)
        .reshape(count, features)
        .astype(jnp.bfloat16)
    )
    dy_flat = dy_rows.reshape(count, features)
    grad_mixed = times_transposed(dy_flat, out_weight).astype(jnp.bfloat16)
    mixed_heads = split_heads(grad_mixed)
    grad_weights = jnp.einsum(
        "fphe,gphe->phfg", mixed_heads, value_heads, preferred_element_type=jnp.float32
    )
    grad_value = (
        jnp.einsum("phfg,fphe->gphe", weights_low, mixed_heads, preferred_element_type=jnp.float32)
        .reshape(count, features)
        .astype(jnp.bfloat16)
    )
    delta_row = jnp.sum(weights * grad_weights, -1, keepdims=True)
    grad_scores = (weights * (grad_weights - delta_row) / math.sqrt(head_size)).astype(jnp.bfloat16)
    grad_query = (
        jnp.einsum("phfg,gphe->fphe", grad_scores, key_heads, preferred_element_type=jnp.float32)
        .reshape(count, features)
        .astype(jnp.bfloat16)
    )
    grad_key = (
        jnp.einsum("phfg,fphe->gphe", grad_scores, query_heads, preferred_element_type=jnp.float32)
        .reshape(count, features)
        .astype(jnp.bfloat16)
    )
    grad_normed = (
        times_transposed(grad_query, query_weight)
        + times_transposed(grad_key, key_weight)
        + times_transposed(grad_value, value_weight)
    )
    grad_standard = grad_normed * norm_gain
    grad_x = dy_flat.astype(jnp.float32) + inv_scale * (
        grad_standard
        - jnp.mean(grad_standard, -1, keepdims=True)
        - standard * jnp.mean(grad_standard * standard, -1, keepdims=True)
    )
    grad_local = grad_x.astype(jnp.bfloat16).reshape(frames, places, features)
    grad_back = lax.all_to_all(grad_local, "tm", split_axis=0, concat_axis=1, tiled=True)
    total_rows = frames * places * lax.axis_size("tm") * lax.axis_size("space")
    summed = weight_sums(
        grad_query, grad_key, grad_value, dy_flat, normed, mixed, 1.0 / math.sqrt(total_rows)
    )
    return (grad_back, summed.T)


def solution(mesh):
    in_specs = (P("tm", "space", None), P("tm", "space", None), P(), P(), P(), P(), P())
    out_specs = (P("tm", "space", None), P(None, ("tm", "space")))
    return jax.shard_map(shards, mesh=mesh, in_specs=in_specs, out_specs=out_specs, check_vma=False)
```

```python
import functools
import math

import jax
import jax.numpy as jnp
from jax import lax
from jax.experimental import pallas as pl
from jax.experimental.pallas import tpu as pltpu
from jax.sharding import PartitionSpec as P

H = 16
D = 1024
HEAD = D // H
PAIRS = H // 2
LOCAL = 24
GROUP = 16
FRAMES = LOCAL * GROUP
TILES = D // 128
EPS = 1e-06
MESH = pl.DeviceIdType.MESH
BF16 = jnp.bfloat16
F32 = jnp.float32


def nn(left, right):
    return lax.dot_general(left, right, (((1,), (0,)), ((), ())), preferred_element_type=F32)


def nt(left, right):
    return lax.dot_general(left, right, (((1,), (1,)), ((), ())), preferred_element_type=F32)


def tn(left, right):
    return lax.dot_general(left, right, (((0,), (0,)), ((), ())), preferred_element_type=F32)


def place():
    tm = lax.axis_index("tm")
    space = lax.axis_index("space")
    return (tm // 4) * 2 + space // 8, tm % 4, (space // 2) % 4, space % 2


def device(z, y, x, core):
    return ((z // 2) * 4 + y, ((z % 2) * 4 + x) * 2 + core)


def remote(src, dst, send, recv, to):
    return pltpu.make_async_remote_copy(
        src_ref=src, dst_ref=dst, send_sem=send, recv_sem=recv, device_id=to, device_id_type=MESH
    )


def loop(count, body):
    def step(i, carry):
        body(i)
        return carry

    lax.fori_loop(0, count, step, 0, unroll=False)


def kernel(
    scale,
    tokens, cotangent, gain, wq_hbm, wk_hbm, wv_hbm, wo_hbm,
    grad_ref, sums_ref,
    raw, turn, grad_normed, x_out, dy_out, x_in, dy_in, back_out, back_in, stats,
    wq, wk, wv, wo,
    normed, query, key, value, mixed, dy, grad_mixed, grad_query, grad_key, grad_value,
    weights, low, low_grad,
    part, pair, first_in, first_fwd, mid, second_in, second_fwd, last, last_in,
    load_sem, in_send, in_recv, back_send, back_recv,
    core_send, core_recv, first_send, first_recv, second_send, second_recv, z_send, z_recv,
):
    z, y, x, core = place()
    z_hi, z_lo = z // 2, z % 2
    me = z_hi * 4 + y
    partner = device(z, y, x, 1 - core)
    x_next, x_prev = device(z, y, (x + 1) % 4, core), device(z, y, (x + 3) % 4, core)
    y_next, y_prev = device(z, (y + 1) % 4, x, core), device(z, (y + 3) % 4, x, core)

    def member(i):
        a, b = i // 4, i % 4
        to = ((z_hi + a) % 4) * 4 + (y + b) % 4
        source = ((z_hi + 4 - a) % 4) * 4 + (y + 4 - b) % 4
        return to, source, device(((z_hi + a) % 4) * 2 + z_lo, (y + b) % 4, x, core)

    loads = [
        pltpu.make_async_copy(tokens, raw.at[0], load_sem.at[0]),
        pltpu.make_async_copy(cotangent, raw.at[1], load_sem.at[1]),
        pltpu.make_async_copy(wq_hbm, wq, load_sem.at[2]),
        pltpu.make_async_copy(wk_hbm, wk, load_sem.at[3]),
        pltpu.make_async_copy(wv_hbm, wv, load_sem.at[4]),
        pltpu.make_async_copy(wo_hbm, wo, load_sem.at[5]),
    ]
    for load in loads:
        load.start()

    barrier = pltpu.get_barrier_semaphore()
    peers = [member(i)[2] for i in range(1, 16)]
    peers += [partner, x_next, x_prev] + [device((z + o) % 8, y, x, core) for o in (1, 3, 5, 7)]
    for peer in peers:
        pl.semaphore_signal(barrier, inc=1, device_id=peer, device_id_type=MESH)

    def positions_first(which, target):
        def frame(f):
            rows = raw[which, f].astype(F32)
            for t in range(TILES):
                turn[pl.ds(pl.multiple_of(t * FRAMES + f * GROUP, 16), GROUP), :] = rows[:, t * 128:(t + 1) * 128]

        loop(LOCAL, frame)

        def position(p):
            rows = [turn[pl.ds(t * FRAMES + p, LOCAL, stride=GROUP), :] for t in range(TILES)]
            target[p] = jnp.concatenate(rows, 1).astype(BF16)

        loop(GROUP, position)

    def in_copy(which, i):
        to, _, peer = member(i)
        source, target = ((x_out, x_in), (dy_out, dy_in))[which]
        return remote(source.at[to], target.at[me], in_send.at[which, i], in_recv.at[which, i], peer)

    def send_in(which):
        loop(12, lambda j: in_copy(which, j + 4).start())
        loop(3, lambda j: in_copy(which, j + 1).start())

    def finish_in(which):
        loop(15, lambda j: in_copy(which, j + 1).wait_recv())

    loads[0].wait()
    positions_first(0, x_out)
    pl.semaphore_wait(barrier, len(peers))
    send_in(0)
    x_in[me] = x_out[me]
    loads[1].wait()
    positions_first(1, dy_out)
    send_in(1)
    dy_in[me] = dy_out[me]

    for load in loads[2:5]:
        load.wait()
    finish_in(0)

    def normalise(i):
        rows = []
        for j in range(2):
            floated = x_in[2 * i + j].astype(F32)
            mean = jnp.mean(floated, -1, keepdims=True)
            centred = floated - mean
            inv_scale = lax.rsqrt(jnp.mean(centred * centred, -1, keepdims=True) + EPS)
            stats[0, 2 * i + j] = jnp.broadcast_to(mean, (LOCAL, 128))
            stats[1, 2 * i + j] = jnp.broadcast_to(inv_scale, (LOCAL, 128))
            rows.append(centred * inv_scale * gain[...])
        normed[pl.ds(pl.multiple_of(i * 48, 16), 48), :] = jnp.concatenate(rows, 0).astype(BF16)

    loop(GROUP // 2, normalise)

    def project(n):
        columns = pl.ds(pl.multiple_of(n * 256, 256), 256)
        rows = normed[...]
        query[:, columns] = (nn(rows, wq[:, columns]).astype(BF16).astype(F32) * (1.0 / math.sqrt(HEAD))).astype(BF16)
        key[:, columns] = nn(rows, wk[:, columns]).astype(BF16)
        value[:, columns] = nn(rows, wv[:, columns]).astype(BF16)

    loop(4, project)

    first_head = lax.broadcasted_iota(jnp.int32, (FRAMES, 128), 1) < HEAD

    def spread(rows):
        zero = jnp.zeros_like(rows)
        return jnp.concatenate([jnp.where(first_head, rows, zero), jnp.where(first_head, zero, rows)], 0)

    def merge(both):
        return jnp.where(first_head, both[:FRAMES], both[FRAMES:])

    def pair_columns(p):
        return pl.ds(pl.multiple_of(p * 128, 128), 128)

    def forward(p):
        columns = pair_columns(p)
        spread_query = spread(query[:, columns])
        keys = key[:, columns]
        for c in range(3):
            part_rows = slice(c * 256, (c + 1) * 256)
            scores = nt(keys, spread_query[part_rows])
            raised = jnp.exp(scores - jnp.max(scores, 0, keepdims=True))
            shares = raised * (1.0 / jnp.sum(raised, 0, keepdims=True))
            weights[p, :, part_rows] = shares
            low[:, part_rows] = shares.astype(BF16)
        mixed[:, columns] = merge(tn(low[...], value[:, columns])).astype(BF16)

    loop(PAIRS, forward)

    loads[5].wait()
    finish_in(1)

    def gather_dy(i):
        rows = [dy_in[2 * i + j].astype(F32) for j in range(2)]
        dy[pl.ds(pl.multiple_of(i * 48, 16), 48), :] = jnp.concatenate(rows, 0).astype(BF16)

    loop(GROUP // 2, gather_dy)

    def project_back(n):
        columns = pl.ds(pl.multiple_of(n * 256, 256), 256)
        grad_mixed[:, columns] = nt(dy[...], wo[columns, :]).astype(BF16)

    loop(4, project_back)

    lefts = [grad_query, grad_key, grad_value, dy]
    rights = [normed, normed, normed, mixed]

    def core_copy(w, r):
        return remote(
            part.at[w, r, :, :, 1 - core], pair.at[w, r], core_send.at[w, r], core_recv.at[w, r], partner
        )

    def product(w):
        for r in range(4):
            total = tn(lefts[w][:, r * 256:(r + 1) * 256], rights[w][...])
            part[w, r] = total.astype(BF16).reshape(2, 4, 2, 16, D)
            core_copy(w, r).start()

    def x_first(w):
        return w % 2 == 1

    def first_axis(w):
        return (x, x_next, x_prev) if x_first(w) else (y, y_next, y_prev)

    def second_axis(w):
        return (y, y_next, y_prev) if x_first(w) else (x, x_next, x_prev)

    def held(w, i, h):
        return pair.at[w, :, h, i] if x_first(w) else pair.at[w, i, h]

    def gather_pair(w):
        for r in range(4):
            core_copy(w, r).wait_recv()

            def add(n):
                h, c = n // 4, n % 4
                pair[w, r, h, c] = (part[w, r, h, c, core].astype(F32) + pair[w, r, h, c].astype(F32)).astype(BF16)

            loop(8, add)

    def ring(w, axis, source, inbox, forwarded, send, recv, k):
        at, after, before = axis
        to, h, slot = (after, before)[k % 2], k % 2, k // 2
        if slot == 0:
            block = source((at + 2) % 4, h)
        elif slot == 1:
            block = source((at + (1, 3)[h]) % 4, 1 - h)
        else:
            block = forwarded.at[w, h]
        return remote(block, inbox.at[w, h, slot], send.at[w, h, slot], recv.at[w, h, slot], to)

    def first_ring(w, k):
        return ring(w, first_axis(w), lambda i, h: held(w, i, h), first_in, first_fwd, first_send, first_recv, k)

    def second_ring(w, k):
        return ring(w, second_axis(w), lambda i, h: mid.at[w, i, h], second_in, second_fwd, second_send, second_recv, k)

    def start_first(w):
        for k in range(4):
            first_ring(w, k).start()

    def forward_first(w):
        at = first_axis(w)[0]
        for h, near in ((0, (at + 1) % 4), (1, (at + 3) % 4)):
            first_ring(w, h).wait_recv()
            first_fwd[w, h] = (first_in[w, h, 0].astype(F32) + held(w, near, h)[...].astype(F32)).astype(BF16)
            first_ring(w, 4 + h).start()

    def finish_first(w):
        at = first_axis(w)[0]
        for k in range(2, 6):
            first_ring(w, k).wait_recv()
        for h in range(2):
            mid[w, :, h] = (
                held(w, at, h)[...].astype(F32) + first_in[w, h, 2].astype(F32) + first_in[w, 1 - h, 1].astype(F32)
            ).astype(BF16)

    def start_second(w):
        for k in range(4):
            second_ring(w, k).start()

    def forward_second(w):
        at = second_axis(w)[0]
        for h, near in ((0, (at + 1) % 4), (1, (at + 3) % 4)):
            second_ring(w, h).wait_recv()
            second_fwd[w, h] = (second_in[w, h, 0].astype(F32) + mid[w, near, h].astype(F32)).astype(BF16)
            second_ring(w, 4 + h).start()

    def finish_second(w):
        at = second_axis(w)[0]
        for k in range(2, 6):
            second_ring(w, k).wait_recv()
        for h in range(2):
            last[2 * w + h] = (
                mid[w, at, h].astype(F32) + second_in[w, h, 2].astype(F32) + second_in[w, 1 - h, 1].astype(F32)
            ).astype(BF16)

    product(3)

    def backward_value(p):
        columns = pair_columns(p)
        low[...] = weights[p].astype(BF16)
        grad_value[:, columns] = nn(low[...], spread(grad_mixed[:, columns])).astype(BF16)

    def backward(p):
        columns = pair_columns(p)
        spread_grad = spread(grad_mixed[:, columns])
        values = value[:, columns]
        for c in range(3):
            part_rows = slice(c * 256, (c + 1) * 256)
            grad_weights = nt(values, spread_grad[part_rows])
            shares = weights[p, :, part_rows]
            delta = jnp.sum(shares * grad_weights, 0, keepdims=True)
            low_grad[:, part_rows] = (shares * (grad_weights - delta)).astype(BF16)
        grad_scores = low_grad[...]
        grad_key[:, columns] = nn(grad_scores, spread(query[:, columns])).astype(BF16)
        grad_query[:, columns] = (merge(tn(grad_scores, key[:, columns])) * (1.0 / math.sqrt(HEAD))).astype(BF16)

    loop(PAIRS, backward_value)
    product(2)
    loop(PAIRS // 2, backward)
    for w in (3, 2):
        gather_pair(w)
        start_first(w)
    loop(PAIRS // 2, lambda p: backward(p + PAIRS // 2))
    for w in (3, 2):
        forward_first(w)

    def unproject(n):
        columns = pl.ds(pl.multiple_of(n * 256, 256), 256)
        total = nt(grad_query[...], wq[columns, :])
        total = total + nt(grad_key[...], wk[columns, :])
        total = total + nt(grad_value[...], wv[columns, :])
        grad_normed[:, columns] = total * gain[:, columns]

    loop(4, unproject)

    def rows_back(t):
        mean = stats[0, t][:, :1]
        inv_scale = stats[1, t][:, :1]
        standard = (x_in[t].astype(F32) - mean) * inv_scale
        grad_standard = grad_normed[pl.ds(pl.multiple_of(t * LOCAL, 8), LOCAL), :]
        grad = dy_in[t].astype(F32) + inv_scale * (
            grad_standard
            - jnp.mean(grad_standard, -1, keepdims=True)
            - standard * jnp.mean(grad_standard * standard, -1, keepdims=True)
        )
        return grad.astype(BF16)

    def back_copy(i):
        to, _, peer = member(i)
        return remote(back_out.at[to], back_in.at[me], back_send.at[i], back_recv.at[i], peer)

    def send_back(i):
        to = member(i)[0]
        back_out[to] = rows_back(to)
        back_copy(i).start()

    loop(12, lambda j: send_back(j + 4))
    loop(3, lambda j: send_back(j + 1))
    back_in[me] = rows_back(me)

    for w in (1, 0):
        product(w)
    for w in (3, 2):
        finish_first(w)
        start_second(w)
    for w in (1, 0):
        gather_pair(w)
        start_first(w)
    for w in (3, 2):
        forward_second(w)
    for w in (1, 0):
        forward_first(w)
    for w in (3, 2):
        finish_second(w)
    for w in (1, 0):
        finish_first(w)
        start_second(w)
    for w in (1, 0):
        forward_second(w)
    for w in (1, 0):
        finish_second(w)

    def z_copy(o):
        return remote(
            last.at[(z + o) % 8], last_in.at[o - 1], z_send.at[o - 1], z_recv.at[o - 1],
            device((z + o) % 8, y, x, core),
        )

    for o in range(1, 8):
        z_copy(o).start()

    loop(15, lambda j: back_copy(j + 1).wait_recv())

    def position_out(p):
        rows = back_in[p].astype(F32)
        for t in range(TILES):
            turn[pl.ds(t * FRAMES + p, LOCAL, stride=GROUP), :] = rows[:, t * 128:(t + 1) * 128]

    loop(GROUP, position_out)

    def frame_out(f):
        rows = [turn[pl.ds(pl.multiple_of(t * FRAMES + f * GROUP, 16), GROUP), :] for t in range(TILES)]
        grad_ref[f] = jnp.concatenate(rows, 1).astype(BF16)

    loop(LOCAL, frame_out)

    total = last[z].astype(F32)
    for o in range(1, 8):
        z_copy(o).wait_recv()
        total = total + last_in[o - 1].astype(F32)
    sums_ref[...] = total * scale

    for which in range(2):
        loop(15, lambda j: in_copy(which, j + 1).wait_send())
    loop(15, lambda j: back_copy(j + 1).wait_send())
    for w in range(4):
        for r in range(4):
            core_copy(w, r).wait_send()
        for k in range(6):
            first_ring(w, k).wait_send()
            second_ring(w, k).wait_send()
    for o in range(1, 8):
        z_copy(o).wait_send()


def shards(tokens, cotangent, norm_gain, query_weight, key_weight, value_weight, out_weight):
    total_rows = FRAMES * lax.axis_size("tm") * lax.axis_size("space")
    anywhere = pl.BlockSpec(memory_space=pl.ANY)
    vmem = pl.BlockSpec(memory_space=pltpu.VMEM)
    dma = pltpu.SemaphoreType.DMA
    rows = pltpu.VMEM((FRAMES, D), BF16)
    block = pltpu.VMEM((GROUP, LOCAL, D), BF16)
    weight = pltpu.VMEM((D, D), BF16)
    grad, sums = pl.pallas_call(
        functools.partial(kernel, 1.0 / math.sqrt(total_rows)),
        out_shape=(
            jax.ShapeDtypeStruct((LOCAL, GROUP, D), BF16),
            jax.ShapeDtypeStruct((16, D), F32),
        ),
        in_specs=[anywhere, anywhere, vmem] + [anywhere] * 4,
        out_specs=(vmem, vmem),
        scratch_shapes=[
            pltpu.VMEM((2, LOCAL, GROUP, D), BF16),
            pltpu.VMEM((TILES * FRAMES, 128), F32),
            pltpu.VMEM((FRAMES, D), F32),
            block, block, block, block, block, block,
            pltpu.VMEM((2, GROUP, LOCAL, 128), F32),
            weight, weight, weight, weight,
            rows, rows, rows, rows, rows, rows, rows, rows, rows, rows,
            pltpu.VMEM((PAIRS, FRAMES, 2 * FRAMES), F32),
            pltpu.VMEM((FRAMES, 2 * FRAMES), BF16),
            pltpu.VMEM((FRAMES, 2 * FRAMES), BF16),
            pltpu.VMEM((4, 4, 2, 4, 2, 16, D), BF16),
            pltpu.VMEM((4, 4, 2, 4, 16, D), BF16),
            pltpu.VMEM((4, 2, 3, 4, 16, D), BF16),
            pltpu.VMEM((4, 2, 4, 16, D), BF16),
            pltpu.VMEM((4, 4, 2, 16, D), BF16),
            pltpu.VMEM((4, 2, 3, 16, D), BF16),
            pltpu.VMEM((4, 2, 16, D), BF16),
            pltpu.VMEM((8, 16, D), BF16),
            pltpu.VMEM((7, 16, D), BF16),
            dma((6,)), dma((2, 16)), dma((2, 16)), dma((16,)), dma((16,)),
            dma((4, 4)), dma((4, 4)),
            dma((4, 2, 3)), dma((4, 2, 3)),
            dma((4, 2, 3)), dma((4, 2, 3)),
            dma((7,)), dma((7,)),
        ],
        compiler_params=pltpu.CompilerParams(
            collective_id=0, has_side_effects=True, vmem_limit_bytes=60 * 1024 * 1024
        ),
    )(tokens, cotangent, norm_gain.reshape(1, D), query_weight, key_weight, value_weight, out_weight)
    return grad, sums.T


def solution(mesh):
    in_specs = (P("tm", "space", None), P("tm", "space", None), P(), P(), P(), P(), P())
    out_specs = (P("tm", "space", None), P(None, ("tm", "space")))
    return jax.shard_map(shards, mesh=mesh, in_specs=in_specs, out_specs=out_specs, check_vma=False)
```

```python
import functools
import math

import jax
import jax.numpy as jnp
from jax import lax
from jax.experimental import pallas as pl
from jax.experimental.pallas import tpu as pltpu
from jax.sharding import PartitionSpec as P

H = 16
D = 1024
HEAD = D // H
PAIRS = H // 2
LOCAL = 24
GROUP = 16
FRAMES = LOCAL * GROUP
TILES = D // 128
EPS = 1e-06
EARLY = 256
LATE = FRAMES - EARLY
OFFSETS = (
    (0, 0), (0, 1), (0, 2), (0, 3),
    (1, 0), (3, 0), (1, 1), (3, 1), (1, 2), (3, 2), (1, 3),
    (3, 3), (2, 0), (2, 1), (2, 2), (2, 3),
)
SEND_ORDER = tuple(range(4, 11)) + (1, 2, 3) + tuple(range(11, 16))
X_FIRST = ((False, False), (True, True), (True, True), (True, False))
MESH = pl.DeviceIdType.MESH
BF16 = jnp.bfloat16
F32 = jnp.float32


def nn(left, right):
    return lax.dot_general(left, right, (((1,), (0,)), ((), ())), preferred_element_type=F32)


def nt(left, right):
    return lax.dot_general(left, right, (((1,), (1,)), ((), ())), preferred_element_type=F32)


def tn(left, right):
    return lax.dot_general(left, right, (((0,), (0,)), ((), ())), preferred_element_type=F32)


def place():
    tm = lax.axis_index("tm")
    space = lax.axis_index("space")
    return (tm // 4) * 2 + space // 8, tm % 4, (space // 2) % 4, space % 2


def device(z, y, x, core):
    return ((z // 2) * 4 + y, ((z % 2) * 4 + x) * 2 + core)


def remote(src, dst, send, recv, to):
    return pltpu.make_async_remote_copy(
        src_ref=src, dst_ref=dst, send_sem=send, recv_sem=recv, device_id=to, device_id_type=MESH
    )


def loop(count, body):
    def step(i, carry):
        body(i)
        return carry

    lax.fori_loop(0, count, step, 0, unroll=False)


def kernel(
    scale,
    tokens, cotangent, gain, wq_hbm, wk_hbm, wv_hbm, wo_hbm,
    back_in, sums_ref,
    raw, turn, x_out, dy_out, x_in, dy_in, back_out, stats,
    wq, wk, wv, wo,
    normed, query, key, value, mixed, dy, grad_mixed, grad_query, grad_key, grad_value,
    weights, lows, low_grad,
    part, pair, first_in, first_fwd, mid, second_in, second_fwd, last, last_in,
    load_sem, in_send, in_recv, back_send, back_recv,
    core_send, core_recv, first_send, first_recv, second_send, second_recv, z_send, z_recv,
):
    z, y, x, core = place()
    z_hi, z_lo = z // 2, z % 2
    me = z_hi * 4 + y
    partner = device(z, y, x, 1 - core)
    x_next, x_prev = device(z, y, (x + 1) % 4, core), device(z, y, (x + 3) % 4, core)
    y_next, y_prev = device(z, (y + 1) % 4, x, core), device(z, (y + 3) % 4, x, core)

    def member(i, sign):
        a, b = OFFSETS[i]
        to_z, to_y = (z_hi + 4 + sign * a) % 4, (y + 4 + sign * b) % 4
        return to_z * 4 + to_y, device(to_z * 2 + z_lo, to_y, x, core)

    loads = [
        pltpu.make_async_copy(tokens, raw.at[0], load_sem.at[0]),
        pltpu.make_async_copy(cotangent, raw.at[1], load_sem.at[1]),
        pltpu.make_async_copy(wq_hbm, wq, load_sem.at[2]),
        pltpu.make_async_copy(wk_hbm, wk, load_sem.at[3]),
        pltpu.make_async_copy(wv_hbm, wv, load_sem.at[4]),
        pltpu.make_async_copy(wo_hbm, wo, load_sem.at[5]),
    ]
    for load in loads:
        load.start()

    barrier = pltpu.get_barrier_semaphore()
    peers = [member(i, 1)[1] for i in range(1, GROUP)]
    peers += [partner, x_next, x_prev] + [device((z + o) % 8, y, x, core) for o in (1, 3, 5, 7)]
    for peer in peers:
        pl.semaphore_signal(barrier, inc=1, device_id=peer, device_id_type=MESH)

    def positions_first(which, target):
        def frame(f):
            rows = raw[which, f].astype(F32)
            for t in range(TILES):
                turn[pl.ds(pl.multiple_of(t * FRAMES + f * GROUP, 16), GROUP), :] = rows[:, t * 128:(t + 1) * 128]

        loop(LOCAL, frame)

        def position(p):
            rows = [turn[pl.ds(t * FRAMES + p, LOCAL, stride=GROUP), :] for t in range(TILES)]
            target[p] = jnp.concatenate(rows, 1).astype(BF16)

        loop(GROUP, position)

    def in_copy(which, i):
        to, peer = member(i, 1)
        source, target = ((x_out, x_in), (dy_out, dy_in))[which]
        return remote(source.at[to], target.at[i], in_send.at[which, i], in_recv.at[which, i], peer)

    loads[0].wait()
    positions_first(0, x_out)
    pl.semaphore_wait(barrier, len(peers))
    for i in SEND_ORDER:
        in_copy(0, i).start()
    x_in[0] = x_out[me]
    loads[1].wait()
    positions_first(1, dy_out)
    for i in SEND_ORDER:
        in_copy(1, i).start()
    dy_in[0] = dy_out[me]

    def normalise(i):
        rows = []
        for j in range(2):
            floated = x_in[2 * i + j].astype(F32)
            mean = jnp.mean(floated, -1, keepdims=True)
            centred = floated - mean
            inv_scale = lax.rsqrt(jnp.mean(centred * centred, -1, keepdims=True) + EPS)
            stats[0, 2 * i + j] = jnp.broadcast_to(mean, (LOCAL, 128))
            stats[1, 2 * i + j] = jnp.broadcast_to(inv_scale, (LOCAL, 128))
            rows.append(centred * inv_scale * gain[...])
        normed[pl.ds(i * 48, 48), :] = jnp.concatenate(rows, 0).astype(BF16)

    def project(start, count):
        def block(n):
            columns = pl.ds(pl.multiple_of(n * 256, 256), 256)
            rows = normed[start:start + count, :]
            query[start:start + count, columns] = (nn(rows, wq[:, columns]) * (1.0 / math.sqrt(HEAD))).astype(BF16)
            key[start:start + count, columns] = nn(rows, wk[:, columns]).astype(BF16)
            value[start:start + count, columns] = nn(rows, wv[:, columns]).astype(BF16)

        loop(4, block)

    for i in range(GROUP // 2):
        for j in range(2):
            if i + j > 0:
                in_copy(0, 2 * i + j).wait_recv()
        if i == 0:
            for load in loads[2:5]:
                load.wait()
        normalise(i)
        if 48 * i < EARLY <= 48 * (i + 1):
            project(0, EARLY)
    project(EARLY, LATE)

    def spread(rows):
        first = lax.broadcasted_iota(jnp.int32, rows.shape, 1) < HEAD
        zero = jnp.zeros_like(rows)
        return jnp.concatenate([jnp.where(first, rows, zero), jnp.where(first, zero, rows)], 0)

    def merge(both):
        count = both.shape[0] // 2
        first = lax.broadcasted_iota(jnp.int32, (count, 128), 1) < HEAD
        return jnp.where(first, both[:count], both[count:])

    def pair_columns(p):
        return pl.ds(pl.multiple_of(p * 128, 128), 128)

    def forward(p):
        columns = pair_columns(p)
        spread_query = spread(query[:, columns])
        keys = key[:, columns]
        for c in range(3):
            part_rows = slice(c * 256, (c + 1) * 256)
            scores = nt(keys, spread_query[part_rows])
            raised = jnp.exp(scores - jnp.max(scores, 0, keepdims=True))
            shares = raised * (1.0 / jnp.sum(raised, 0, keepdims=True))
            weights[p, :, part_rows] = shares
            lows[p, :, part_rows] = shares.astype(BF16)
        mixed[:, columns] = merge(tn(lows[p], value[:, columns])).astype(BF16)

    loop(PAIRS, forward)

    def gather_dy(i):
        rows = [dy_in[2 * i + j].astype(F32) for j in range(2)]
        dy[pl.ds(i * 48, 48), :] = jnp.concatenate(rows, 0).astype(BF16)

    def project_back(start, count):
        def block(n):
            columns = pl.ds(pl.multiple_of(n * 256, 256), 256)
            grad_mixed[start:start + count, columns] = nt(dy[start:start + count, :], wo[columns, :]).astype(BF16)

        loop(4, block)

    early_slots = -(-EARLY // LOCAL)
    for i in range(1, early_slots):
        in_copy(1, i).wait_recv()
    for i in range(EARLY // 48):
        gather_dy(i)
    dy[EARLY // 48 * 48:EARLY, :] = dy_in[early_slots - 1][:EARLY - LOCAL * (early_slots - 1)]
    loads[5].wait()
    project_back(0, EARLY)

    def backward_early(p):
        columns = pair_columns(p)
        spread_grad = spread(grad_mixed[:EARLY, columns])
        values, keys = value[:, columns], key[:, columns]
        both = []
        for c in range(2):
            at = slice(c * FRAMES, c * FRAMES + EARLY)
            grad_weights = nt(values, spread_grad[c * EARLY:(c + 1) * EARLY])
            shares = weights[p, :, at]
            delta = jnp.sum(shares * grad_weights, 0, keepdims=True)
            scores = shares * (grad_weights - delta)
            weights[p, :, at] = scores
            both.append(tn(scores.astype(BF16), keys))
        first = lax.broadcasted_iota(jnp.int32, (EARLY, 128), 1) < HEAD
        grad_query[:EARLY, columns] = (jnp.where(first, both[0], both[1]) * (1.0 / math.sqrt(HEAD))).astype(BF16)

    loop(PAIRS, backward_early)

    for i in range(early_slots, GROUP):
        in_copy(1, i).wait_recv()
    for i in range(EARLY // 48, GROUP // 2):
        gather_dy(i)
    project_back(EARLY, LATE)

    def backward_late(p):
        columns = pair_columns(p)
        grads = grad_mixed[:, columns]
        values, keys = value[:, columns], key[:, columns]
        grad_value[:, columns] = nn(lows[p], spread(grads)).astype(BF16)
        grad_weights = nt(values, spread(grads[EARLY:]))
        shares = jnp.concatenate([weights[p, :, EARLY:FRAMES], weights[p, :, FRAMES + EARLY:]], 1)
        delta = jnp.sum(shares * grad_weights, 0, keepdims=True)
        scores = (shares * (grad_weights - delta)).astype(BF16)
        grad_query[EARLY:, columns] = (merge(tn(scores, keys)) * (1.0 / math.sqrt(HEAD))).astype(BF16)
        for c in range(2):
            low_grad[:, c * FRAMES:c * FRAMES + EARLY] = weights[p, :, c * FRAMES:c * FRAMES + EARLY].astype(BF16)
            low_grad[:, c * FRAMES + EARLY:(c + 1) * FRAMES] = scores[:, c * LATE:(c + 1) * LATE]
        grad_key[:, columns] = nn(low_grad[...], spread(query[:, columns])).astype(BF16)

    lefts = [grad_query, grad_key, grad_value, dy]
    rights = [normed, normed, normed, mixed]

    def core_copy(w, h):
        return remote(
            part.at[w, :, h, :, 1 - core], pair.at[w, :, h], core_send.at[w, h], core_recv.at[w, h], partner
        )

    def product(w, h):
        left = lefts[w]
        for r in (0, 2):
            rows = [left[:, (r + j) * 256 + h * 128:(r + j) * 256 + h * 128 + 128] for j in range(2)]
            total = tn(jnp.concatenate(rows, 1), rights[w][...]).astype(BF16).reshape(2, 4, 2, 16, D)
            for j in range(2):
                part[w, r + j, h] = total[j]
        core_copy(w, h).start()

    def first_axis(w, h):
        return (x, x_next, x_prev) if X_FIRST[w][h] else (y, y_next, y_prev)

    def second_axis(w, h):
        return (y, y_next, y_prev) if X_FIRST[w][h] else (x, x_next, x_prev)

    def held(w, h, i, s):
        return pair.at[w, pl.ds(2 * s, 2), h, i] if X_FIRST[w][h] else pair.at[w, i, h, pl.ds(2 * s, 2)]

    def start_unit(w, h):
        core_copy(w, h).wait_recv()

        def add(n):
            r, c = n // 4, n % 4
            pair[w, r, h, c] = (part[w, r, h, c, core].astype(F32) + pair[w, r, h, c].astype(F32)).astype(BF16)

        loop(16, add)
        for k in range(4):
            first_ring(w, h, k).start()

    def ring(axis, source, inbox, forwarded, send, recv, k):
        at, after, before = axis
        to, d, slot = (after, before)[k % 2], k % 2, k // 2
        if slot == 0:
            block = source((at + 2) % 4, d)
        elif slot == 1:
            block = source((at + (1, 3)[d]) % 4, 1 - d)
        else:
            block = forwarded.at[d]
        return remote(block, inbox.at[d, slot], send.at[d, slot], recv.at[d, slot], to)

    def first_ring(w, h, k):
        return ring(
            first_axis(w, h), lambda i, s: held(w, h, i, s), first_in.at[w, h], first_fwd.at[w, h],
            first_send.at[w, h], first_recv.at[w, h], k,
        )

    def middle(w, h, i, s):
        return mid.at[w, h, i, :, pl.ds(s * 512, 512)]

    def second_ring(w, h, k):
        return ring(
            second_axis(w, h), lambda i, s: middle(w, h, i, s), second_in.at[w, h], second_fwd.at[w, h],
            second_send.at[w, h], second_recv.at[w, h], k,
        )

    def forward_first(w, h):
        at = first_axis(w, h)[0]
        for d in range(2):
            first_ring(w, h, d).wait_recv()
            own = held(w, h, (at + (1, 3)[d]) % 4, d)[...]
            first_fwd[w, h, d] = (first_in[w, h, d, 0].astype(F32) + own.astype(F32)).astype(BF16)
            first_ring(w, h, 4 + d).start()

    def finish_first(w, h):
        at = first_axis(w, h)[0]
        for k in range(2, 6):
            first_ring(w, h, k).wait_recv()
        for s in range(2):
            mid[w, h, 2 * s:2 * s + 2] = (
                held(w, h, at, s)[...].astype(F32)
                + first_in[w, h, s, 2].astype(F32) + first_in[w, h, 1 - s, 1].astype(F32)
            ).astype(BF16)
        for k in range(4):
            second_ring(w, h, k).start()

    def forward_second(w, h):
        at = second_axis(w, h)[0]
        for d in range(2):
            second_ring(w, h, d).wait_recv()
            own = middle(w, h, (at + (1, 3)[d]) % 4, d)[...]
            second_fwd[w, h, d] = (second_in[w, h, d, 0].astype(F32) + own.astype(F32)).astype(BF16)
            second_ring(w, h, 4 + d).start()

    def z_copy(w, h):
        to = 2 * w + h
        slot = (to + 8 - z) % 8
        return remote(
            last.at[to], last_in.at[slot], z_send.at[to], z_recv.at[slot], device(to, y, x, core)
        )

    def finish_second(w, h):
        at = second_axis(w, h)[0]
        for k in range(2, 6):
            second_ring(w, h, k).wait_recv()
        for s in range(2):
            last[2 * w + h, :, s * 512:(s + 1) * 512] = (
                middle(w, h, at, s)[...].astype(F32)
                + second_in[w, h, s, 2].astype(F32) + second_in[w, h, 1 - s, 1].astype(F32)
            ).astype(BF16)

        @pl.when(z != 2 * w + h)
        def _():
            z_copy(w, h).start()

    def unproject(start, count):
        def block(n):
            columns = pl.ds(pl.multiple_of(n * 256, 256), 256)
            total = nt(grad_query[start:start + count, :], wq[columns, :])
            total = total + nt(grad_key[start:start + count, :], wk[columns, :])
            total = total + nt(grad_value[start:start + count, :], wv[columns, :])
            total = total * gain[:, columns]
            for t in range(2):
                row = pl.multiple_of((2 * n + t) * FRAMES + start, 8)
                turn[pl.ds(row, count), :] = total[:, t * 128:(t + 1) * 128]

        loop(4, block)

    def rows_back(i):
        mean = stats[0, i][:, :1]
        inv_scale = stats[1, i][:, :1]
        standard = (x_in[i].astype(F32) - mean) * inv_scale
        tiles = [turn[pl.ds(t * FRAMES + i * LOCAL, LOCAL), :] for t in range(TILES)]
        grad_standard = jnp.concatenate(tiles, 1)
        grad = dy_in[i].astype(F32) + inv_scale * (
            grad_standard
            - jnp.mean(grad_standard, -1, keepdims=True)
            - standard * jnp.mean(grad_standard * standard, -1, keepdims=True)
        )
        back_out[i] = grad.astype(BF16)

    def back_copy(i):
        _, peer = member(i, -1)
        return remote(back_out.at[i], back_in.at[me], back_send.at[i], back_recv.at[i], peer)

    def send_back(i):
        rows_back(i)
        back_copy(i).start()

    own_copy = pltpu.make_async_copy(back_out.at[0], back_in.at[me], back_send.at[0])

    for unit in ((3, 0), (3, 1)):
        product(*unit)
    loop(PAIRS // 2, lambda i: backward_late(2 * i))
    for unit in ((3, 0), (3, 1)):
        start_unit(*unit)
    evens, odds, outs = ((2, 0), (1, 0), (0, 0)), ((2, 1), (1, 1), (0, 1)), ((3, 0), (3, 1))
    for unit in evens:
        product(*unit)
    loop(PAIRS // 2, lambda i: backward_late(2 * i + 1))
    for unit in outs:
        forward_first(*unit)
    for unit in evens:
        start_unit(*unit)
    for unit in odds:
        product(*unit)
    unproject(FRAMES // 2, FRAMES // 2)
    for i in range(GROUP // 2, GROUP):
        send_back(i)
    for unit in odds:
        start_unit(*unit)
    unproject(0, FRAMES // 2)
    for i in list(range(4, GROUP // 2)) + [1, 2, 3]:
        send_back(i)
    rows_back(0)
    own_copy.start()
    for unit in outs:
        finish_first(*unit)
    for unit in evens:
        forward_first(*unit)
    for unit in outs:
        forward_second(*unit)
    for unit in odds:
        forward_first(*unit)
    for unit in outs:
        finish_second(*unit)
    for unit in evens:
        finish_first(*unit)
    for unit in evens:
        forward_second(*unit)
    for unit in odds:
        finish_first(*unit)
    for unit in evens:
        finish_second(*unit)
    for unit in odds:
        forward_second(*unit)
    for unit in odds:
        finish_second(*unit)

    total = last[z].astype(F32)
    for o in range(1, 8):
        remote(
            last.at[0], last_in.at[o], z_send.at[0], z_recv.at[o], device((z + o) % 8, y, x, core)
        ).wait_recv()
        total = total + last_in[o].astype(F32)
    sums_ref[...] = total * scale

    own_copy.wait()
    for i in range(1, GROUP):
        back_copy(i).wait_recv()
    for i in range(1, GROUP):
        in_copy(0, i).wait_send()
        in_copy(1, i).wait_send()
        back_copy(i).wait_send()
    for w in range(4):
        for h in range(2):
            core_copy(w, h).wait_send()
            for k in range(6):
                first_ring(w, h, k).wait_send()
                second_ring(w, h, k).wait_send()

            @pl.when(z != 2 * w + h)
            def _():
                z_copy(w, h).wait_send()


def frames_first(back, sums, grad, sums_out, turn):
    tiles = back.shape[2] // 128

    def position(p):
        rows = back[p].astype(F32)
        for t in range(tiles):
            turn[pl.ds(t * FRAMES + p, LOCAL, stride=GROUP), :] = rows[:, t * 128:(t + 1) * 128]

    loop(GROUP, position)

    def frame(f):
        rows = [turn[pl.ds(pl.multiple_of(t * FRAMES + f * GROUP, 16), GROUP), :] for t in range(tiles)]
        grad[f] = jnp.concatenate(rows, 1).astype(BF16)

    loop(LOCAL, frame)
    sums_out[...] = sums[...].T


def shards(tokens, cotangent, norm_gain, query_weight, key_weight, value_weight, out_weight):
    total_rows = FRAMES * lax.axis_size("tm") * lax.axis_size("space")
    anywhere = pl.BlockSpec(memory_space=pl.ANY)
    vmem = pl.BlockSpec(memory_space=pltpu.VMEM)
    dma = pltpu.SemaphoreType.DMA
    rows = pltpu.VMEM((FRAMES, D), BF16)
    block = pltpu.VMEM((GROUP, LOCAL, D), BF16)
    weight = pltpu.VMEM((D, D), BF16)
    back, sums = pl.pallas_call(
        functools.partial(kernel, 1.0 / math.sqrt(total_rows)),
        out_shape=(
            jax.ShapeDtypeStruct((GROUP, LOCAL, D), BF16),
            jax.ShapeDtypeStruct((16, D), F32),
        ),
        in_specs=[anywhere, anywhere, vmem] + [anywhere] * 4,
        out_specs=(anywhere, vmem),
        scratch_shapes=[
            pltpu.VMEM((2, LOCAL, GROUP, D), BF16),
            pltpu.VMEM((TILES * FRAMES, 128), F32),
            block, block, block, block, block,
            pltpu.VMEM((2, GROUP, LOCAL, 128), F32),
            weight, weight, weight, weight,
            rows, rows, rows, rows, rows, rows, rows, rows, rows, rows,
            pltpu.VMEM((PAIRS, FRAMES, 2 * FRAMES), F32),
            pltpu.VMEM((PAIRS, FRAMES, 2 * FRAMES), BF16),
            pltpu.VMEM((FRAMES, 2 * FRAMES), BF16),
            pltpu.VMEM((4, 4, 2, 4, 2, 16, D), BF16),
            pltpu.VMEM((4, 4, 2, 4, 16, D), BF16),
            pltpu.VMEM((4, 2, 2, 3, 2, 16, D), BF16),
            pltpu.VMEM((4, 2, 2, 2, 16, D), BF16),
            pltpu.VMEM((4, 2, 4, 16, D), BF16),
            pltpu.VMEM((4, 2, 2, 3, 16, D // 2), BF16),
            pltpu.VMEM((4, 2, 2, 16, D // 2), BF16),
            pltpu.VMEM((8, 16, D), BF16),
            pltpu.VMEM((8, 16, D), BF16),
            dma((6,)), dma((2, 16)), dma((2, 16)), dma((16,)), dma((16,)),
            dma((4, 2)), dma((4, 2)),
            dma((4, 2, 2, 3)), dma((4, 2, 2, 3)),
            dma((4, 2, 2, 3)), dma((4, 2, 2, 3)),
            dma((8,)), dma((8,)),
        ],
        compiler_params=pltpu.CompilerParams(
            collective_id=0, has_side_effects=True, vmem_limit_bytes=61 * 1024 * 1024
        ),
    )(tokens, cotangent, norm_gain.reshape(1, D), query_weight, key_weight, value_weight, out_weight)
    steps = 4
    wide = D // steps
    return pl.pallas_call(
        frames_first,
        grid=(steps,),
        out_shape=(
            jax.ShapeDtypeStruct((LOCAL, GROUP, D), BF16),
            jax.ShapeDtypeStruct((D, 16), F32),
        ),
        in_specs=[
            pl.BlockSpec((GROUP, LOCAL, wide), lambda n: (0, 0, n)),
            pl.BlockSpec((16, wide), lambda n: (0, n)),
        ],
        out_specs=(
            pl.BlockSpec((LOCAL, GROUP, wide), lambda n: (0, 0, n)),
            pl.BlockSpec((wide, 16), lambda n: (n, 0)),
        ),
        scratch_shapes=[pltpu.VMEM((wide // 128 * FRAMES, 128), F32)],
        compiler_params=pltpu.CompilerParams(vmem_limit_bytes=16 * 1024 * 1024),
    )(back, sums)


def solution(mesh):
    in_specs = (P("tm", "space", None), P("tm", "space", None), P(), P(), P(), P(), P())
    out_specs = (P("tm", "space", None), P(None, ("tm", "space")))
    return jax.shard_map(shards, mesh=mesh, in_specs=in_specs, out_specs=out_specs, check_vma=False)
```

```python
import functools
import math

import jax
import jax.numpy as jnp
from jax import lax
from jax.experimental import pallas as pl
from jax.experimental.pallas import tpu as pltpu
from jax.sharding import PartitionSpec as P

H = 16
D = 1024
HEAD = D // H
PAIRS = H // 2
LOCAL = 24
GROUP = 16
FRAMES = LOCAL * GROUP
TILES = D // 128
EPS = 1e-06
EARLY = 256
LATE = FRAMES - EARLY
OFFSETS = (
    (0, 0), (0, 1), (0, 2), (0, 3),
    (1, 0), (3, 0), (1, 1), (3, 1), (1, 2), (3, 2), (1, 3),
    (3, 3), (2, 0), (2, 1), (2, 2), (2, 3),
)
SEND_ORDER = tuple(range(4, 11)) + (1, 2, 3) + tuple(range(11, 16))
X_FIRST = ((False, False), (True, True), (True, False), (True, False))
MESH = pl.DeviceIdType.MESH
BF16 = jnp.bfloat16
F32 = jnp.float32


def nn(left, right):
    return lax.dot_general(left, right, (((1,), (0,)), ((), ())), preferred_element_type=F32)


def nt(left, right):
    return lax.dot_general(left, right, (((1,), (1,)), ((), ())), preferred_element_type=F32)


def tn(left, right):
    return lax.dot_general(left, right, (((0,), (0,)), ((), ())), preferred_element_type=F32)


def place():
    tm = lax.axis_index("tm")
    space = lax.axis_index("space")
    return (tm // 4) * 2 + space // 8, tm % 4, (space // 2) % 4, space % 2


def device(z, y, x, core):
    return ((z // 2) * 4 + y, ((z % 2) * 4 + x) * 2 + core)


def remote(src, dst, send, recv, to):
    return pltpu.make_async_remote_copy(
        src_ref=src, dst_ref=dst, send_sem=send, recv_sem=recv, device_id=to, device_id_type=MESH
    )


def loop(count, body, unroll=1):
    def step(i, carry):
        body(i)
        return carry

    lax.fori_loop(0, count, step, 0, unroll=unroll)


def kernel(
    scale,
    tokens, cotangent, gain, wq_hbm, wk_hbm, wv_hbm, wo_hbm,
    back_in, sums_ref,
    raw, turn, x_out, dy_out, x_in, dy_in, back_out, stats,
    wq, wk, wv, wo,
    normed, query, key, value, mixed, dy, grad_mixed, grad_query, grad_key, grad_value,
    weights, lows, low_early,
    part, pair, first_in, first_fwd, mid, second_in, last, last_in,
    load_sem, in_send, in_recv, back_send, back_recv,
    core_send, core_recv, first_send, first_recv, second_send, second_recv, z_send, z_recv,
):
    z, y, x, core = place()
    z_hi, z_lo = z // 2, z % 2
    me = z_hi * 4 + y
    partner = device(z, y, x, 1 - core)
    x_next, x_prev = device(z, y, (x + 1) % 4, core), device(z, y, (x + 3) % 4, core)
    y_next, y_prev = device(z, (y + 1) % 4, x, core), device(z, (y + 3) % 4, x, core)

    def member(i, sign):
        a, b = OFFSETS[i]
        to_z, to_y = (z_hi + 4 + sign * a) % 4, (y + 4 + sign * b) % 4
        return to_z * 4 + to_y, device(to_z * 2 + z_lo, to_y, x, core)

    loads = [
        pltpu.make_async_copy(tokens, raw.at[0], load_sem.at[0]),
        pltpu.make_async_copy(cotangent, raw.at[1], load_sem.at[1]),
        pltpu.make_async_copy(wq_hbm, wq, load_sem.at[2]),
        pltpu.make_async_copy(wk_hbm, wk, load_sem.at[3]),
        pltpu.make_async_copy(wv_hbm, wv, load_sem.at[4]),
        pltpu.make_async_copy(wo_hbm, wo, load_sem.at[5]),
    ]
    for load in loads:
        load.start()

    barrier = pltpu.get_barrier_semaphore()
    peers = [member(i, 1)[1] for i in range(1, GROUP)]
    peers += [partner, x_next, x_prev, device(z, y, (x + 2) % 4, core)] + [device((z + o) % 8, y, x, core) for o in (1, 3, 5, 7)]
    for peer in peers:
        pl.semaphore_signal(barrier, inc=1, device_id=peer, device_id_type=MESH)

    def positions_first(which, target):
        def frame(f):
            rows = raw[which, f].astype(F32)
            for t in range(TILES):
                turn[pl.ds(pl.multiple_of(t * FRAMES + f * GROUP, 16), GROUP), :] = rows[:, t * 128:(t + 1) * 128]

        loop(LOCAL, frame)

        def position(p):
            rows = [turn[pl.ds(t * FRAMES + p, LOCAL, stride=GROUP), :] for t in range(TILES)]
            target[p] = jnp.concatenate(rows, 1).astype(BF16)

        loop(GROUP, position)

    def in_copy(which, i):
        to, peer = member(i, 1)
        source, target = ((x_out, x_in), (dy_out, dy_in))[which]
        return remote(source.at[to], target.at[i], in_send.at[which, i], in_recv.at[which, i], peer)

    loads[0].wait()
    positions_first(0, x_out)
    pl.semaphore_wait(barrier, len(peers))
    for i in SEND_ORDER:
        in_copy(0, i).start()
    x_in[0] = x_out[me]
    loads[1].wait()
    positions_first(1, dy_out)
    for i in SEND_ORDER:
        in_copy(1, i).start()
    dy_in[0] = dy_out[me]

    def normalise(i):
        rows = []
        for j in range(2):
            floated = x_in[2 * i + j].astype(F32)
            mean = jnp.mean(floated, -1, keepdims=True)
            centred = floated - mean
            inv_scale = lax.rsqrt(jnp.mean(centred * centred, -1, keepdims=True) + EPS)
            stats[0, 2 * i + j] = jnp.broadcast_to(mean, (LOCAL, 128))
            stats[1, 2 * i + j] = jnp.broadcast_to(inv_scale, (LOCAL, 128))
            rows.append(centred * inv_scale * gain[...])
        normed[pl.ds(i * 48, 48), :] = jnp.concatenate(rows, 0).astype(BF16)

    def project(start, count):
        def block(n):
            columns = pl.ds(pl.multiple_of(n * 256, 256), 256)
            rows = normed[start:start + count, :]
            query[start:start + count, columns] = (nn(rows, wq[:, columns]) * (1.0 / math.sqrt(HEAD))).astype(BF16)
            key[start:start + count, columns] = nn(rows, wk[:, columns]).astype(BF16)
            value[start:start + count, columns] = nn(rows, wv[:, columns]).astype(BF16)

        loop(4, block, 4)

    for i in range(GROUP // 2):
        for j in range(2):
            if i + j > 0:
                in_copy(0, 2 * i + j).wait_recv()
        if i == 0:
            for load in loads[2:5]:
                load.wait()
        normalise(i)
        if 48 * i < EARLY <= 48 * (i + 1):
            project(0, EARLY)
    project(EARLY, LATE)

    def spread(rows):
        first = lax.broadcasted_iota(jnp.int32, rows.shape, 1) < HEAD
        zero = jnp.zeros_like(rows)
        return jnp.concatenate([jnp.where(first, rows, zero), jnp.where(first, zero, rows)], 0)

    def merge(both):
        count = both.shape[0] // 2
        first = lax.broadcasted_iota(jnp.int32, (count, 128), 1) < HEAD
        return jnp.where(first, both[:count], both[count:])

    def pair_columns(p):
        return pl.ds(pl.multiple_of(p * 128, 128), 128)

    def forward(p):
        columns = pair_columns(p)
        spread_query = spread(query[:, columns])
        keys = key[:, columns]
        values, outs = value[:, columns], []
        for c in range(3):
            part_rows = slice(c * 256, (c + 1) * 256)
            scores = nt(keys, spread_query[part_rows])
            raised = jnp.exp(scores - jnp.max(scores, 0, keepdims=True))
            shares = raised * (1.0 / jnp.sum(raised, 0, keepdims=True))
            weights[p, :, part_rows] = shares
            shares = shares.astype(BF16)
            lows[p, :, part_rows] = shares
            outs.append(tn(shares, values))
        mixed[:, columns] = merge(jnp.concatenate(outs, 0)).astype(BF16)

    loop(PAIRS, forward, 8)

    def gather_dy(i):
        rows = [dy_in[2 * i + j].astype(F32) for j in range(2)]
        dy[pl.ds(i * 48, 48), :] = jnp.concatenate(rows, 0).astype(BF16)

    def project_back(start, count):
        def block(n):
            columns = pl.ds(pl.multiple_of(n * 256, 256), 256)
            grad_mixed[start:start + count, columns] = nt(dy[start:start + count, :], wo[columns, :]).astype(BF16)

        loop(4, block, 4)

    early_slots = -(-EARLY // LOCAL)
    for i in range(1, early_slots):
        in_copy(1, i).wait_recv()
    for i in range(EARLY // 48):
        gather_dy(i)
    dy[EARLY // 48 * 48:EARLY, :] = dy_in[early_slots - 1][:EARLY - LOCAL * (early_slots - 1)]
    loads[5].wait()
    project_back(0, EARLY)

    def backward_early(p):
        columns = pair_columns(p)
        spread_grad = spread(grad_mixed[:EARLY, columns])
        values, keys = value[:, columns], key[:, columns]
        both = []
        for c in range(2):
            at = slice(c * FRAMES, c * FRAMES + EARLY)
            grad_weights = nt(values, spread_grad[c * EARLY:(c + 1) * EARLY])
            shares = weights[p, :, at]
            delta = jnp.sum(shares * grad_weights, 0, keepdims=True)
            scores = shares * (grad_weights - delta)
            scores = scores.astype(BF16)
            low_early[p, :, c * EARLY:(c + 1) * EARLY] = scores
            both.append(tn(scores, keys))
        first = lax.broadcasted_iota(jnp.int32, (EARLY, 128), 1) < HEAD
        grad_query[:EARLY, columns] = (jnp.where(first, both[0], both[1]) * (1.0 / math.sqrt(HEAD))).astype(BF16)

    loop(PAIRS, backward_early, 8)

    for i in range(early_slots, GROUP):
        in_copy(1, i).wait_recv()
    for i in range(EARLY // 48, GROUP // 2):
        gather_dy(i)
    project_back(EARLY, LATE)

    def backward_value(p):
        columns = pair_columns(p)
        grad_value[:, columns] = nn(lows[p], spread(grad_mixed[:, columns])).astype(BF16)

    def backward_late(p):
        columns = pair_columns(p)
        values, keys = value[:, columns], key[:, columns]
        grad_weights = nt(values, spread(grad_mixed[EARLY:, columns]))
        shares = jnp.concatenate([weights[p, :, EARLY:FRAMES], weights[p, :, FRAMES + EARLY:]], 1)
        delta = jnp.sum(shares * grad_weights, 0, keepdims=True)
        scores = (shares * (grad_weights - delta)).astype(BF16)
        grad_query[EARLY:, columns] = (merge(tn(scores, keys)) * (1.0 / math.sqrt(HEAD))).astype(BF16)
        pieces = []
        for c in range(2):
            pieces.append(low_early[p, :, c * EARLY:(c + 1) * EARLY])
            pieces.append(scores[:, c * LATE:(c + 1) * LATE])
        grad_key[:, columns] = nn(jnp.concatenate(pieces, 1), spread(query[:, columns])).astype(BF16)

    lefts = [grad_query, grad_key, grad_value, dy]
    rights = [normed, normed, normed, mixed]

    def core_copy(w, h):
        return remote(
            part.at[w, :, h, :, 1 - core], pair.at[w, :, h], core_send.at[w, h], core_recv.at[w, h], partner
        )

    def product(w, h):
        left = lefts[w]
        for r in (0, 2):
            rows = [left[:, (r + j) * 256 + h * 128:(r + j) * 256 + h * 128 + 128] for j in range(2)]
            total = tn(jnp.concatenate(rows, 1), rights[w][...]).astype(BF16).reshape(2, 4, 2, 16, D)
            for j in range(2):
                part[w, r + j, h] = total[j]
        core_copy(w, h).start()

    def first_axis(w, h):
        return (x, x_next, x_prev) if X_FIRST[w][h] else (y, y_next, y_prev)

    def held(w, h, i, s):
        return pair.at[w, pl.ds(2 * s, 2), h, i] if X_FIRST[w][h] else pair.at[w, i, h, pl.ds(2 * s, 2)]

    def start_unit(w, h):
        core_copy(w, h).wait_recv()

        def add(n):
            r, c = n // 4, n % 4
            pair[w, r, h, c] = (part[w, r, h, c, core].astype(F32) + pair[w, r, h, c].astype(F32)).astype(BF16)

        loop(16, add, 4)
        for k in range(4):
            first_ring(w, h, k).start()

    def ring(axis, source, inbox, forwarded, send, recv, k):
        at, after, before = axis
        to, d, slot = (after, before)[k % 2], k % 2, k // 2
        if slot == 0:
            block = source((at + 2) % 4, d)
        elif slot == 1:
            block = source((at + (1, 3)[d]) % 4, 1 - d)
        else:
            block = forwarded.at[d]
        return remote(block, inbox.at[d, slot], send.at[d, slot], recv.at[d, slot], to)

    def first_ring(w, h, k):
        return ring(
            first_axis(w, h), lambda i, s: held(w, h, i, s), first_in.at[w, h], first_fwd.at[w, h],
            first_send.at[w, h], first_recv.at[w, h], k,
        )

    def second_copy(w, h, o):
        at = (y if X_FIRST[w][h] else x) + o
        to = device(z, at % 4, x, core) if X_FIRST[w][h] else device(z, y, at % 4, core)
        return remote(
            mid.at[w, h, at % 4], second_in.at[w, h, o - 1], second_send.at[w, h, o - 1], second_recv.at[w, h, o - 1], to
        )

    def forward_first(w, h):
        at = first_axis(w, h)[0]
        for d in range(2):
            first_ring(w, h, d).wait_recv()
            own = held(w, h, (at + (1, 3)[d]) % 4, d)[...]
            first_fwd[w, h, d] = (first_in[w, h, d, 0].astype(F32) + own.astype(F32)).astype(BF16)
            first_ring(w, h, 4 + d).start()

    def finish_first(w, h):
        at = first_axis(w, h)[0]
        for k in range(2, 6):
            first_ring(w, h, k).wait_recv()
        for s in range(2):
            mid[w, h, 2 * s:2 * s + 2] = (
                held(w, h, at, s)[...].astype(F32)
                + first_in[w, h, s, 2].astype(F32) + first_in[w, h, 1 - s, 1].astype(F32)
            ).astype(BF16)
        for o in (2, 1, 3):
            second_copy(w, h, o).start()

    def z_copy(w, h):
        to = 2 * w + h
        slot = (to + 8 - z) % 8
        return remote(
            last.at[to], last_in.at[slot], z_send.at[to], z_recv.at[slot], device(to, y, x, core)
        )

    def finish_second(w, h):
        total = mid[w, h, y if X_FIRST[w][h] else x].astype(F32)
        for o in range(1, 4):
            second_copy(w, h, o).wait_recv()
            total = total + second_in[w, h, o - 1].astype(F32)
        last[2 * w + h] = total.astype(BF16)

        @pl.when(z != 2 * w + h)
        def _():
            z_copy(w, h).start()

    def unproject(start, count):
        def block(n):
            columns = pl.ds(pl.multiple_of(n * 256, 256), 256)
            total = nt(grad_query[start:start + count, :], wq[columns, :])
            total = total + nt(grad_key[start:start + count, :], wk[columns, :])
            total = total + nt(grad_value[start:start + count, :], wv[columns, :])
            total = total * gain[:, columns]
            for t in range(2):
                row = pl.multiple_of((2 * n + t) * FRAMES + start, 8)
                turn[pl.ds(row, count), :] = total[:, t * 128:(t + 1) * 128]

        loop(4, block, 4)

    def rows_back(i):
        mean = stats[0, i][:, :1]
        inv_scale = stats[1, i][:, :1]
        standard = (x_in[i].astype(F32) - mean) * inv_scale
        tiles = [turn[pl.ds(t * FRAMES + i * LOCAL, LOCAL), :] for t in range(TILES)]
        grad_standard = jnp.concatenate(tiles, 1)
        grad = dy_in[i].astype(F32) + inv_scale * (
            grad_standard
            - jnp.mean(grad_standard, -1, keepdims=True)
            - standard * jnp.mean(grad_standard * standard, -1, keepdims=True)
        )
        back_out[i] = grad.astype(BF16)

    def back_copy(i):
        _, peer = member(i, -1)
        return remote(back_out.at[i], back_in.at[me], back_send.at[i], back_recv.at[i], peer)

    def send_back(i):
        rows_back(i)
        back_copy(i).start()

    own_copy = pltpu.make_async_copy(back_out.at[0], back_in.at[me], back_send.at[0])

    firsts, evens, odds = ((3, 0), (3, 1), (2, 0), (2, 1)), ((1, 0), (0, 0)), ((1, 1), (0, 1))
    for unit in firsts[:2]:
        product(*unit)
    loop(PAIRS, backward_value, 8)
    for unit in firsts[2:]:
        product(*unit)
    for unit in firsts[:2]:
        start_unit(*unit)
    loop(PAIRS // 2, lambda i: backward_late(2 * i), 4)
    for unit in firsts[2:]:
        start_unit(*unit)
    for unit in evens:
        product(*unit)
    for unit in firsts[:2]:
        forward_first(*unit)
    loop(PAIRS // 2, lambda i: backward_late(2 * i + 1), 4)
    for unit in evens:
        start_unit(*unit)
    for unit in odds:
        product(*unit)
    for unit in firsts[2:]:
        forward_first(*unit)
    unproject(FRAMES // 2, FRAMES // 2)
    for unit in odds:
        start_unit(*unit)
    for i in range(GROUP // 2, GROUP):
        send_back(i)
    for unit in firsts[:2]:
        finish_first(*unit)
    unproject(0, FRAMES // 2)
    for i in list(range(4, GROUP // 2)) + [1, 2, 3]:
        send_back(i)
    rows_back(0)
    own_copy.start()
    for unit in evens:
        forward_first(*unit)
    for unit in firsts[2:]:
        finish_first(*unit)
    for unit in firsts[:2]:
        finish_second(*unit)
    for unit in odds:
        forward_first(*unit)
    for unit in evens:
        finish_first(*unit)
    for unit in firsts[2:]:
        finish_second(*unit)
    for unit in odds:
        finish_first(*unit)
    for unit in evens + odds:
        finish_second(*unit)

    total = last[z].astype(F32)
    for o in range(1, 8):
        remote(
            last.at[0], last_in.at[o], z_send.at[0], z_recv.at[o], device((z + o) % 8, y, x, core)
        ).wait_recv()
        total = total + last_in[o].astype(F32)
    sums_ref[...] = total * scale

    own_copy.wait()
    for i in range(1, GROUP):
        back_copy(i).wait_recv()
    for i in range(1, GROUP):
        in_copy(0, i).wait_send()
        in_copy(1, i).wait_send()
        back_copy(i).wait_send()
    for w in range(4):
        for h in range(2):
            core_copy(w, h).wait_send()
            for k in range(6):
                first_ring(w, h, k).wait_send()
            for o in range(1, 4):
                second_copy(w, h, o).wait_send()

            @pl.when(z != 2 * w + h)
            def _():
                z_copy(w, h).wait_send()


def frames_first(back, sums, grad, sums_out, turn):
    tiles = back.shape[2] // 128

    def position(p):
        rows = back[p].astype(F32)
        for t in range(tiles):
            turn[pl.ds(t * FRAMES + p, LOCAL, stride=GROUP), :] = rows[:, t * 128:(t + 1) * 128]

    loop(GROUP, position)

    def frame(f):
        rows = [turn[pl.ds(pl.multiple_of(t * FRAMES + f * GROUP, 16), GROUP), :] for t in range(tiles)]
        grad[f] = jnp.concatenate(rows, 1).astype(BF16)

    loop(LOCAL, frame)
    sums_out[...] = sums[...]


def shards(tokens, cotangent, norm_gain, query_weight, key_weight, value_weight, out_weight):
    total_rows = FRAMES * lax.axis_size("tm") * lax.axis_size("space")
    anywhere = pl.BlockSpec(memory_space=pl.ANY)
    vmem = pl.BlockSpec(memory_space=pltpu.VMEM)
    dma = pltpu.SemaphoreType.DMA
    rows = pltpu.VMEM((FRAMES, D), BF16)
    block = pltpu.VMEM((GROUP, LOCAL, D), BF16)
    weight = pltpu.VMEM((D, D), BF16)
    back, sums = pl.pallas_call(
        functools.partial(kernel, 1.0 / math.sqrt(total_rows)),
        out_shape=(
            jax.ShapeDtypeStruct((GROUP, LOCAL, D), BF16),
            jax.ShapeDtypeStruct((16, D), F32),
        ),
        in_specs=[anywhere, anywhere, vmem] + [anywhere] * 4,
        out_specs=(anywhere, vmem),
        scratch_shapes=[
            pltpu.VMEM((2, LOCAL, GROUP, D), BF16),
            pltpu.VMEM((TILES * FRAMES, 128), F32),
            block, block, block, block, block,
            pltpu.VMEM((2, GROUP, LOCAL, 128), F32),
            weight, weight, weight, weight,
            rows, rows, rows, rows, rows, rows, rows, rows, rows, rows,
            pltpu.VMEM((PAIRS, FRAMES, 2 * FRAMES), F32),
            pltpu.VMEM((PAIRS, FRAMES, 2 * FRAMES), BF16),
            pltpu.VMEM((PAIRS, FRAMES, 2 * EARLY), BF16),
            pltpu.VMEM((4, 4, 2, 4, 2, 16, D), BF16),
            pltpu.VMEM((4, 4, 2, 4, 16, D), BF16),
            pltpu.VMEM((4, 2, 2, 3, 2, 16, D), BF16),
            pltpu.VMEM((4, 2, 2, 2, 16, D), BF16),
            pltpu.VMEM((4, 2, 4, 16, D), BF16),
            pltpu.VMEM((4, 2, 3, 16, D), BF16),
            pltpu.VMEM((8, 16, D), BF16),
            pltpu.VMEM((8, 16, D), BF16),
            dma((6,)), dma((2, 16)), dma((2, 16)), dma((16,)), dma((16,)),
            dma((4, 2)), dma((4, 2)),
            dma((4, 2, 2, 3)), dma((4, 2, 2, 3)),
            dma((4, 2, 3)), dma((4, 2, 3)),
            dma((8,)), dma((8,)),
        ],
        compiler_params=pltpu.CompilerParams(
            collective_id=0, has_side_effects=True, vmem_limit_bytes=63 * 1024 * 1024
        ),
    )(tokens, cotangent, norm_gain.reshape(1, D), query_weight, key_weight, value_weight, out_weight)
    steps = 4
    wide = D // steps
    grad, sums = pl.pallas_call(
        frames_first,
        grid=(steps,),
        out_shape=(
            jax.ShapeDtypeStruct((LOCAL, GROUP, D), BF16),
            jax.ShapeDtypeStruct((16, D), F32),
        ),
        in_specs=[
            pl.BlockSpec((GROUP, LOCAL, wide), lambda n: (0, 0, n)),
            pl.BlockSpec((16, wide), lambda n: (0, n)),
        ],
        out_specs=(
            pl.BlockSpec((LOCAL, GROUP, wide), lambda n: (0, 0, n)),
            pl.BlockSpec((16, wide), lambda n: (0, n)),
        ),
        scratch_shapes=[pltpu.VMEM((wide // 128 * FRAMES, 128), F32)],
        compiler_params=pltpu.CompilerParams(vmem_limit_bytes=62 * 1024 * 1024),
    )(back, sums)
    return grad, sums.T


def solution(mesh):
    in_specs = (P("tm", "space", None), P("tm", "space", None), P(), P(), P(), P(), P())
    out_specs = (P("tm", "space", None), P(None, ("tm", "space")))
    return jax.shard_map(shards, mesh=mesh, in_specs=in_specs, out_specs=out_specs, check_vma=False)
```

```python
import functools
import math

import jax
import jax.numpy as jnp
from jax import lax
from jax.experimental import pallas as pl
from jax.experimental.pallas import tpu as pltpu
from jax.sharding import PartitionSpec as P

H = 16
D = 1024
HEAD = D // H
PAIRS = H // 2
LOCAL = 24
GROUP = 16
FRAMES = LOCAL * GROUP
TILES = D // 128
EPS = 1e-06
EARLY = 256
LATE = FRAMES - EARLY
OFFSETS = (
    (0, 0), (0, 1), (0, 2), (0, 3),
    (1, 0), (3, 0), (1, 1), (3, 1), (1, 2), (3, 2), (1, 3),
    (3, 3), (2, 0), (2, 1), (2, 2), (2, 3),
)
SEND_ORDER = tuple(range(4, 11)) + (1, 2, 3) + tuple(range(11, 16))
X_FIRST = ((False, True), (True, True), (True, False), (True, False))
MESH = pl.DeviceIdType.MESH
BF16 = jnp.bfloat16
F32 = jnp.float32


def nn(left, right):
    return lax.dot_general(left, right, (((1,), (0,)), ((), ())), preferred_element_type=F32)


def nt(left, right):
    return lax.dot_general(left, right, (((1,), (1,)), ((), ())), preferred_element_type=F32)


def tn(left, right):
    return lax.dot_general(left, right, (((0,), (0,)), ((), ())), preferred_element_type=F32)


def place():
    tm = lax.axis_index("tm")
    space = lax.axis_index("space")
    return (tm // 4) * 2 + space // 8, tm % 4, (space // 2) % 4, space % 2


def device(z, y, x, core):
    return ((z // 2) * 4 + y, ((z % 2) * 4 + x) * 2 + core)


def remote(src, dst, send, recv, to):
    return pltpu.make_async_remote_copy(
        src_ref=src, dst_ref=dst, send_sem=send, recv_sem=recv, device_id=to, device_id_type=MESH
    )


def loop(count, body, unroll=1):
    def step(i, carry):
        body(i)
        return carry

    lax.fori_loop(0, count, step, 0, unroll=unroll)


def kernel(
    scale,
    tokens, cotangent, gain, wq_hbm, wk_hbm, wv_hbm, wo_hbm,
    back_in, sums_ref,
    raw, turn, x_out, dy_out, x_in, dy_in, back_out, stats,
    wq, wk, wv, wo,
    normed, query, key, value, mixed, dy, grad_mixed, grad_query, grad_key, grad_value,
    weights, lows, low_early,
    part, pair, first_in, first_fwd, mid, second_in, last, last_in,
    load_sem, in_send, in_recv, back_send, back_recv,
    core_send, core_recv, first_send, first_recv, second_send, second_recv, z_send, z_recv,
):
    z, y, x, core = place()
    z_hi, z_lo = z // 2, z % 2
    me = z_hi * 4 + y
    partner = device(z, y, x, 1 - core)
    x_next, x_prev = device(z, y, (x + 1) % 4, core), device(z, y, (x + 3) % 4, core)
    y_next, y_prev = device(z, (y + 1) % 4, x, core), device(z, (y + 3) % 4, x, core)

    def member(i, sign):
        a, b = OFFSETS[i]
        to_z, to_y = (z_hi + 4 + sign * a) % 4, (y + 4 + sign * b) % 4
        return to_z * 4 + to_y, device(to_z * 2 + z_lo, to_y, x, core)

    loads = [
        pltpu.make_async_copy(tokens, raw.at[0], load_sem.at[0]),
        pltpu.make_async_copy(cotangent, raw.at[1], load_sem.at[1]),
        pltpu.make_async_copy(wq_hbm, wq, load_sem.at[2]),
        pltpu.make_async_copy(wk_hbm, wk, load_sem.at[3]),
        pltpu.make_async_copy(wv_hbm, wv, load_sem.at[4]),
        pltpu.make_async_copy(wo_hbm, wo, load_sem.at[5]),
    ]
    for load in loads:
        load.start()

    barrier = pltpu.get_barrier_semaphore()
    peers = [member(i, 1)[1] for i in range(1, GROUP)]
    peers += [partner, x_next, x_prev, device(z, y, (x + 2) % 4, core)] + [device((z + o) % 8, y, x, core) for o in (1, 3, 5, 7)]
    for peer in peers:
        pl.semaphore_signal(barrier, inc=1, device_id=peer, device_id_type=MESH)

    def positions_first(which, target):
        def frame(f):
            rows = raw[which, f].astype(F32)
            for t in range(TILES):
                turn[pl.ds(pl.multiple_of(t * FRAMES + f * GROUP, 16), GROUP), :] = rows[:, t * 128:(t + 1) * 128]

        loop(LOCAL, frame, 4)

        def position(p):
            rows = [turn[pl.ds(t * FRAMES + p, LOCAL, stride=GROUP), :] for t in range(TILES)]
            target[p] = jnp.concatenate(rows, 1).astype(BF16)

        loop(GROUP, position, 4)

    def in_copy(which, i):
        to, peer = member(i, 1)
        source, target = ((x_out, x_in), (dy_out, dy_in))[which]
        return remote(source.at[to], target.at[i], in_send.at[which, i], in_recv.at[which, i], peer)

    loads[0].wait()
    positions_first(0, x_out)
    pl.semaphore_wait(barrier, len(peers))
    for i in SEND_ORDER:
        in_copy(0, i).start()
    x_in[0] = x_out[me]
    loads[1].wait()
    positions_first(1, dy_out)
    for i in SEND_ORDER:
        in_copy(1, i).start()
    dy_in[0] = dy_out[me]

    def normalise(i):
        rows = []
        for j in range(2):
            floated = x_in[2 * i + j].astype(F32)
            mean = jnp.mean(floated, -1, keepdims=True)
            centred = floated - mean
            inv_scale = lax.rsqrt(jnp.mean(centred * centred, -1, keepdims=True) + EPS)
            stats[0, 2 * i + j] = jnp.broadcast_to(mean, (LOCAL, 128))
            stats[1, 2 * i + j] = jnp.broadcast_to(inv_scale, (LOCAL, 128))
            rows.append(centred * inv_scale * gain[...])
        normed[pl.ds(i * 48, 48), :] = jnp.concatenate(rows, 0).astype(BF16)

    def project(start, count):
        def block(n):
            columns = pl.ds(pl.multiple_of(n * 256, 256), 256)
            rows = normed[start:start + count, :]
            query[start:start + count, columns] = (nn(rows, wq[:, columns]) * (1.0 / math.sqrt(HEAD))).astype(BF16)
            key[start:start + count, columns] = nn(rows, wk[:, columns]).astype(BF16)
            value[start:start + count, columns] = nn(rows, wv[:, columns]).astype(BF16)

        loop(4, block, 4)

    for i in range(GROUP // 2):
        for j in range(2):
            if i + j > 0:
                in_copy(0, 2 * i + j).wait_recv()
        if i == 0:
            for load in loads[2:5]:
                load.wait()
        normalise(i)
        if 48 * i < EARLY <= 48 * (i + 1):
            project(0, EARLY)
    project(EARLY, LATE)

    def spread(rows):
        first = lax.broadcasted_iota(jnp.int32, rows.shape, 1) < HEAD
        zero = jnp.zeros_like(rows)
        return jnp.concatenate([jnp.where(first, rows, zero), jnp.where(first, zero, rows)], 0)

    def merge(both):
        count = both.shape[0] // 2
        first = lax.broadcasted_iota(jnp.int32, (count, 128), 1) < HEAD
        return jnp.where(first, both[:count], both[count:])

    def pair_columns(p):
        return pl.ds(pl.multiple_of(p * 128, 128), 128)

    def forward(p):
        columns = pair_columns(p)
        spread_query = spread(query[:, columns])
        keys = key[:, columns]
        values, outs = value[:, columns], []
        for c in range(3):
            part_rows = slice(c * 256, (c + 1) * 256)
            scores = nt(keys, spread_query[part_rows])
            raised = jnp.exp(scores - jnp.max(scores, 0, keepdims=True))
            shares = raised * (1.0 / jnp.sum(raised, 0, keepdims=True))
            weights[p, :, part_rows] = shares
            shares = shares.astype(BF16)
            lows[p, :, part_rows] = shares
            outs.append(tn(shares, values))
        mixed[:, columns] = merge(jnp.concatenate(outs, 0)).astype(BF16)

    loop(PAIRS, forward, 8)

    def gather_dy(i):
        rows = [dy_in[2 * i + j].astype(F32) for j in range(2)]
        dy[pl.ds(i * 48, 48), :] = jnp.concatenate(rows, 0).astype(BF16)

    def project_back(start, count):
        def block(n):
            columns = pl.ds(pl.multiple_of(n * 256, 256), 256)
            grad_mixed[start:start + count, columns] = nt(dy[start:start + count, :], wo[columns, :]).astype(BF16)

        loop(4, block, 4)

    early_slots = -(-EARLY // LOCAL)
    for i in range(1, early_slots):
        in_copy(1, i).wait_recv()
    for i in range(EARLY // 48):
        gather_dy(i)
    dy[EARLY // 48 * 48:EARLY, :] = dy_in[early_slots - 1][:EARLY - LOCAL * (early_slots - 1)]
    loads[5].wait()
    project_back(0, EARLY)

    def backward_early(p):
        columns = pair_columns(p)
        spread_grad = spread(grad_mixed[:EARLY, columns])
        values, keys = value[:, columns], key[:, columns]
        both = []
        for c in range(2):
            at = slice(c * FRAMES, c * FRAMES + EARLY)
            grad_weights = nt(values, spread_grad[c * EARLY:(c + 1) * EARLY])
            shares = weights[p, :, at]
            delta = jnp.sum(shares * grad_weights, 0, keepdims=True)
            scores = shares * (grad_weights - delta)
            scores = scores.astype(BF16)
            low_early[p, :, c * EARLY:(c + 1) * EARLY] = scores
            both.append(tn(scores, keys))
        first = lax.broadcasted_iota(jnp.int32, (EARLY, 128), 1) < HEAD
        grad_query[:EARLY, columns] = (jnp.where(first, both[0], both[1]) * (1.0 / math.sqrt(HEAD))).astype(BF16)

    loop(PAIRS, backward_early, 8)

    for i in range(early_slots, GROUP):
        in_copy(1, i).wait_recv()
    for i in range(EARLY // 48, GROUP // 2):
        gather_dy(i)
    def backward_value(p):
        columns = pair_columns(p)
        grad_value[:, columns] = nn(lows[p], spread(grad_mixed[:, columns])).astype(BF16)

    def backward_late(p):
        columns = pair_columns(p)
        values, keys = value[:, columns], key[:, columns]
        grad_weights = nt(values, spread(grad_mixed[EARLY:, columns]))
        shares = jnp.concatenate([weights[p, :, EARLY:FRAMES], weights[p, :, FRAMES + EARLY:]], 1)
        delta = jnp.sum(shares * grad_weights, 0, keepdims=True)
        scores = (shares * (grad_weights - delta)).astype(BF16)
        grad_query[EARLY:, columns] = (merge(tn(scores, keys)) * (1.0 / math.sqrt(HEAD))).astype(BF16)
        pieces = []
        for c in range(2):
            pieces.append(low_early[p, :, c * EARLY:(c + 1) * EARLY])
            pieces.append(scores[:, c * LATE:(c + 1) * LATE])
        grad_key[:, columns] = nn(jnp.concatenate(pieces, 1), spread(query[:, columns])).astype(BF16)

    lefts = [grad_query, grad_key, grad_value, dy]
    rights = [normed, normed, normed, mixed]

    def core_copy(w, h):
        return remote(
            part.at[w, :, h, :, 1 - core], pair.at[w, :, h], core_send.at[w, h], core_recv.at[w, h], partner
        )

    def product(w, h):
        left = lefts[w]
        for r in (0, 2):
            rows = [left[:, (r + j) * 256 + h * 128:(r + j) * 256 + h * 128 + 128] for j in range(2)]
            total = tn(jnp.concatenate(rows, 1), rights[w][...]).astype(BF16).reshape(2, 4, 2, 16, D)
            for j in range(2):
                part[w, r + j, h] = total[j]
        core_copy(w, h).start()

    def first_axis(w, h):
        return (x, x_next, x_prev) if X_FIRST[w][h] else (y, y_next, y_prev)

    def held(w, h, i, s):
        return pair.at[w, pl.ds(2 * s, 2), h, i] if X_FIRST[w][h] else pair.at[w, i, h, pl.ds(2 * s, 2)]

    def start_unit(w, h):
        core_copy(w, h).wait_recv()

        def add(n):
            r, c = n // 4, n % 4
            pair[w, r, h, c] = (part[w, r, h, c, core].astype(F32) + pair[w, r, h, c].astype(F32)).astype(BF16)

        loop(16, add, 4)
        for k in range(4):
            first_ring(w, h, k).start()

    def ring(axis, source, inbox, forwarded, send, recv, k):
        at, after, before = axis
        to, d, slot = (after, before)[k % 2], k % 2, k // 2
        if slot == 0:
            block = source((at + 2) % 4, d)
        elif slot == 1:
            block = source((at + (1, 3)[d]) % 4, 1 - d)
        else:
            block = forwarded.at[d]
        return remote(block, inbox.at[d, slot], send.at[d, slot], recv.at[d, slot], to)

    def first_ring(w, h, k):
        return ring(
            first_axis(w, h), lambda i, s: held(w, h, i, s), first_in.at[w, h], first_fwd.at[w, h],
            first_send.at[w, h], first_recv.at[w, h], k,
        )

    def second_copy(w, h, o):
        at = (y if X_FIRST[w][h] else x) + o
        to = device(z, at % 4, x, core) if X_FIRST[w][h] else device(z, y, at % 4, core)
        return remote(
            mid.at[w, h, at % 4], second_in.at[w, h, o - 1], second_send.at[w, h, o - 1], second_recv.at[w, h, o - 1], to
        )

    def forward_first(w, h):
        at = first_axis(w, h)[0]
        for d in range(2):
            first_ring(w, h, d).wait_recv()
            own = held(w, h, (at + (1, 3)[d]) % 4, d)[...]
            first_fwd[w, h, d] = (first_in[w, h, d, 0].astype(F32) + own.astype(F32)).astype(BF16)
            first_ring(w, h, 4 + d).start()

    def finish_first(w, h):
        at = first_axis(w, h)[0]
        for k in range(2, 6):
            first_ring(w, h, k).wait_recv()
        for s in range(2):
            mid[w, h, 2 * s:2 * s + 2] = (
                held(w, h, at, s)[...].astype(F32)
                + first_in[w, h, s, 2].astype(F32) + first_in[w, h, 1 - s, 1].astype(F32)
            ).astype(BF16)
        for o in (2, 1, 3):
            second_copy(w, h, o).start()

    def z_copy(w, h):
        to = 2 * w + h
        slot = (to + 8 - z) % 8
        return remote(
            last.at[to], last_in.at[slot], z_send.at[to], z_recv.at[slot], device(to, y, x, core)
        )

    def finish_second(w, h):
        total = mid[w, h, y if X_FIRST[w][h] else x].astype(F32)
        for o in range(1, 4):
            second_copy(w, h, o).wait_recv()
            total = total + second_in[w, h, o - 1].astype(F32)
        last[2 * w + h] = total.astype(BF16)

        @pl.when(z != 2 * w + h)
        def _():
            z_copy(w, h).start()

    def unproject(start, count):
        def block(n):
            columns = pl.ds(pl.multiple_of(n * 256, 256), 256)
            total = nt(grad_query[start:start + count, :], wq[columns, :])
            total = total + nt(grad_key[start:start + count, :], wk[columns, :])
            total = total + nt(grad_value[start:start + count, :], wv[columns, :])
            total = total * gain[:, columns]
            for t in range(2):
                row = pl.multiple_of((2 * n + t) * FRAMES + start, 8)
                turn[pl.ds(row, count), :] = total[:, t * 128:(t + 1) * 128]

        loop(4, block, 4)

    def rows_back(i):
        mean = stats[0, i][:, :1]
        inv_scale = stats[1, i][:, :1]
        standard = (x_in[i].astype(F32) - mean) * inv_scale
        tiles = [turn[pl.ds(t * FRAMES + i * LOCAL, LOCAL), :] for t in range(TILES)]
        grad_standard = jnp.concatenate(tiles, 1)
        grad = dy_in[i].astype(F32) + inv_scale * (
            grad_standard
            - jnp.mean(grad_standard, -1, keepdims=True)
            - standard * jnp.mean(grad_standard * standard, -1, keepdims=True)
        )
        back_out[i] = grad.astype(BF16)

    def back_copy(i):
        _, peer = member(i, -1)
        return remote(back_out.at[i], back_in.at[me], back_send.at[i], back_recv.at[i], peer)

    def send_back(i):
        rows_back(i)
        back_copy(i).start()

    own_copy = pltpu.make_async_copy(back_out.at[0], back_in.at[me], back_send.at[0])

    firsts, evens, odds = ((3, 0), (3, 1), (2, 0), (2, 1)), ((1, 0), (0, 0)), ((1, 1), (0, 1))
    for unit in firsts[:2]:
        product(*unit)
    project_back(EARLY, LATE)
    loop(PAIRS, backward_value, 8)
    for unit in firsts[2:]:
        product(*unit)
    for unit in firsts[:2]:
        start_unit(*unit)
    loop(PAIRS // 2, lambda i: backward_late(2 * i), 4)
    for unit in firsts[2:]:
        start_unit(*unit)
    for unit in evens:
        product(*unit)
    for unit in firsts[:2]:
        forward_first(*unit)
    loop(PAIRS // 2, lambda i: backward_late(2 * i + 1), 4)
    for unit in evens:
        start_unit(*unit)
    for unit in odds:
        product(*unit)
    for unit in firsts[2:]:
        forward_first(*unit)
    for unit in odds:
        start_unit(*unit)
    unproject(FRAMES // 2, FRAMES // 2)
    for i in range(GROUP // 2, GROUP):
        send_back(i)
    for unit in evens:
        forward_first(*unit)
    for unit in firsts[:2]:
        finish_first(*unit)
    unproject(0, FRAMES // 2)
    for i in list(range(4, GROUP // 2)) + [1, 2, 3]:
        send_back(i)
    rows_back(0)
    own_copy.start()
    for unit in odds:
        forward_first(*unit)
    for unit in firsts[2:] + evens:
        finish_first(*unit)
    for unit in firsts[:2]:
        finish_second(*unit)
    for unit in odds:
        finish_first(*unit)
    for unit in firsts[2:] + evens + odds:
        finish_second(*unit)

    total = last[z].astype(F32)
    for o in range(1, 8):
        remote(
            last.at[0], last_in.at[o], z_send.at[0], z_recv.at[o], device((z + o) % 8, y, x, core)
        ).wait_recv()
        total = total + last_in[o].astype(F32)
    sums_ref[...] = total * scale

    own_copy.wait()
    for i in range(1, GROUP):
        back_copy(i).wait_recv()
    for i in range(1, GROUP):
        in_copy(0, i).wait_send()
        in_copy(1, i).wait_send()
        back_copy(i).wait_send()
    for w in range(4):
        for h in range(2):
            core_copy(w, h).wait_send()
            for k in range(6):
                first_ring(w, h, k).wait_send()
            for o in range(1, 4):
                second_copy(w, h, o).wait_send()

            @pl.when(z != 2 * w + h)
            def _():
                z_copy(w, h).wait_send()


def frames_first(back, sums, grad, sums_out, turn):
    tiles = back.shape[2] // 128

    def position(p):
        rows = back[p].astype(F32)
        for t in range(tiles):
            turn[pl.ds(t * FRAMES + p, LOCAL, stride=GROUP), :] = rows[:, t * 128:(t + 1) * 128]

    loop(GROUP, position, 4)

    def frame(f):
        rows = [turn[pl.ds(pl.multiple_of(t * FRAMES + f * GROUP, 16), GROUP), :] for t in range(tiles)]
        grad[f] = jnp.concatenate(rows, 1).astype(BF16)

    loop(LOCAL, frame, 4)
    sums_out[...] = sums[...]


def shards(tokens, cotangent, norm_gain, query_weight, key_weight, value_weight, out_weight):
    total_rows = FRAMES * lax.axis_size("tm") * lax.axis_size("space")
    anywhere = pl.BlockSpec(memory_space=pl.ANY)
    vmem = pl.BlockSpec(memory_space=pltpu.VMEM)
    dma = pltpu.SemaphoreType.DMA
    rows = pltpu.VMEM((FRAMES, D), BF16)
    block = pltpu.VMEM((GROUP, LOCAL, D), BF16)
    weight = pltpu.VMEM((D, D), BF16)
    back, sums = pl.pallas_call(
        functools.partial(kernel, 1.0 / math.sqrt(total_rows)),
        out_shape=(
            jax.ShapeDtypeStruct((GROUP, LOCAL, D), BF16),
            jax.ShapeDtypeStruct((16, D), F32),
        ),
        in_specs=[anywhere, anywhere, vmem] + [anywhere] * 4,
        out_specs=(anywhere, vmem),
        scratch_shapes=[
            pltpu.VMEM((2, LOCAL, GROUP, D), BF16),
            pltpu.VMEM((TILES * FRAMES, 128), F32),
            block, block, block, block, block,
            pltpu.VMEM((2, GROUP, LOCAL, 128), F32),
            weight, weight, weight, weight,
            rows, rows, rows, rows, rows, rows, rows, rows, rows, rows,
            pltpu.VMEM((PAIRS, FRAMES, 2 * FRAMES), F32),
            pltpu.VMEM((PAIRS, FRAMES, 2 * FRAMES), BF16),
            pltpu.VMEM((PAIRS, FRAMES, 2 * EARLY), BF16),
            pltpu.VMEM((4, 4, 2, 4, 2, 16, D), BF16),
            pltpu.VMEM((4, 4, 2, 4, 16, D), BF16),
            pltpu.VMEM((4, 2, 2, 3, 2, 16, D), BF16),
            pltpu.VMEM((4, 2, 2, 2, 16, D), BF16),
            pltpu.VMEM((4, 2, 4, 16, D), BF16),
            pltpu.VMEM((4, 2, 3, 16, D), BF16),
            pltpu.VMEM((8, 16, D), BF16),
            pltpu.VMEM((8, 16, D), BF16),
            dma((6,)), dma((2, 16)), dma((2, 16)), dma((16,)), dma((16,)),
            dma((4, 2)), dma((4, 2)),
            dma((4, 2, 2, 3)), dma((4, 2, 2, 3)),
            dma((4, 2, 3)), dma((4, 2, 3)),
            dma((8,)), dma((8,)),
        ],
        compiler_params=pltpu.CompilerParams(
            collective_id=0, has_side_effects=True, vmem_limit_bytes=63 * 1024 * 1024
        ),
    )(tokens, cotangent, norm_gain.reshape(1, D), query_weight, key_weight, value_weight, out_weight)
    steps = 2
    wide = D // steps
    grad, sums = pl.pallas_call(
        frames_first,
        grid=(steps,),
        out_shape=(
            jax.ShapeDtypeStruct((LOCAL, GROUP, D), BF16),
            jax.ShapeDtypeStruct((16, D), F32),
        ),
        in_specs=[
            pl.BlockSpec((GROUP, LOCAL, wide), lambda n: (0, 0, n)),
            pl.BlockSpec((16, wide), lambda n: (0, n)),
        ],
        out_specs=(
            pl.BlockSpec((LOCAL, GROUP, wide), lambda n: (0, 0, n)),
            pl.BlockSpec((16, wide), lambda n: (0, n)),
        ),
        scratch_shapes=[pltpu.VMEM((wide // 128 * FRAMES, 128), F32)],
        compiler_params=pltpu.CompilerParams(vmem_limit_bytes=62 * 1024 * 1024),
    )(back, sums)
    return grad, sums.T


def solution(mesh):
    in_specs = (P("tm", "space", None), P("tm", "space", None), P(), P(), P(), P(), P())
    out_specs = (P("tm", "space", None), P(None, ("tm", "space")))
    return jax.shard_map(shards, mesh=mesh, in_specs=in_specs, out_specs=out_specs, check_vma=False)
```

```python
import functools
import math

import jax
import jax.numpy as jnp
from jax import lax
from jax.experimental import pallas as pl
from jax.experimental.pallas import tpu as pltpu
from jax.sharding import PartitionSpec as P

H = 16
D = 1024
HEAD = D // H
PAIRS = H // 2
LOCAL = 24
GROUP = 16
FRAMES = LOCAL * GROUP
TILES = D // 128
EPS = 1e-06
EARLY = 256
LATE = FRAMES - EARLY
OFFSETS = (
    (0, 0), (0, 1), (0, 2), (0, 3),
    (1, 0), (3, 0), (1, 1), (3, 1), (1, 2), (3, 2), (1, 3),
    (3, 3), (2, 0), (2, 1), (2, 2), (2, 3),
)
SEND_ORDER = tuple(range(4, 11)) + (1, 2, 3) + tuple(range(11, 16))
X_FIRST = ((False, True), (True, True), (True, False), (True, False))
MESH = pl.DeviceIdType.MESH
BF16 = jnp.bfloat16
F32 = jnp.float32


def nn(left, right):
    return lax.dot_general(left, right, (((1,), (0,)), ((), ())), preferred_element_type=F32)


def nt(left, right):
    return lax.dot_general(left, right, (((1,), (1,)), ((), ())), preferred_element_type=F32)


def tn(left, right):
    return lax.dot_general(left, right, (((0,), (0,)), ((), ())), preferred_element_type=F32)


def place():
    tm = lax.axis_index("tm")
    space = lax.axis_index("space")
    return (tm // 4) * 2 + space // 8, tm % 4, (space // 2) % 4, space % 2


def device(z, y, x, core):
    return ((z // 2) * 4 + y, ((z % 2) * 4 + x) * 2 + core)


def remote(src, dst, send, recv, to):
    return pltpu.make_async_remote_copy(
        src_ref=src, dst_ref=dst, send_sem=send, recv_sem=recv, device_id=to, device_id_type=MESH
    )


def loop(count, body, unroll=1):
    def step(i, carry):
        body(i)
        return carry

    lax.fori_loop(0, count, step, 0, unroll=unroll)


def kernel(
    scale,
    tokens, cotangent, gain, wq_hbm, wk_hbm, wv_hbm, wo_hbm,
    back_in, sums_ref,
    raw, turn, x_out, dy_out, x_in, dy_in, back_out, stats,
    wq, wk, wv, wo,
    normed, query, key, value, mixed, dy, grad_mixed, grad_query, grad_key, grad_value,
    weights, lows, low_early,
    part, pair, first_in, first_fwd, mid, second_in, last, last_in,
    load_sem, in_send, in_recv, back_send, back_recv,
    core_send, core_recv, first_send, first_recv, second_send, second_recv, z_send, z_recv,
):
    z, y, x, core = place()
    z_hi, z_lo = z // 2, z % 2
    me = z_hi * 4 + y
    partner = device(z, y, x, 1 - core)
    x_next, x_prev = device(z, y, (x + 1) % 4, core), device(z, y, (x + 3) % 4, core)
    y_next, y_prev = device(z, (y + 1) % 4, x, core), device(z, (y + 3) % 4, x, core)

    def member(i, sign):
        a, b = OFFSETS[i]
        to_z, to_y = (z_hi + 4 + sign * a) % 4, (y + 4 + sign * b) % 4
        return to_z * 4 + to_y, device(to_z * 2 + z_lo, to_y, x, core)

    loads = [
        pltpu.make_async_copy(tokens, raw.at[0], load_sem.at[0]),
        pltpu.make_async_copy(cotangent, raw.at[1], load_sem.at[1]),
        pltpu.make_async_copy(wq_hbm, wq, load_sem.at[2]),
        pltpu.make_async_copy(wk_hbm, wk, load_sem.at[3]),
        pltpu.make_async_copy(wv_hbm, wv, load_sem.at[4]),
        pltpu.make_async_copy(wo_hbm, wo, load_sem.at[5]),
    ]
    loads[0].start()

    barrier = pltpu.get_barrier_semaphore()
    peers = [member(i, 1)[1] for i in range(1, GROUP)]
    peers += [partner, x_next, x_prev, device(z, y, (x + 2) % 4, core)] + [device((z + o) % 8, y, x, core) for o in (1, 3, 5, 7)]
    for peer in peers:
        pl.semaphore_signal(barrier, inc=1, device_id=peer, device_id_type=MESH)

    def positions_first(which, target):
        def frame(f):
            rows = raw[which, f].astype(F32)
            for t in range(TILES):
                turn[pl.ds(pl.multiple_of(t * FRAMES + f * GROUP, 16), GROUP), :] = rows[:, t * 128:(t + 1) * 128]

        loop(LOCAL, frame, 4)

        def position(p):
            rows = [turn[pl.ds(t * FRAMES + p, LOCAL, stride=GROUP), :] for t in range(TILES)]
            target[p] = jnp.concatenate(rows, 1).astype(BF16)

        loop(GROUP, position, 4)

    def in_copy(which, i):
        to, peer = member(i, 1)
        source, target = ((x_out, x_in), (dy_out, dy_in))[which]
        return remote(source.at[to], target.at[i], in_send.at[which, i], in_recv.at[which, i], peer)

    loads[0].wait()
    for load in loads[1:]:
        load.start()
    positions_first(0, x_out)
    pl.semaphore_wait(barrier, len(peers))
    for i in SEND_ORDER:
        in_copy(0, i).start()
    x_in[0] = x_out[me]
    loads[1].wait()
    positions_first(1, dy_out)
    for i in SEND_ORDER:
        in_copy(1, i).start()
    dy_in[0] = dy_out[me]

    def normalise(i):
        rows = []
        for j in range(2):
            floated = x_in[2 * i + j].astype(F32)
            mean = jnp.mean(floated, -1, keepdims=True)
            centred = floated - mean
            inv_scale = lax.rsqrt(jnp.mean(centred * centred, -1, keepdims=True) + EPS)
            stats[0, 2 * i + j] = jnp.broadcast_to(mean, (LOCAL, 128))
            stats[1, 2 * i + j] = jnp.broadcast_to(inv_scale, (LOCAL, 128))
            rows.append(centred * inv_scale * gain[...])
        normed[pl.ds(i * 48, 48), :] = jnp.concatenate(rows, 0).astype(BF16)

    def project(start, count):
        def block(n):
            columns = pl.ds(pl.multiple_of(n * 256, 256), 256)
            rows = normed[start:start + count, :]
            query[start:start + count, columns] = (nn(rows, wq[:, columns]) * (1.0 / math.sqrt(HEAD))).astype(BF16)
            key[start:start + count, columns] = nn(rows, wk[:, columns]).astype(BF16)
            value[start:start + count, columns] = nn(rows, wv[:, columns]).astype(BF16)

        loop(4, block, 4)

    for i in range(GROUP // 2):
        for j in range(2):
            if i + j > 0:
                in_copy(0, 2 * i + j).wait_recv()
        if i == 0:
            for load in loads[2:5]:
                load.wait()
        normalise(i)
        if 48 * i < EARLY <= 48 * (i + 1):
            project(0, EARLY)
    project(EARLY, LATE)

    def spread(rows):
        first = lax.broadcasted_iota(jnp.int32, rows.shape, 1) < HEAD
        zero = jnp.zeros_like(rows)
        return jnp.concatenate([jnp.where(first, rows, zero), jnp.where(first, zero, rows)], 0)

    def merge(both):
        count = both.shape[0] // 2
        first = lax.broadcasted_iota(jnp.int32, (count, 128), 1) < HEAD
        return jnp.where(first, both[:count], both[count:])

    def pair_columns(p):
        return pl.ds(pl.multiple_of(p * 128, 128), 128)

    def forward(p):
        columns = pair_columns(p)
        spread_query = spread(query[:, columns])
        keys = key[:, columns]
        values, outs = value[:, columns], []
        for c in range(3):
            part_rows = slice(c * 256, (c + 1) * 256)
            scores = nt(keys, spread_query[part_rows])
            raised = jnp.exp(scores - jnp.max(scores, 0, keepdims=True))
            shares = raised * (1.0 / jnp.sum(raised, 0, keepdims=True))
            weights[p, :, part_rows] = shares
            shares = shares.astype(BF16)
            lows[p, :, part_rows] = shares
            outs.append(tn(shares, values))
        mixed[:, columns] = merge(jnp.concatenate(outs, 0)).astype(BF16)

    loop(PAIRS, forward, 8)

    def gather_dy(i):
        rows = [dy_in[2 * i + j].astype(F32) for j in range(2)]
        dy[pl.ds(i * 48, 48), :] = jnp.concatenate(rows, 0).astype(BF16)

    def project_back(start, count):
        def block(n):
            columns = pl.ds(pl.multiple_of(n * 256, 256), 256)
            grad_mixed[start:start + count, columns] = nt(dy[start:start + count, :], wo[columns, :]).astype(BF16)

        loop(4, block, 4)

    early_slots = -(-EARLY // LOCAL)
    for i in range(1, early_slots):
        in_copy(1, i).wait_recv()
    for i in range(EARLY // 48):
        gather_dy(i)
    dy[EARLY // 48 * 48:EARLY, :] = dy_in[early_slots - 1][:EARLY - LOCAL * (early_slots - 1)]
    loads[5].wait()
    project_back(0, EARLY)

    def backward_early(p):
        columns = pair_columns(p)
        spread_grad = spread(grad_mixed[:EARLY, columns])
        values, keys = value[:, columns], key[:, columns]
        both = []
        for c in range(2):
            at = slice(c * FRAMES, c * FRAMES + EARLY)
            grad_weights = nt(values, spread_grad[c * EARLY:(c + 1) * EARLY])
            shares = weights[p, :, at]
            delta = jnp.sum(shares * grad_weights, 0, keepdims=True)
            scores = shares * (grad_weights - delta)
            scores = scores.astype(BF16)
            low_early[p, :, c * EARLY:(c + 1) * EARLY] = scores
            both.append(tn(scores, keys))
        first = lax.broadcasted_iota(jnp.int32, (EARLY, 128), 1) < HEAD
        grad_query[:EARLY, columns] = (jnp.where(first, both[0], both[1]) * (1.0 / math.sqrt(HEAD))).astype(BF16)

    loop(PAIRS, backward_early, 8)

    for i in range(early_slots, GROUP):
        in_copy(1, i).wait_recv()
    for i in range(EARLY // 48, GROUP // 2):
        gather_dy(i)
    def backward_value(p):
        columns = pair_columns(p)
        grad_value[:, columns] = nn(lows[p], spread(grad_mixed[:, columns])).astype(BF16)

    def backward_late(p):
        columns = pair_columns(p)
        values, keys = value[:, columns], key[:, columns]
        grad_weights = nt(values, spread(grad_mixed[EARLY:, columns]))
        shares = jnp.concatenate([weights[p, :, EARLY:FRAMES], weights[p, :, FRAMES + EARLY:]], 1)
        delta = jnp.sum(shares * grad_weights, 0, keepdims=True)
        scores = (shares * (grad_weights - delta)).astype(BF16)
        grad_query[EARLY:, columns] = (merge(tn(scores, keys)) * (1.0 / math.sqrt(HEAD))).astype(BF16)
        pieces = []
        for c in range(2):
            pieces.append(low_early[p, :, c * EARLY:(c + 1) * EARLY])
            pieces.append(scores[:, c * LATE:(c + 1) * LATE])
        grad_key[:, columns] = nn(jnp.concatenate(pieces, 1), spread(query[:, columns])).astype(BF16)

    lefts = [grad_query, grad_key, grad_value, dy]
    rights = [normed, normed, normed, mixed]

    def core_copy(w, h):
        return remote(
            part.at[w, :, h, :, 1 - core], pair.at[w, :, h], core_send.at[w, h], core_recv.at[w, h], partner
        )

    def product(w, h):
        left = lefts[w]
        for r in (0, 2):
            rows = [left[:, (r + j) * 256 + h * 128:(r + j) * 256 + h * 128 + 128] for j in range(2)]
            total = tn(jnp.concatenate(rows, 1), rights[w][...]).astype(BF16).reshape(2, 4, 2, 16, D)
            for j in range(2):
                part[w, r + j, h] = total[j]
        core_copy(w, h).start()

    def first_axis(w, h):
        return (x, x_next, x_prev) if X_FIRST[w][h] else (y, y_next, y_prev)

    def held(w, h, i, s):
        return pair.at[w, pl.ds(2 * s, 2), h, i] if X_FIRST[w][h] else pair.at[w, i, h, pl.ds(2 * s, 2)]

    def start_unit(w, h):
        core_copy(w, h).wait_recv()

        def add(n):
            r, c = n // 4, n % 4
            pair[w, r, h, c] = (part[w, r, h, c, core].astype(F32) + pair[w, r, h, c].astype(F32)).astype(BF16)

        loop(16, add, 4)
        for k in range(4):
            first_ring(w, h, k).start()

    def ring(axis, source, inbox, forwarded, send, recv, k):
        at, after, before = axis
        to, d, slot = (after, before)[k % 2], k % 2, k // 2
        if slot == 0:
            block = source((at + 2) % 4, d)
        elif slot == 1:
            block = source((at + (1, 3)[d]) % 4, 1 - d)
        else:
            block = forwarded.at[d]
        return remote(block, inbox.at[d, slot], send.at[d, slot], recv.at[d, slot], to)

    def first_ring(w, h, k):
        return ring(
            first_axis(w, h), lambda i, s: held(w, h, i, s), first_in.at[w, h], first_fwd.at[w, h],
            first_send.at[w, h], first_recv.at[w, h], k,
        )

    def second_copy(w, h, o):
        at = (y if X_FIRST[w][h] else x) + o
        to = device(z, at % 4, x, core) if X_FIRST[w][h] else device(z, y, at % 4, core)
        return remote(
            mid.at[w, h, at % 4], second_in.at[w, h, o - 1], second_send.at[w, h, o - 1], second_recv.at[w, h, o - 1], to
        )

    def forward_first(w, h):
        at = first_axis(w, h)[0]
        for d in range(2):
            first_ring(w, h, d).wait_recv()
            own = held(w, h, (at + (1, 3)[d]) % 4, d)[...]
            first_fwd[w, h, d] = (first_in[w, h, d, 0].astype(F32) + own.astype(F32)).astype(BF16)
            first_ring(w, h, 4 + d).start()

    def finish_first(w, h):
        at = first_axis(w, h)[0]
        for k in range(2, 6):
            first_ring(w, h, k).wait_recv()
        for s in range(2):
            mid[w, h, 2 * s:2 * s + 2] = (
                held(w, h, at, s)[...].astype(F32)
                + first_in[w, h, s, 2].astype(F32) + first_in[w, h, 1 - s, 1].astype(F32)
            ).astype(BF16)
        for o in (2, 1, 3):
            second_copy(w, h, o).start()

    def z_copy(w, h):
        to = 2 * w + h
        slot = (to + 8 - z) % 8
        return remote(
            last.at[to], last_in.at[slot], z_send.at[to], z_recv.at[slot], device(to, y, x, core)
        )

    def finish_second(w, h):
        total = mid[w, h, y if X_FIRST[w][h] else x].astype(F32)
        for o in range(1, 4):
            second_copy(w, h, o).wait_recv()
            total = total + second_in[w, h, o - 1].astype(F32)
        last[2 * w + h] = total.astype(BF16)

        @pl.when(z != 2 * w + h)
        def _():
            z_copy(w, h).start()

    def unproject(start, count):
        def block(n):
            columns = pl.ds(pl.multiple_of(n * 256, 256), 256)
            total = nt(grad_query[start:start + count, :], wq[columns, :])
            total = total + nt(grad_key[start:start + count, :], wk[columns, :])
            total = total + nt(grad_value[start:start + count, :], wv[columns, :])
            total = total * gain[:, columns]
            for t in range(2):
                row = pl.multiple_of((2 * n + t) * FRAMES + start, 8)
                turn[pl.ds(row, count), :] = total[:, t * 128:(t + 1) * 128]

        loop(4, block, 4)

    def rows_back(i):
        mean = stats[0, i][:, :1]
        inv_scale = stats[1, i][:, :1]
        standard = (x_in[i].astype(F32) - mean) * inv_scale
        tiles = [turn[pl.ds(t * FRAMES + i * LOCAL, LOCAL), :] for t in range(TILES)]
        grad_standard = jnp.concatenate(tiles, 1)
        grad = dy_in[i].astype(F32) + inv_scale * (
            grad_standard
            - jnp.mean(grad_standard, -1, keepdims=True)
            - standard * jnp.mean(grad_standard * standard, -1, keepdims=True)
        )
        back_out[i] = grad.astype(BF16)

    def back_copy(i):
        _, peer = member(i, -1)
        return remote(back_out.at[i], back_in.at[me], back_send.at[i], back_recv.at[i], peer)

    def send_back(i):
        rows_back(i)
        back_copy(i).start()

    own_copy = pltpu.make_async_copy(back_out.at[0], back_in.at[me], back_send.at[0])

    firsts, evens, odds = ((3, 0), (3, 1), (2, 0), (2, 1)), ((1, 0), (0, 0)), ((1, 1), (0, 1))
    for unit in firsts[:2]:
        product(*unit)
    project_back(EARLY, LATE)
    loop(PAIRS, backward_value, 8)
    for unit in firsts[2:]:
        product(*unit)
    for unit in firsts[:2]:
        start_unit(*unit)
    loop(PAIRS // 2, lambda i: backward_late(2 * i), 4)
    for unit in firsts[2:]:
        start_unit(*unit)
    for unit in evens:
        product(*unit)
    for unit in firsts[:2]:
        forward_first(*unit)
    loop(PAIRS // 2, lambda i: backward_late(2 * i + 1), 4)
    for unit in evens:
        start_unit(*unit)
    for unit in firsts[2:]:
        forward_first(*unit)
    unproject(FRAMES // 2, FRAMES // 2)
    for i in range(GROUP // 2, GROUP):
        send_back(i)
    for unit in odds:
        product(*unit)
    for unit in evens:
        forward_first(*unit)
    unproject(0, FRAMES // 2)
    for unit in odds:
        start_unit(*unit)
    for i in list(range(4, GROUP // 2)) + [1, 2, 3]:
        send_back(i)
    rows_back(0)
    own_copy.start()
    for unit in firsts:
        finish_first(*unit)
    for unit in odds:
        forward_first(*unit)
    for unit in evens:
        finish_first(*unit)
    for unit in firsts:
        finish_second(*unit)
    for unit in odds:
        finish_first(*unit)
    for unit in evens + odds:
        finish_second(*unit)

    total = last[z].astype(F32)
    for o in range(1, 8):
        remote(
            last.at[0], last_in.at[o], z_send.at[0], z_recv.at[o], device((z + o) % 8, y, x, core)
        ).wait_recv()
        total = total + last_in[o].astype(F32)
    sums_ref[...] = total * scale

    own_copy.wait()
    for i in range(1, GROUP):
        back_copy(i).wait_recv()
    for i in range(1, GROUP):
        in_copy(0, i).wait_send()
        in_copy(1, i).wait_send()
        back_copy(i).wait_send()
    for w in range(4):
        for h in range(2):
            core_copy(w, h).wait_send()
            for k in range(6):
                first_ring(w, h, k).wait_send()
            for o in range(1, 4):
                second_copy(w, h, o).wait_send()

            @pl.when(z != 2 * w + h)
            def _():
                z_copy(w, h).wait_send()


def frames_first(back, sums, grad, sums_out, turn):
    tiles = back.shape[2] // 128

    def position(p):
        rows = back[p].astype(F32)
        for t in range(tiles):
            turn[pl.ds(t * FRAMES + p, LOCAL, stride=GROUP), :] = rows[:, t * 128:(t + 1) * 128]

    loop(GROUP, position, 4)

    def frame(f):
        rows = [turn[pl.ds(pl.multiple_of(t * FRAMES + f * GROUP, 16), GROUP), :] for t in range(tiles)]
        grad[f] = jnp.concatenate(rows, 1).astype(BF16)

    loop(LOCAL, frame, 4)
    sums_out[...] = sums[...]


def shards(tokens, cotangent, norm_gain, query_weight, key_weight, value_weight, out_weight):
    total_rows = FRAMES * lax.axis_size("tm") * lax.axis_size("space")
    anywhere = pl.BlockSpec(memory_space=pl.ANY)
    vmem = pl.BlockSpec(memory_space=pltpu.VMEM)
    dma = pltpu.SemaphoreType.DMA
    rows = pltpu.VMEM((FRAMES, D), BF16)
    block = pltpu.VMEM((GROUP, LOCAL, D), BF16)
    weight = pltpu.VMEM((D, D), BF16)
    back, sums = pl.pallas_call(
        functools.partial(kernel, 1.0 / math.sqrt(total_rows)),
        out_shape=(
            jax.ShapeDtypeStruct((GROUP, LOCAL, D), BF16),
            jax.ShapeDtypeStruct((16, D), F32),
        ),
        in_specs=[anywhere, anywhere, vmem] + [anywhere] * 4,
        out_specs=(anywhere, vmem),
        scratch_shapes=[
            pltpu.VMEM((2, LOCAL, GROUP, D), BF16),
            pltpu.VMEM((TILES * FRAMES, 128), F32),
            block, block, block, block, block,
            pltpu.VMEM((2, GROUP, LOCAL, 128), F32),
            weight, weight, weight, weight,
            rows, rows, rows, rows, rows, rows, rows, rows, rows, rows,
            pltpu.VMEM((PAIRS, FRAMES, 2 * FRAMES), F32),
            pltpu.VMEM((PAIRS, FRAMES, 2 * FRAMES), BF16),
            pltpu.VMEM((PAIRS, FRAMES, 2 * EARLY), BF16),
            pltpu.VMEM((4, 4, 2, 4, 2, 16, D), BF16),
            pltpu.VMEM((4, 4, 2, 4, 16, D), BF16),
            pltpu.VMEM((4, 2, 2, 3, 2, 16, D), BF16),
            pltpu.VMEM((4, 2, 2, 2, 16, D), BF16),
            pltpu.VMEM((4, 2, 4, 16, D), BF16),
            pltpu.VMEM((4, 2, 3, 16, D), BF16),
            pltpu.VMEM((8, 16, D), BF16),
            pltpu.VMEM((8, 16, D), BF16),
            dma((6,)), dma((2, 16)), dma((2, 16)), dma((16,)), dma((16,)),
            dma((4, 2)), dma((4, 2)),
            dma((4, 2, 2, 3)), dma((4, 2, 2, 3)),
            dma((4, 2, 3)), dma((4, 2, 3)),
            dma((8,)), dma((8,)),
        ],
        compiler_params=pltpu.CompilerParams(
            collective_id=0, has_side_effects=True, vmem_limit_bytes=63 * 1024 * 1024
        ),
    )(tokens, cotangent, norm_gain.reshape(1, D), query_weight, key_weight, value_weight, out_weight)
    steps = 2
    wide = D // steps
    grad, sums = pl.pallas_call(
        frames_first,
        grid=(steps,),
        out_shape=(
            jax.ShapeDtypeStruct((LOCAL, GROUP, D), BF16),
            jax.ShapeDtypeStruct((16, D), F32),
        ),
        in_specs=[
            pl.BlockSpec((GROUP, LOCAL, wide), lambda n: (0, 0, n)),
            pl.BlockSpec((16, wide), lambda n: (0, n)),
        ],
        out_specs=(
            pl.BlockSpec((LOCAL, GROUP, wide), lambda n: (0, 0, n)),
            pl.BlockSpec((16, wide), lambda n: (0, n)),
        ),
        scratch_shapes=[pltpu.VMEM((wide // 128 * FRAMES, 128), F32)],
        compiler_params=pltpu.CompilerParams(vmem_limit_bytes=62 * 1024 * 1024),
    )(back, sums)
    return grad, sums.T


def solution(mesh):
    in_specs = (P("tm", "space", None), P("tm", "space", None), P(), P(), P(), P(), P())
    out_specs = (P("tm", "space", None), P(None, ("tm", "space")))
    return jax.shard_map(shards, mesh=mesh, in_specs=in_specs, out_specs=out_specs, check_vma=False)
```

```python
import functools
import math

import jax
import jax.numpy as jnp
from jax import lax
from jax.experimental import pallas as pl
from jax.experimental.pallas import tpu as pltpu
from jax.sharding import PartitionSpec as P

H = 16
D = 1024
HEAD = D // H
PAIRS = H // 2
LOCAL = 24
GROUP = 16
FRAMES = LOCAL * GROUP
TILES = D // 128
EPS = 1e-06
EARLY = 256
LATE = FRAMES - EARLY
OFFSETS = (
    (0, 0), (0, 1), (0, 2), (0, 3),
    (1, 0), (3, 0), (1, 1), (3, 1), (1, 2), (3, 2), (1, 3),
    (3, 3), (2, 0), (2, 1), (2, 2), (2, 3),
)
SEND_ORDER = tuple(range(4, 11)) + (1, 2, 3) + tuple(range(11, 16))
X_FIRST = ((False, True), (True, True), (True, False), (True, False))
MESH = pl.DeviceIdType.MESH
BF16 = jnp.bfloat16
F32 = jnp.float32


def nn(left, right):
    return lax.dot_general(left, right, (((1,), (0,)), ((), ())), preferred_element_type=F32)


def nt(left, right):
    return lax.dot_general(left, right, (((1,), (1,)), ((), ())), preferred_element_type=F32)


def tn(left, right):
    return lax.dot_general(left, right, (((0,), (0,)), ((), ())), preferred_element_type=F32)


def place():
    tm = lax.axis_index("tm")
    space = lax.axis_index("space")
    return (tm // 4) * 2 + space // 8, tm % 4, (space // 2) % 4, space % 2


def device(z, y, x, core):
    return ((z // 2) * 4 + y, ((z % 2) * 4 + x) * 2 + core)


def remote(src, dst, send, recv, to):
    return pltpu.make_async_remote_copy(
        src_ref=src, dst_ref=dst, send_sem=send, recv_sem=recv, device_id=to, device_id_type=MESH
    )


def loop(count, body, unroll=1):
    def step(i, carry):
        body(i)
        return carry

    lax.fori_loop(0, count, step, 0, unroll=unroll)


def kernel(
    scale,
    tokens, cotangent, gain, wq_hbm, wk_hbm, wv_hbm, wo_hbm,
    grad_ref, sums_ref,
    raw, turn, x_out, dy_out, x_in, dy_in, back_out, back_in, result, stats,
    wq, wk, wv, wo,
    normed, query, key, value, mixed, dy, grad_mixed, grad_query, grad_key, grad_value,
    weights, lows, low_early,
    part, pair, first_in, first_fwd, mid, second_in, last, last_in,
    load_sem, in_send, in_recv, back_send, back_recv,
    core_send, core_recv, first_send, first_recv, second_send, second_recv, z_send, z_recv,
):
    z, y, x, core = place()
    z_hi, z_lo = z // 2, z % 2
    me = z_hi * 4 + y
    partner = device(z, y, x, 1 - core)
    x_next, x_prev = device(z, y, (x + 1) % 4, core), device(z, y, (x + 3) % 4, core)
    y_next, y_prev = device(z, (y + 1) % 4, x, core), device(z, (y + 3) % 4, x, core)

    def member(i, sign):
        a, b = OFFSETS[i]
        to_z, to_y = (z_hi + 4 + sign * a) % 4, (y + 4 + sign * b) % 4
        return to_z * 4 + to_y, device(to_z * 2 + z_lo, to_y, x, core)

    loads = [
        pltpu.make_async_copy(tokens, raw.at[0], load_sem.at[0]),
        pltpu.make_async_copy(cotangent, raw.at[1], load_sem.at[1]),
        pltpu.make_async_copy(wq_hbm, wq, load_sem.at[2]),
        pltpu.make_async_copy(wk_hbm, wk, load_sem.at[3]),
        pltpu.make_async_copy(wv_hbm, wv, load_sem.at[4]),
        pltpu.make_async_copy(wo_hbm, wo, load_sem.at[5]),
    ]
    loads[0].start()

    barrier = pltpu.get_barrier_semaphore()
    peers = [member(i, 1)[1] for i in range(1, GROUP)]
    peers += [partner, x_next, x_prev, device(z, y, (x + 2) % 4, core)] + [device((z + o) % 8, y, x, core) for o in (1, 3, 5, 7)]
    for peer in peers:
        pl.semaphore_signal(barrier, inc=1, device_id=peer, device_id_type=MESH)

    def positions_first(which, target):
        def frame(f):
            rows = raw[which, f].astype(F32)
            for t in range(TILES):
                turn[pl.ds(pl.multiple_of(t * FRAMES + f * GROUP, 16), GROUP), :] = rows[:, t * 128:(t + 1) * 128]

        loop(LOCAL, frame, 4)

        def position(p):
            rows = [turn[pl.ds(t * FRAMES + p, LOCAL, stride=GROUP), :] for t in range(TILES)]
            target[p] = jnp.concatenate(rows, 1).astype(BF16)

        loop(GROUP, position, 4)

    def in_copy(which, i):
        to, peer = member(i, 1)
        source, target = ((x_out, x_in), (dy_out, dy_in))[which]
        return remote(source.at[to], target.at[i], in_send.at[which, i], in_recv.at[which, i], peer)

    loads[0].wait()
    for load in loads[1:]:
        load.start()
    positions_first(0, x_out)
    pl.semaphore_wait(barrier, len(peers))
    for i in SEND_ORDER:
        in_copy(0, i).start()
    x_in[0] = x_out[me]
    loads[1].wait()
    positions_first(1, dy_out)
    for i in SEND_ORDER:
        in_copy(1, i).start()
    dy_in[0] = dy_out[me]

    def normalise(i):
        rows = []
        for j in range(2):
            floated = x_in[2 * i + j].astype(F32)
            mean = jnp.mean(floated, -1, keepdims=True)
            centred = floated - mean
            inv_scale = lax.rsqrt(jnp.mean(centred * centred, -1, keepdims=True) + EPS)
            stats[0, 2 * i + j] = jnp.broadcast_to(mean, (LOCAL, 128))
            stats[1, 2 * i + j] = jnp.broadcast_to(inv_scale, (LOCAL, 128))
            rows.append(centred * inv_scale * gain[...])
        normed[pl.ds(i * 48, 48), :] = jnp.concatenate(rows, 0).astype(BF16)

    def project(start, count):
        def block(n):
            columns = pl.ds(pl.multiple_of(n * 256, 256), 256)
            rows = normed[start:start + count, :]
            query[start:start + count, columns] = (nn(rows, wq[:, columns]) * (1.0 / math.sqrt(HEAD))).astype(BF16)
            key[start:start + count, columns] = nn(rows, wk[:, columns]).astype(BF16)
            value[start:start + count, columns] = nn(rows, wv[:, columns]).astype(BF16)

        loop(4, block, 4)

    for i in range(GROUP // 2):
        for j in range(2):
            if i + j > 0:
                in_copy(0, 2 * i + j).wait_recv()
        if i == 0:
            for load in loads[2:5]:
                load.wait()
        normalise(i)
        if 48 * i < EARLY <= 48 * (i + 1):
            project(0, EARLY)
    project(EARLY, LATE)

    def spread(rows):
        first = lax.broadcasted_iota(jnp.int32, rows.shape, 1) < HEAD
        zero = jnp.zeros_like(rows)
        return jnp.concatenate([jnp.where(first, rows, zero), jnp.where(first, zero, rows)], 0)

    def merge(both):
        count = both.shape[0] // 2
        first = lax.broadcasted_iota(jnp.int32, (count, 128), 1) < HEAD
        return jnp.where(first, both[:count], both[count:])

    def pair_columns(p):
        return pl.ds(pl.multiple_of(p * 128, 128), 128)

    def forward(p):
        columns = pair_columns(p)
        spread_query = spread(query[:, columns])
        keys = key[:, columns]
        values, outs = value[:, columns], []
        for c in range(3):
            part_rows = slice(c * 256, (c + 1) * 256)
            scores = nt(keys, spread_query[part_rows])
            raised = jnp.exp(scores - jnp.max(scores, 0, keepdims=True))
            shares = raised * (1.0 / jnp.sum(raised, 0, keepdims=True))
            weights[p, :, part_rows] = shares
            shares = shares.astype(BF16)
            lows[p, :, part_rows] = shares
            outs.append(tn(shares, values))
        mixed[:, columns] = merge(jnp.concatenate(outs, 0)).astype(BF16)

    loop(PAIRS, forward, 8)

    def gather_dy(i):
        rows = [dy_in[2 * i + j].astype(F32) for j in range(2)]
        dy[pl.ds(i * 48, 48), :] = jnp.concatenate(rows, 0).astype(BF16)

    def project_back(start, count):
        def block(n):
            columns = pl.ds(pl.multiple_of(n * 256, 256), 256)
            grad_mixed[start:start + count, columns] = nt(dy[start:start + count, :], wo[columns, :]).astype(BF16)

        loop(4, block, 4)

    early_slots = -(-EARLY // LOCAL)
    for i in range(1, early_slots):
        in_copy(1, i).wait_recv()
    for i in range(EARLY // 48):
        gather_dy(i)
    dy[EARLY // 48 * 48:EARLY, :] = dy_in[early_slots - 1][:EARLY - LOCAL * (early_slots - 1)]
    loads[5].wait()
    project_back(0, EARLY)

    def backward_early(p):
        columns = pair_columns(p)
        spread_grad = spread(grad_mixed[:EARLY, columns])
        values, keys = value[:, columns], key[:, columns]
        both = []
        for c in range(2):
            at = slice(c * FRAMES, c * FRAMES + EARLY)
            grad_weights = nt(values, spread_grad[c * EARLY:(c + 1) * EARLY])
            shares = weights[p, :, at]
            delta = jnp.sum(shares * grad_weights, 0, keepdims=True)
            scores = shares * (grad_weights - delta)
            scores = scores.astype(BF16)
            low_early[p, :, c * EARLY:(c + 1) * EARLY] = scores
            both.append(tn(scores, keys))
        first = lax.broadcasted_iota(jnp.int32, (EARLY, 128), 1) < HEAD
        grad_query[:EARLY, columns] = (jnp.where(first, both[0], both[1]) * (1.0 / math.sqrt(HEAD))).astype(BF16)

    loop(PAIRS, backward_early, 8)

    for i in range(early_slots, GROUP):
        in_copy(1, i).wait_recv()
    for i in range(EARLY // 48, GROUP // 2):
        gather_dy(i)
    def backward_value(p):
        columns = pair_columns(p)
        grad_value[:, columns] = nn(lows[p], spread(grad_mixed[:, columns])).astype(BF16)

    def backward_late(p):
        columns = pair_columns(p)
        values, keys = value[:, columns], key[:, columns]
        grad_weights = nt(values, spread(grad_mixed[EARLY:, columns]))
        shares = jnp.concatenate([weights[p, :, EARLY:FRAMES], weights[p, :, FRAMES + EARLY:]], 1)
        delta = jnp.sum(shares * grad_weights, 0, keepdims=True)
        scores = (shares * (grad_weights - delta)).astype(BF16)
        grad_query[EARLY:, columns] = (merge(tn(scores, keys)) * (1.0 / math.sqrt(HEAD))).astype(BF16)
        pieces = []
        for c in range(2):
            pieces.append(low_early[p, :, c * EARLY:(c + 1) * EARLY])
            pieces.append(scores[:, c * LATE:(c + 1) * LATE])
        grad_key[:, columns] = nn(jnp.concatenate(pieces, 1), spread(query[:, columns])).astype(BF16)

    lefts = [grad_query, grad_key, grad_value, dy]
    rights = [normed, normed, normed, mixed]

    def core_copy(w, h, r):
        rows = pl.ds(r, 2)
        return remote(
            part.at[w, rows, h, :, 1 - core], pair.at[w, rows, h],
            core_send.at[w, h, r // 2], core_recv.at[w, h, r // 2], partner,
        )

    def product(w, h):
        left = lefts[w]
        for r in (0, 2):
            rows = [left[:, (r + j) * 256 + h * 128:(r + j) * 256 + h * 128 + 128] for j in range(2)]
            total = tn(jnp.concatenate(rows, 1), rights[w][...]).astype(BF16).reshape(2, 4, 2, 16, D)
            for j in range(2):
                part[w, r + j, h] = total[j]
            core_copy(w, h, r).start()

    def first_axis(w, h):
        return (x, x_next, x_prev) if X_FIRST[w][h] else (y, y_next, y_prev)

    def held(w, h, i, s):
        return pair.at[w, pl.ds(2 * s, 2), h, i] if X_FIRST[w][h] else pair.at[w, i, h, pl.ds(2 * s, 2)]

    def start_unit(w, h):
        for half in (0, 2):
            core_copy(w, h, half).wait_recv()

            def add(n):
                r, c = half + n // 4, n % 4
                pair[w, r, h, c] = (part[w, r, h, c, core].astype(F32) + pair[w, r, h, c].astype(F32)).astype(BF16)

            loop(8, add, 4)
        for k in range(4):
            first_ring(w, h, k).start()

    def ring(axis, source, inbox, forwarded, send, recv, k):
        at, after, before = axis
        to, d, slot = (after, before)[k % 2], k % 2, k // 2
        if slot == 0:
            block = source((at + 2) % 4, d)
        elif slot == 1:
            block = source((at + (1, 3)[d]) % 4, 1 - d)
        else:
            block = forwarded.at[d]
        return remote(block, inbox.at[d, slot], send.at[d, slot], recv.at[d, slot], to)

    def first_ring(w, h, k):
        return ring(
            first_axis(w, h), lambda i, s: held(w, h, i, s), first_in.at[w, h], first_fwd.at[w, h],
            first_send.at[w, h], first_recv.at[w, h], k,
        )

    def second_copy(w, h, o):
        at = (y if X_FIRST[w][h] else x) + o
        to = device(z, at % 4, x, core) if X_FIRST[w][h] else device(z, y, at % 4, core)
        return remote(
            mid.at[w, h, at % 4], second_in.at[w, h, o - 1], second_send.at[w, h, o - 1], second_recv.at[w, h, o - 1], to
        )

    def forward_first(w, h):
        at = first_axis(w, h)[0]
        for d in range(2):
            first_ring(w, h, d).wait_recv()
            own = held(w, h, (at + (1, 3)[d]) % 4, d)[...]
            first_fwd[w, h, d] = (first_in[w, h, d, 0].astype(F32) + own.astype(F32)).astype(BF16)
            first_ring(w, h, 4 + d).start()

    def finish_first(w, h):
        at = first_axis(w, h)[0]
        for k in range(2, 6):
            first_ring(w, h, k).wait_recv()
        for s in range(2):
            mid[w, h, 2 * s:2 * s + 2] = (
                held(w, h, at, s)[...].astype(F32)
                + first_in[w, h, s, 2].astype(F32) + first_in[w, h, 1 - s, 1].astype(F32)
            ).astype(BF16)
        for o in (2, 1, 3):
            second_copy(w, h, o).start()

    def z_copy(w, h):
        to = 2 * w + h
        slot = (to + 8 - z) % 8
        return remote(
            last.at[to], last_in.at[slot], z_send.at[to], z_recv.at[slot], device(to, y, x, core)
        )

    def finish_second(w, h):
        total = mid[w, h, y if X_FIRST[w][h] else x].astype(F32)
        for o in range(1, 4):
            second_copy(w, h, o).wait_recv()
            total = total + second_in[w, h, o - 1].astype(F32)
        last[2 * w + h] = total.astype(BF16)

        @pl.when(z != 2 * w + h)
        def _():
            z_copy(w, h).start()

    def unproject(start, count):
        def block(n):
            columns = pl.ds(pl.multiple_of(n * 256, 256), 256)
            total = nt(grad_query[start:start + count, :], wq[columns, :])
            total = total + nt(grad_key[start:start + count, :], wk[columns, :])
            total = total + nt(grad_value[start:start + count, :], wv[columns, :])
            total = total * gain[:, columns]
            for t in range(2):
                row = pl.multiple_of((2 * n + t) * FRAMES + start, 8)
                turn[pl.ds(row, count), :] = total[:, t * 128:(t + 1) * 128]

        loop(4, block, 4)

    def rows_back(i):
        mean = stats[0, i][:, :1]
        inv_scale = stats[1, i][:, :1]
        standard = (x_in[i].astype(F32) - mean) * inv_scale
        tiles = [turn[pl.ds(t * FRAMES + i * LOCAL, LOCAL), :] for t in range(TILES)]
        grad_standard = jnp.concatenate(tiles, 1)
        grad = dy_in[i].astype(F32) + inv_scale * (
            grad_standard
            - jnp.mean(grad_standard, -1, keepdims=True)
            - standard * jnp.mean(grad_standard * standard, -1, keepdims=True)
        )
        back_out[i] = grad.astype(BF16)

    def back_copy(i):
        _, peer = member(i, -1)
        return remote(back_out.at[i], back_in.at[me], back_send.at[i], back_recv.at[i], peer)

    def send_back(i):
        rows_back(i)
        back_copy(i).start()

    firsts, evens, odds = ((3, 0), (3, 1), (2, 0), (2, 1)), ((1, 0), (0, 0)), ((1, 1), (0, 1))
    for unit in firsts[:2]:
        product(*unit)
    project_back(EARLY, LATE)
    loop(PAIRS, backward_value, 8)
    for unit in firsts[2:]:
        product(*unit)
    for unit in firsts[:2]:
        start_unit(*unit)
    loop(PAIRS // 2, lambda i: backward_late(2 * i), 4)
    for unit in firsts[2:]:
        start_unit(*unit)
    for unit in evens:
        product(*unit)
    for unit in firsts[:2]:
        forward_first(*unit)
    loop(PAIRS // 2, lambda i: backward_late(2 * i + 1), 4)
    for unit in evens:
        start_unit(*unit)
    for unit in odds:
        product(*unit)
    for unit in firsts[2:]:
        forward_first(*unit)
    unproject(FRAMES // 2, FRAMES // 2)
    for unit in odds:
        start_unit(*unit)
    for i in range(GROUP // 2, GROUP):
        send_back(i)
    for unit in evens:
        forward_first(*unit)
    for unit in firsts[:2]:
        finish_first(*unit)
    unproject(0, FRAMES // 2)
    for i in list(range(4, GROUP // 2)) + [1, 2, 3]:
        send_back(i)
    rows_back(0)
    for unit in odds:
        forward_first(*unit)
    for unit in firsts[2:] + evens:
        finish_first(*unit)
    for unit in firsts[:2]:
        finish_second(*unit)
    for unit in odds:
        finish_first(*unit)
    for unit in firsts[2:] + evens + odds:
        finish_second(*unit)

    back_in[me] = back_out[0]
    for i in range(1, GROUP):
        back_copy(i).wait_recv()

    def position_out(p):
        rows = back_in[p].astype(F32)
        for t in range(TILES):
            turn[pl.ds(t * FRAMES + p, LOCAL, stride=GROUP), :] = rows[:, t * 128:(t + 1) * 128]

    loop(GROUP, position_out, 4)

    def frame_out(f):
        rows = [turn[pl.ds(pl.multiple_of(t * FRAMES + f * GROUP, 16), GROUP), :] for t in range(TILES)]
        result[f] = jnp.concatenate(rows, 1).astype(BF16)

    loop(LOCAL, frame_out, 4)
    store = pltpu.make_async_copy(result, grad_ref, load_sem.at[0])
    store.start()

    total = last[z].astype(F32)
    for o in range(1, 8):
        remote(
            last.at[0], last_in.at[o], z_send.at[0], z_recv.at[o], device((z + o) % 8, y, x, core)
        ).wait_recv()
        total = total + last_in[o].astype(F32)
    sums_ref[...] = total * scale
    store.wait()

    for i in range(1, GROUP):
        in_copy(0, i).wait_send()
        in_copy(1, i).wait_send()
        back_copy(i).wait_send()
    for w in range(4):
        for h in range(2):
            core_copy(w, h, 0).wait_send()
            core_copy(w, h, 2).wait_send()
            for k in range(6):
                first_ring(w, h, k).wait_send()
            for o in range(1, 4):
                second_copy(w, h, o).wait_send()

            @pl.when(z != 2 * w + h)
            def _():
                z_copy(w, h).wait_send()


def hand_over(grad, sums, grad_out, sums_out, held, held_sums, sem):
    steps = [(grad.at[pl.ds(6 * i, 6)], held.at[pl.ds(6 * i, 6)], grad_out.at[pl.ds(6 * i, 6)]) for i in range(4)]
    steps.append((sums, held_sums, sums_out))
    inward = [pltpu.make_async_copy(step[0], step[1], sem.at[0, i]) for i, step in enumerate(steps)]
    outward = [pltpu.make_async_copy(step[1], step[2], sem.at[1, i]) for i, step in enumerate(steps)]
    for copy in inward:
        copy.start()
    for copy, onward in zip(inward, outward):
        copy.wait()
        onward.start()
    for onward in outward:
        onward.wait()


def shards(tokens, cotangent, norm_gain, query_weight, key_weight, value_weight, out_weight):
    total_rows = FRAMES * lax.axis_size("tm") * lax.axis_size("space")
    anywhere = pl.BlockSpec(memory_space=pl.ANY)
    vmem = pl.BlockSpec(memory_space=pltpu.VMEM)
    dma = pltpu.SemaphoreType.DMA
    rows = pltpu.VMEM((FRAMES, D), BF16)
    block = pltpu.VMEM((GROUP, LOCAL, D), BF16)
    weight = pltpu.VMEM((D, D), BF16)
    grad, sums = pl.pallas_call(
        functools.partial(kernel, 1.0 / math.sqrt(total_rows)),
        out_shape=(
            jax.ShapeDtypeStruct((LOCAL, GROUP, D), BF16),
            jax.ShapeDtypeStruct((16, D), F32),
        ),
        in_specs=[anywhere, anywhere, vmem] + [anywhere] * 4,
        out_specs=(anywhere, vmem),
        scratch_shapes=[
            pltpu.VMEM((2, LOCAL, GROUP, D), BF16),
            pltpu.VMEM((TILES * FRAMES, 128), F32),
            block, block, block, block, block, block,
            pltpu.VMEM((LOCAL, GROUP, D), BF16),
            pltpu.VMEM((2, GROUP, LOCAL, 128), F32),
            weight, weight, weight, weight,
            rows, rows, rows, rows, rows, rows, rows, rows, rows, rows,
            pltpu.VMEM((PAIRS, FRAMES, 2 * FRAMES), F32),
            pltpu.VMEM((PAIRS, FRAMES, 2 * FRAMES), BF16),
            pltpu.VMEM((PAIRS, FRAMES, 2 * EARLY), BF16),
            pltpu.VMEM((4, 4, 2, 4, 2, 16, D), BF16),
            pltpu.VMEM((4, 4, 2, 4, 16, D), BF16),
            pltpu.VMEM((4, 2, 2, 3, 2, 16, D), BF16),
            pltpu.VMEM((4, 2, 2, 2, 16, D), BF16),
            pltpu.VMEM((4, 2, 4, 16, D), BF16),
            pltpu.VMEM((4, 2, 3, 16, D), BF16),
            pltpu.VMEM((8, 16, D), BF16),
            pltpu.VMEM((8, 16, D), BF16),
            dma((6,)), dma((2, 16)), dma((2, 16)), dma((16,)), dma((16,)),
            dma((4, 2, 2)), dma((4, 2, 2)),
            dma((4, 2, 2, 3)), dma((4, 2, 2, 3)),
            dma((4, 2, 3)), dma((4, 2, 3)),
            dma((8,)), dma((8,)),
        ],
        compiler_params=pltpu.CompilerParams(
            collective_id=0, has_side_effects=True, vmem_limit_bytes=63 * 1024 * 1024
        ),
    )(tokens, cotangent, norm_gain.reshape(1, D), query_weight, key_weight, value_weight, out_weight)
    grad, sums = pl.pallas_call(
        hand_over,
        out_shape=(
            jax.ShapeDtypeStruct((LOCAL, GROUP, D), BF16),
            jax.ShapeDtypeStruct((16, D), F32),
        ),
        in_specs=[anywhere, anywhere],
        out_specs=(anywhere, anywhere),
        scratch_shapes=[pltpu.VMEM((LOCAL, GROUP, D), BF16), pltpu.VMEM((16, D), F32), dma((2, 5))],
        compiler_params=pltpu.CompilerParams(vmem_limit_bytes=62 * 1024 * 1024),
    )(grad, sums)
    return grad, sums.T


def solution(mesh):
    in_specs = (P("tm", "space", None), P("tm", "space", None), P(), P(), P(), P(), P())
    out_specs = (P("tm", "space", None), P(None, ("tm", "space")))
    return jax.shard_map(shards, mesh=mesh, in_specs=in_specs, out_specs=out_specs, check_vma=False)
```

```python
import functools
import math

import jax
import jax.numpy as jnp
from jax import lax
from jax.experimental import pallas as pl
from jax.experimental.pallas import tpu as pltpu
from jax.sharding import PartitionSpec as P

H = 16
D = 1024
HEAD = D // H
PAIRS = H // 2
LOCAL = 24
GROUP = 16
FRAMES = LOCAL * GROUP
TILES = D // 128
EPS = 1e-06
EARLY = 256
LATE = FRAMES - EARLY
OFFSETS = (
    (0, 0), (0, 1), (0, 2), (0, 3),
    (1, 0), (3, 0), (1, 1), (3, 1), (1, 2), (3, 2), (1, 3),
    (3, 3), (2, 0), (2, 1), (2, 2), (2, 3),
)
SEND_ORDER = tuple(range(4, 11)) + (1, 2, 3) + tuple(range(11, 16))
X_FIRST = ((False, True), (True, True), (True, False), (True, False))
MESH = pl.DeviceIdType.MESH
BF16 = jnp.bfloat16
F32 = jnp.float32


def nn(left, right):
    return lax.dot_general(left, right, (((1,), (0,)), ((), ())), preferred_element_type=F32)


def nt(left, right):
    return lax.dot_general(left, right, (((1,), (1,)), ((), ())), preferred_element_type=F32)


def tn(left, right):
    return lax.dot_general(left, right, (((0,), (0,)), ((), ())), preferred_element_type=F32)


def place():
    tm = lax.axis_index("tm")
    space = lax.axis_index("space")
    return (tm // 4) * 2 + space // 8, tm % 4, (space // 2) % 4, space % 2


def device(z, y, x, core):
    return ((z // 2) * 4 + y, ((z % 2) * 4 + x) * 2 + core)


def remote(src, dst, send, recv, to):
    return pltpu.make_async_remote_copy(
        src_ref=src, dst_ref=dst, send_sem=send, recv_sem=recv, device_id=to, device_id_type=MESH
    )


def loop(count, body, unroll=1):
    def step(i, carry):
        body(i)
        return carry

    lax.fori_loop(0, count, step, 0, unroll=unroll)


def kernel(
    scale,
    tokens, cotangent, gain, wq_hbm, wk_hbm, wv_hbm, wo_hbm,
    grad_ref, sums_ref,
    raw, turn, x_out, dy_out, x_in, dy_in, back_out, back_in, result, stats,
    wq, wk, wv, wo,
    normed, query, key, value, mixed, dy, grad_mixed, grad_query, grad_key, grad_value,
    weights, lows, low_early,
    part, pair, first_in, first_fwd, mid, second_in, last, last_in,
    load_sem, in_send, in_recv, back_send, back_recv,
    core_send, core_recv, first_send, first_recv, second_send, second_recv, z_send, z_recv,
):
    z, y, x, core = place()
    z_hi, z_lo = z // 2, z % 2
    me = z_hi * 4 + y
    partner = device(z, y, x, 1 - core)
    x_next, x_prev = device(z, y, (x + 1) % 4, core), device(z, y, (x + 3) % 4, core)
    y_next, y_prev = device(z, (y + 1) % 4, x, core), device(z, (y + 3) % 4, x, core)

    def member(i, sign):
        a, b = OFFSETS[i]
        to_z, to_y = (z_hi + 4 + sign * a) % 4, (y + 4 + sign * b) % 4
        return to_z * 4 + to_y, device(to_z * 2 + z_lo, to_y, x, core)

    loads = [
        pltpu.make_async_copy(tokens, raw.at[0], load_sem.at[0]),
        pltpu.make_async_copy(cotangent, raw.at[1], load_sem.at[1]),
        pltpu.make_async_copy(wq_hbm, wq, load_sem.at[2]),
        pltpu.make_async_copy(wk_hbm, wk, load_sem.at[3]),
        pltpu.make_async_copy(wv_hbm, wv, load_sem.at[4]),
        pltpu.make_async_copy(wo_hbm, wo, load_sem.at[5]),
    ]
    loads[0].start()

    barrier = pltpu.get_barrier_semaphore()
    peers = [member(i, 1)[1] for i in range(1, GROUP)]
    peers += [partner, x_next, x_prev, device(z, y, (x + 2) % 4, core)] + [device((z + o) % 8, y, x, core) for o in (1, 3, 5, 7)]
    for peer in peers:
        pl.semaphore_signal(barrier, inc=1, device_id=peer, device_id_type=MESH)

    def positions_first(which, target):
        def frame(f):
            rows = raw[which, f].astype(F32)
            for t in range(TILES):
                turn[pl.ds(pl.multiple_of(t * FRAMES + f * GROUP, 16), GROUP), :] = rows[:, t * 128:(t + 1) * 128]

        loop(LOCAL, frame, 4)

        def position(p):
            rows = [turn[pl.ds(t * FRAMES + p, LOCAL, stride=GROUP), :] for t in range(TILES)]
            target[p] = jnp.concatenate(rows, 1).astype(BF16)

        loop(GROUP, position, 4)

    def in_copy(which, i):
        to, peer = member(i, 1)
        source, target = ((x_out, x_in), (dy_out, dy_in))[which]
        return remote(source.at[to], target.at[i], in_send.at[which, i], in_recv.at[which, i], peer)

    loads[0].wait()
    for load in loads[1:]:
        load.start()
    positions_first(0, x_out)
    pl.semaphore_wait(barrier, len(peers))
    for i in SEND_ORDER:
        in_copy(0, i).start()
    x_in[0] = x_out[me]
    loads[1].wait()
    positions_first(1, dy_out)
    for i in SEND_ORDER:
        in_copy(1, i).start()
    dy_in[0] = dy_out[me]

    def normalise(i):
        rows = []
        for j in range(2):
            floated = x_in[2 * i + j].astype(F32)
            mean = jnp.mean(floated, -1, keepdims=True)
            centred = floated - mean
            inv_scale = lax.rsqrt(jnp.mean(centred * centred, -1, keepdims=True) + EPS)
            stats[0, 2 * i + j] = jnp.broadcast_to(mean, (LOCAL, 128))
            stats[1, 2 * i + j] = jnp.broadcast_to(inv_scale, (LOCAL, 128))
            rows.append(centred * inv_scale * gain[...])
        normed[pl.ds(i * 48, 48), :] = jnp.concatenate(rows, 0).astype(BF16)

    def project(start, count):
        def block(n):
            columns = pl.ds(pl.multiple_of(n * 256, 256), 256)
            rows = normed[start:start + count, :]
            query[start:start + count, columns] = (nn(rows, wq[:, columns]) * (1.0 / math.sqrt(HEAD))).astype(BF16)
            key[start:start + count, columns] = nn(rows, wk[:, columns]).astype(BF16)
            value[start:start + count, columns] = nn(rows, wv[:, columns]).astype(BF16)

        loop(4, block, 4)

    for i in range(GROUP // 2):
        for j in range(2):
            if i + j > 0:
                in_copy(0, 2 * i + j).wait_recv()
        if i == 0:
            for load in loads[2:5]:
                load.wait()
        normalise(i)
        if 48 * i < EARLY <= 48 * (i + 1):
            project(0, EARLY)
    project(EARLY, LATE)

    def spread(rows):
        first = lax.broadcasted_iota(jnp.int32, rows.shape, 1) < HEAD
        zero = jnp.zeros_like(rows)
        return jnp.concatenate([jnp.where(first, rows, zero), jnp.where(first, zero, rows)], 0)

    def merge(both):
        count = both.shape[0] // 2
        first = lax.broadcasted_iota(jnp.int32, (count, 128), 1) < HEAD
        return jnp.where(first, both[:count], both[count:])

    def pair_columns(p):
        return pl.ds(pl.multiple_of(p * 128, 128), 128)

    def forward(p):
        columns = pair_columns(p)
        spread_query = spread(query[:, columns])
        keys = key[:, columns]
        values, outs = value[:, columns], []
        for c in range(3):
            part_rows = slice(c * 256, (c + 1) * 256)
            scores = nt(keys, spread_query[part_rows])
            raised = jnp.exp(scores - jnp.max(scores, 0, keepdims=True))
            shares = raised * (1.0 / jnp.sum(raised, 0, keepdims=True))
            weights[p, :, part_rows] = shares
            shares = shares.astype(BF16)
            lows[p, :, part_rows] = shares
            outs.append(tn(shares, values))
        mixed[:, columns] = merge(jnp.concatenate(outs, 0)).astype(BF16)

    loop(PAIRS, forward, 8)

    def gather_dy(i):
        rows = [dy_in[2 * i + j].astype(F32) for j in range(2)]
        dy[pl.ds(i * 48, 48), :] = jnp.concatenate(rows, 0).astype(BF16)

    def project_back(start, count):
        def block(n):
            columns = pl.ds(pl.multiple_of(n * 256, 256), 256)
            grad_mixed[start:start + count, columns] = nt(dy[start:start + count, :], wo[columns, :]).astype(BF16)

        loop(4, block, 4)

    early_slots = -(-EARLY // LOCAL)
    for i in range(1, early_slots):
        in_copy(1, i).wait_recv()
    for i in range(EARLY // 48):
        gather_dy(i)
    dy[EARLY // 48 * 48:EARLY, :] = dy_in[early_slots - 1][:EARLY - LOCAL * (early_slots - 1)]
    loads[5].wait()
    project_back(0, EARLY)

    def backward_early(p):
        columns = pair_columns(p)
        spread_grad = spread(grad_mixed[:EARLY, columns])
        values, keys = value[:, columns], key[:, columns]
        both = []
        for c in range(2):
            at = slice(c * FRAMES, c * FRAMES + EARLY)
            grad_weights = nt(values, spread_grad[c * EARLY:(c + 1) * EARLY])
            shares = weights[p, :, at]
            delta = jnp.sum(shares * grad_weights, 0, keepdims=True)
            scores = shares * (grad_weights - delta)
            scores = scores.astype(BF16)
            low_early[p, :, c * EARLY:(c + 1) * EARLY] = scores
            both.append(tn(scores, keys))
        first = lax.broadcasted_iota(jnp.int32, (EARLY, 128), 1) < HEAD
        grad_query[:EARLY, columns] = (jnp.where(first, both[0], both[1]) * (1.0 / math.sqrt(HEAD))).astype(BF16)

    loop(PAIRS, backward_early, 8)

    for i in range(early_slots, GROUP):
        in_copy(1, i).wait_recv()
    for i in range(EARLY // 48, GROUP // 2):
        gather_dy(i)
    def backward_value(p):
        columns = pair_columns(p)
        grad_value[:, columns] = nn(lows[p], spread(grad_mixed[:, columns])).astype(BF16)

    def backward_late(p):
        columns = pair_columns(p)
        values, keys = value[:, columns], key[:, columns]
        grad_weights = nt(values, spread(grad_mixed[EARLY:, columns]))
        shares = jnp.concatenate([weights[p, :, EARLY:FRAMES], weights[p, :, FRAMES + EARLY:]], 1)
        delta = jnp.sum(shares * grad_weights, 0, keepdims=True)
        scores = (shares * (grad_weights - delta)).astype(BF16)
        grad_query[EARLY:, columns] = (merge(tn(scores, keys)) * (1.0 / math.sqrt(HEAD))).astype(BF16)
        pieces = []
        for c in range(2):
            pieces.append(low_early[p, :, c * EARLY:(c + 1) * EARLY])
            pieces.append(scores[:, c * LATE:(c + 1) * LATE])
        grad_key[:, columns] = nn(jnp.concatenate(pieces, 1), spread(query[:, columns])).astype(BF16)

    lefts = [grad_query, grad_key, grad_value, dy]
    rights = [normed, normed, normed, mixed]

    def core_copy(w, h, r):
        rows = pl.ds(r, 2)
        return remote(
            part.at[w, rows, h, :, 1 - core], pair.at[w, rows, h],
            core_send.at[w, h, r // 2], core_recv.at[w, h, r // 2], partner,
        )

    def product(w, h):
        left = lefts[w]
        for r in (0, 2):
            rows = [left[:, (r + j) * 256 + h * 128:(r + j) * 256 + h * 128 + 128] for j in range(2)]
            total = tn(jnp.concatenate(rows, 1), rights[w][...]).astype(BF16).reshape(2, 4, 2, 16, D)
            for j in range(2):
                part[w, r + j, h] = total[j]
            core_copy(w, h, r).start()

    def first_axis(w, h):
        return (x, x_next, x_prev) if X_FIRST[w][h] else (y, y_next, y_prev)

    def held(w, h, i, s):
        return pair.at[w, pl.ds(2 * s, 2), h, i] if X_FIRST[w][h] else pair.at[w, i, h, pl.ds(2 * s, 2)]

    def start_unit(w, h):
        for half in (0, 2):
            core_copy(w, h, half).wait_recv()

            def add(n):
                r, c = half + n // 4, n % 4
                pair[w, r, h, c] = (part[w, r, h, c, core].astype(F32) + pair[w, r, h, c].astype(F32)).astype(BF16)

            loop(8, add, 4)
        for k in range(4):
            first_ring(w, h, k).start()

    def ring(axis, source, inbox, forwarded, send, recv, k):
        at, after, before = axis
        to, d, slot = (after, before)[k % 2], k % 2, k // 2
        if slot == 0:
            block = source((at + 2) % 4, d)
        elif slot == 1:
            block = source((at + (1, 3)[d]) % 4, 1 - d)
        else:
            block = forwarded.at[d]
        return remote(block, inbox.at[d, slot], send.at[d, slot], recv.at[d, slot], to)

    def first_ring(w, h, k):
        return ring(
            first_axis(w, h), lambda i, s: held(w, h, i, s), first_in.at[w, h], first_fwd.at[w, h],
            first_send.at[w, h], first_recv.at[w, h], k,
        )

    def second_copy(w, h, o):
        at = (y if X_FIRST[w][h] else x) + o
        to = device(z, at % 4, x, core) if X_FIRST[w][h] else device(z, y, at % 4, core)
        return remote(
            mid.at[w, h, at % 4], second_in.at[w, h, o - 1], second_send.at[w, h, o - 1], second_recv.at[w, h, o - 1], to
        )

    def forward_first(w, h):
        at = first_axis(w, h)[0]
        for d in range(2):
            first_ring(w, h, d).wait_recv()
            own = held(w, h, (at + (1, 3)[d]) % 4, d)[...]
            first_fwd[w, h, d] = (first_in[w, h, d, 0].astype(F32) + own.astype(F32)).astype(BF16)
            first_ring(w, h, 4 + d).start()

    def finish_first(w, h):
        at = first_axis(w, h)[0]
        for k in range(2, 6):
            first_ring(w, h, k).wait_recv()
        for s in range(2):
            mid[w, h, 2 * s:2 * s + 2] = (
                held(w, h, at, s)[...].astype(F32)
                + first_in[w, h, s, 2].astype(F32) + first_in[w, h, 1 - s, 1].astype(F32)
            ).astype(BF16)
        for o in (2, 1, 3):
            second_copy(w, h, o).start()

    def z_copy(w, h):
        to = 2 * w + h
        slot = (to + 8 - z) % 8
        return remote(
            last.at[to], last_in.at[slot], z_send.at[to], z_recv.at[slot], device(to, y, x, core)
        )

    def finish_second(w, h):
        total = mid[w, h, y if X_FIRST[w][h] else x].astype(F32)
        for o in range(1, 4):
            second_copy(w, h, o).wait_recv()
            total = total + second_in[w, h, o - 1].astype(F32)
        last[2 * w + h] = total.astype(BF16)

        @pl.when(z != 2 * w + h)
        def _():
            z_copy(w, h).start()

    def unproject(start, count):
        def block(n):
            columns = pl.ds(pl.multiple_of(n * 256, 256), 256)
            total = nt(grad_query[start:start + count, :], wq[columns, :])
            total = total + nt(grad_key[start:start + count, :], wk[columns, :])
            total = total + nt(grad_value[start:start + count, :], wv[columns, :])
            total = total * gain[:, columns]
            for t in range(2):
                row = pl.multiple_of((2 * n + t) * FRAMES + start, 8)
                turn[pl.ds(row, count), :] = total[:, t * 128:(t + 1) * 128]

        loop(4, block, 4)

    def rows_back(i):
        mean = stats[0, i][:, :1]
        inv_scale = stats[1, i][:, :1]
        standard = (x_in[i].astype(F32) - mean) * inv_scale
        tiles = [turn[pl.ds(t * FRAMES + i * LOCAL, LOCAL), :] for t in range(TILES)]
        grad_standard = jnp.concatenate(tiles, 1)
        grad = dy_in[i].astype(F32) + inv_scale * (
            grad_standard
            - jnp.mean(grad_standard, -1, keepdims=True)
            - standard * jnp.mean(grad_standard * standard, -1, keepdims=True)
        )
        back_out[i] = grad.astype(BF16)

    def back_copy(i):
        _, peer = member(i, -1)
        return remote(back_out.at[i], back_in.at[me], back_send.at[i], back_recv.at[i], peer)

    def send_back(i):
        rows_back(i)
        back_copy(i).start()

    firsts, evens, odds = ((3, 0), (3, 1), (2, 0), (2, 1)), ((1, 0), (0, 0)), ((1, 1), (0, 1))
    outs, values = firsts[:2], firsts[2:]
    for unit in outs:
        product(*unit)
    project_back(EARLY, LATE)
    for unit in outs:
        start_unit(*unit)
    loop(PAIRS, backward_value, 8)
    for unit in values:
        product(*unit)
    for unit in outs:
        forward_first(*unit)
    loop(PAIRS // 2, lambda i: backward_late(2 * i), 4)
    for unit in values:
        start_unit(*unit)
    for unit in evens:
        product(*unit)
    for unit in outs:
        finish_first(*unit)
    loop(PAIRS // 2, lambda i: backward_late(2 * i + 1), 4)
    for unit in evens:
        start_unit(*unit)
    for unit in odds:
        product(*unit)
    for unit in values:
        forward_first(*unit)
    unproject(FRAMES // 2, FRAMES // 2)
    for unit in odds:
        start_unit(*unit)
    for i in range(GROUP // 2, GROUP):
        send_back(i)
    for unit in evens:
        forward_first(*unit)
    unproject(0, FRAMES // 2)
    for i in list(range(4, GROUP // 2)) + [1, 2, 3]:
        send_back(i)
    rows_back(0)
    for unit in values:
        finish_first(*unit)
    for unit in outs:
        finish_second(*unit)
    forward_first(*odds[0])
    for unit in evens:
        finish_first(*unit)
    forward_first(*odds[1])
    for unit in values:
        finish_second(*unit)
    finish_first(*odds[0])
    for unit in evens:
        finish_second(*unit)
    finish_first(*odds[1])
    for unit in odds:
        finish_second(*unit)

    back_in[me] = back_out[0]
    for i in range(1, GROUP):
        back_copy(i).wait_recv()

    def position_out(p):
        rows = back_in[p].astype(F32)
        for t in range(TILES):
            turn[pl.ds(t * FRAMES + p, LOCAL, stride=GROUP), :] = rows[:, t * 128:(t + 1) * 128]

    loop(GROUP, position_out, 4)

    def frame_out(f):
        rows = [turn[pl.ds(pl.multiple_of(t * FRAMES + f * GROUP, 16), GROUP), :] for t in range(TILES)]
        result[f] = jnp.concatenate(rows, 1).astype(BF16)

    loop(LOCAL, frame_out, 4)
    store = pltpu.make_async_copy(result, grad_ref, load_sem.at[0])
    store.start()

    total = last[z].astype(F32)
    for o in range(1, 8):
        remote(
            last.at[0], last_in.at[o], z_send.at[0], z_recv.at[o], device((z + o) % 8, y, x, core)
        ).wait_recv()
        total = total + last_in[o].astype(F32)
    sums_ref[...] = total * scale
    store.wait()

    for i in range(1, GROUP):
        in_copy(0, i).wait_send()
        in_copy(1, i).wait_send()
        back_copy(i).wait_send()
    for w in range(4):
        for h in range(2):
            core_copy(w, h, 0).wait_send()
            core_copy(w, h, 2).wait_send()
            for k in range(6):
                first_ring(w, h, k).wait_send()
            for o in range(1, 4):
                second_copy(w, h, o).wait_send()

            @pl.when(z != 2 * w + h)
            def _():
                z_copy(w, h).wait_send()


def hand_over(grad, sums, grad_out, sums_out, held, held_sums, sem):
    steps = [(grad.at[pl.ds(6 * i, 6)], held.at[pl.ds(6 * i, 6)], grad_out.at[pl.ds(6 * i, 6)]) for i in range(4)]
    steps.append((sums, held_sums, sums_out))
    inward = [pltpu.make_async_copy(step[0], step[1], sem.at[0, i]) for i, step in enumerate(steps)]
    outward = [pltpu.make_async_copy(step[1], step[2], sem.at[1, i]) for i, step in enumerate(steps)]
    for copy in inward:
        copy.start()
    for copy, onward in zip(inward, outward):
        copy.wait()
        onward.start()
    for onward in outward:
        onward.wait()


def shards(tokens, cotangent, norm_gain, query_weight, key_weight, value_weight, out_weight):
    total_rows = FRAMES * lax.axis_size("tm") * lax.axis_size("space")
    anywhere = pl.BlockSpec(memory_space=pl.ANY)
    vmem = pl.BlockSpec(memory_space=pltpu.VMEM)
    dma = pltpu.SemaphoreType.DMA
    rows = pltpu.VMEM((FRAMES, D), BF16)
    block = pltpu.VMEM((GROUP, LOCAL, D), BF16)
    weight = pltpu.VMEM((D, D), BF16)
    grad, sums = pl.pallas_call(
        functools.partial(kernel, 1.0 / math.sqrt(total_rows)),
        out_shape=(
            jax.ShapeDtypeStruct((LOCAL, GROUP, D), BF16),
            jax.ShapeDtypeStruct((16, D), F32),
        ),
        in_specs=[anywhere, anywhere, vmem] + [anywhere] * 4,
        out_specs=(anywhere, vmem),
        scratch_shapes=[
            pltpu.VMEM((2, LOCAL, GROUP, D), BF16),
            pltpu.VMEM((TILES * FRAMES, 128), F32),
            block, block, block, block, block, block,
            pltpu.VMEM((LOCAL, GROUP, D), BF16),
            pltpu.VMEM((2, GROUP, LOCAL, 128), F32),
            weight, weight, weight, weight,
            rows, rows, rows, rows, rows, rows, rows, rows, rows, rows,
            pltpu.VMEM((PAIRS, FRAMES, 2 * FRAMES), F32),
            pltpu.VMEM((PAIRS, FRAMES, 2 * FRAMES), BF16),
            pltpu.VMEM((PAIRS, FRAMES, 2 * EARLY), BF16),
            pltpu.VMEM((4, 4, 2, 4, 2, 16, D), BF16),
            pltpu.VMEM((4, 4, 2, 4, 16, D), BF16),
            pltpu.VMEM((4, 2, 2, 3, 2, 16, D), BF16),
            pltpu.VMEM((4, 2, 2, 2, 16, D), BF16),
            pltpu.VMEM((4, 2, 4, 16, D), BF16),
            pltpu.VMEM((4, 2, 3, 16, D), BF16),
            pltpu.VMEM((8, 16, D), BF16),
            pltpu.VMEM((8, 16, D), BF16),
            dma((6,)), dma((2, 16)), dma((2, 16)), dma((16,)), dma((16,)),
            dma((4, 2, 2)), dma((4, 2, 2)),
            dma((4, 2, 2, 3)), dma((4, 2, 2, 3)),
            dma((4, 2, 3)), dma((4, 2, 3)),
            dma((8,)), dma((8,)),
        ],
        compiler_params=pltpu.CompilerParams(
            collective_id=0, has_side_effects=True, vmem_limit_bytes=63 * 1024 * 1024
        ),
    )(tokens, cotangent, norm_gain.reshape(1, D), query_weight, key_weight, value_weight, out_weight)
    grad, sums = pl.pallas_call(
        hand_over,
        out_shape=(
            jax.ShapeDtypeStruct((LOCAL, GROUP, D), BF16),
            jax.ShapeDtypeStruct((16, D), F32),
        ),
        in_specs=[anywhere, anywhere],
        out_specs=(anywhere, anywhere),
        scratch_shapes=[pltpu.VMEM((LOCAL, GROUP, D), BF16), pltpu.VMEM((16, D), F32), dma((2, 5))],
        compiler_params=pltpu.CompilerParams(vmem_limit_bytes=62 * 1024 * 1024),
    )(grad, sums)
    return grad, sums.T


def solution(mesh):
    in_specs = (P("tm", "space", None), P("tm", "space", None), P(), P(), P(), P(), P())
    out_specs = (P("tm", "space", None), P(None, ("tm", "space")))
    return jax.shard_map(shards, mesh=mesh, in_specs=in_specs, out_specs=out_specs, check_vma=False)
```

```python
import functools
import math

import jax
import jax.numpy as jnp
from jax import lax
from jax.experimental import pallas as pl
from jax.experimental.pallas import tpu as pltpu
from jax.sharding import PartitionSpec as P

H = 16
D = 1024
HEAD = D // H
PAIRS = H // 2
LOCAL = 24
GROUP = 16
FRAMES = LOCAL * GROUP
TILES = D // 128
EPS = 1e-06
EARLY = 256
LATE = FRAMES - EARLY
OFFSETS = (
    (0, 0), (0, 1), (0, 2), (0, 3),
    (1, 0), (3, 0), (1, 1), (3, 1), (1, 2), (3, 2), (1, 3),
    (3, 3), (2, 0), (2, 1), (2, 2), (2, 3),
)
SEND_ORDER = tuple(range(4, 11)) + (1, 2, 3) + tuple(range(11, 16))
X_FIRST = ((False, True), (True, True), (True, False), (True, False))
MESH = pl.DeviceIdType.MESH
BF16 = jnp.bfloat16
F32 = jnp.float32


def nn(left, right):
    return lax.dot_general(left, right, (((1,), (0,)), ((), ())), preferred_element_type=F32)


def nt(left, right):
    return lax.dot_general(left, right, (((1,), (1,)), ((), ())), preferred_element_type=F32)


def tn(left, right):
    return lax.dot_general(left, right, (((0,), (0,)), ((), ())), preferred_element_type=F32)


def place():
    tm = lax.axis_index("tm")
    space = lax.axis_index("space")
    return (tm // 4) * 2 + space // 8, tm % 4, (space // 2) % 4, space % 2


def device(z, y, x, core):
    return ((z // 2) * 4 + y, ((z % 2) * 4 + x) * 2 + core)


def remote(src, dst, send, recv, to):
    return pltpu.make_async_remote_copy(
        src_ref=src, dst_ref=dst, send_sem=send, recv_sem=recv, device_id=to, device_id_type=MESH
    )


def loop(count, body, unroll=1):
    def step(i, carry):
        body(i)
        return carry

    lax.fori_loop(0, count, step, 0, unroll=unroll)


def kernel(
    scale,
    tokens, cotangent, gain, wq_hbm, wk_hbm, wv_hbm, wo_hbm,
    grad_ref, sums_ref,
    raw, turn, x_out, dy_out, x_in, dy_in, back_out, back_in, result, stats,
    wq, wk, wv, wo,
    normed, query, key, value, mixed, dy, grad_mixed, grad_query, grad_key, grad_value,
    weights, lows, low_early,
    part, pair, first_in, first_fwd, mid, second_in, last, last_in,
    load_sem, in_send, in_recv, back_send, back_recv,
    core_send, core_recv, first_send, first_recv, second_send, second_recv, z_send, z_recv,
):
    z, y, x, core = place()
    z_hi, z_lo = z // 2, z % 2
    me = z_hi * 4 + y
    partner = device(z, y, x, 1 - core)
    x_next, x_prev = device(z, y, (x + 1) % 4, core), device(z, y, (x + 3) % 4, core)
    y_next, y_prev = device(z, (y + 1) % 4, x, core), device(z, (y + 3) % 4, x, core)

    def member(i, sign):
        a, b = OFFSETS[i]
        to_z, to_y = (z_hi + 4 + sign * a) % 4, (y + 4 + sign * b) % 4
        return to_z * 4 + to_y, device(to_z * 2 + z_lo, to_y, x, core)

    loads = [
        pltpu.make_async_copy(tokens, raw.at[0], load_sem.at[0]),
        pltpu.make_async_copy(cotangent, raw.at[1], load_sem.at[1]),
        pltpu.make_async_copy(wq_hbm, wq, load_sem.at[2]),
        pltpu.make_async_copy(wk_hbm, wk, load_sem.at[3]),
        pltpu.make_async_copy(wv_hbm, wv, load_sem.at[4]),
        pltpu.make_async_copy(wo_hbm, wo, load_sem.at[5]),
    ]
    loads[0].start()

    barrier = pltpu.get_barrier_semaphore()
    peers = [member(i, 1)[1] for i in range(1, GROUP)]
    peers += [partner, x_next, x_prev, device(z, y, (x + 2) % 4, core)] + [device((z + o) % 8, y, x, core) for o in (1, 3, 5, 7)]
    for peer in peers:
        pl.semaphore_signal(barrier, inc=1, device_id=peer, device_id_type=MESH)

    def positions_first(which, target):
        def frame(f):
            rows = raw[which, f].astype(F32)
            for t in range(TILES):
                turn[pl.ds(pl.multiple_of(t * FRAMES + f * GROUP, 16), GROUP), :] = rows[:, t * 128:(t + 1) * 128]

        loop(LOCAL, frame, 4)

        def position(p):
            rows = [turn[pl.ds(t * FRAMES + p, LOCAL, stride=GROUP), :] for t in range(TILES)]
            target[p] = jnp.concatenate(rows, 1).astype(BF16)

        loop(GROUP, position, 4)

    def in_copy(which, i):
        to, peer = member(i, 1)
        source, target = ((x_out, x_in), (dy_out, dy_in))[which]
        return remote(source.at[to], target.at[i], in_send.at[which, i], in_recv.at[which, i], peer)

    loads[0].wait()
    for load in loads[1:]:
        load.start()
    positions_first(0, x_out)
    pl.semaphore_wait(barrier, len(peers))
    for i in SEND_ORDER:
        in_copy(0, i).start()
    x_in[0] = x_out[me]
    loads[1].wait()
    positions_first(1, dy_out)
    for i in SEND_ORDER:
        in_copy(1, i).start()
    dy_in[0] = dy_out[me]

    def normalise(i):
        rows = []
        for j in range(2):
            floated = x_in[2 * i + j].astype(F32)
            mean = jnp.mean(floated, -1, keepdims=True)
            centred = floated - mean
            inv_scale = lax.rsqrt(jnp.mean(centred * centred, -1, keepdims=True) + EPS)
            stats[0, 2 * i + j] = jnp.broadcast_to(mean, (LOCAL, 128))
            stats[1, 2 * i + j] = jnp.broadcast_to(inv_scale, (LOCAL, 128))
            rows.append(centred * inv_scale * gain[...])
        normed[pl.ds(i * 48, 48), :] = jnp.concatenate(rows, 0).astype(BF16)

    def project(start, count):
        def block(n):
            columns = pl.ds(pl.multiple_of(n * 256, 256), 256)
            rows = normed[start:start + count, :]
            query[start:start + count, columns] = (nn(rows, wq[:, columns]) * (1.0 / math.sqrt(HEAD))).astype(BF16)
            key[start:start + count, columns] = nn(rows, wk[:, columns]).astype(BF16)
            value[start:start + count, columns] = nn(rows, wv[:, columns]).astype(BF16)

        loop(4, block, 4)

    for i in range(GROUP // 2):
        for j in range(2):
            if i + j > 0:
                in_copy(0, 2 * i + j).wait_recv()
        if i == 0:
            for load in loads[2:5]:
                load.wait()
        normalise(i)
        if 48 * i < EARLY <= 48 * (i + 1):
            project(0, EARLY)
    project(EARLY, LATE)

    def spread(rows):
        first = lax.broadcasted_iota(jnp.int32, rows.shape, 1) < HEAD
        zero = jnp.zeros_like(rows)
        return jnp.concatenate([jnp.where(first, rows, zero), jnp.where(first, zero, rows)], 0)

    def merge(both):
        count = both.shape[0] // 2
        first = lax.broadcasted_iota(jnp.int32, (count, 128), 1) < HEAD
        return jnp.where(first, both[:count], both[count:])

    def pair_columns(p):
        return pl.ds(pl.multiple_of(p * 128, 128), 128)

    def forward(p):
        columns = pair_columns(p)
        spread_query = spread(query[:, columns])
        keys = key[:, columns]
        values, outs = value[:, columns], []
        for c in range(3):
            part_rows = slice(c * 256, (c + 1) * 256)
            scores = nt(keys, spread_query[part_rows])
            raised = jnp.exp(scores - jnp.max(scores, 0, keepdims=True))
            shares = raised * (1.0 / jnp.sum(raised, 0, keepdims=True))
            weights[p, :, part_rows] = shares
            shares = shares.astype(BF16)
            lows[p, :, part_rows] = shares
            outs.append(tn(shares, values))
        mixed[:, columns] = merge(jnp.concatenate(outs, 0)).astype(BF16)

    loop(PAIRS, forward, 8)

    def gather_dy(i):
        rows = [dy_in[2 * i + j].astype(F32) for j in range(2)]
        dy[pl.ds(i * 48, 48), :] = jnp.concatenate(rows, 0).astype(BF16)

    def project_back(start, count):
        def block(n):
            columns = pl.ds(pl.multiple_of(n * 256, 256), 256)
            grad_mixed[start:start + count, columns] = nt(dy[start:start + count, :], wo[columns, :]).astype(BF16)

        loop(4, block, 4)

    early_slots = -(-EARLY // LOCAL)
    for i in range(1, early_slots):
        in_copy(1, i).wait_recv()
    for i in range(EARLY // 48):
        gather_dy(i)
    dy[EARLY // 48 * 48:EARLY, :] = dy_in[early_slots - 1][:EARLY - LOCAL * (early_slots - 1)]
    loads[5].wait()
    project_back(0, EARLY)

    def backward_early(p):
        columns = pair_columns(p)
        spread_grad = spread(grad_mixed[:EARLY, columns])
        values, keys = value[:, columns], key[:, columns]
        both = []
        for c in range(2):
            at = slice(c * FRAMES, c * FRAMES + EARLY)
            grad_weights = nt(values, spread_grad[c * EARLY:(c + 1) * EARLY])
            shares = weights[p, :, at]
            delta = jnp.sum(shares * grad_weights, 0, keepdims=True)
            scores = shares * (grad_weights - delta)
            scores = scores.astype(BF16)
            low_early[p, :, c * EARLY:(c + 1) * EARLY] = scores
            both.append(tn(scores, keys))
        first = lax.broadcasted_iota(jnp.int32, (EARLY, 128), 1) < HEAD
        grad_query[:EARLY, columns] = (jnp.where(first, both[0], both[1]) * (1.0 / math.sqrt(HEAD))).astype(BF16)

    loop(PAIRS, backward_early, 8)

    for i in range(early_slots, GROUP):
        in_copy(1, i).wait_recv()
    for i in range(EARLY // 48, GROUP // 2):
        gather_dy(i)
    def backward_value(p):
        columns = pair_columns(p)
        grad_value[:, columns] = nn(lows[p], spread(grad_mixed[:, columns])).astype(BF16)

    def backward_late(p):
        columns = pair_columns(p)
        values, keys = value[:, columns], key[:, columns]
        grad_weights = nt(values, spread(grad_mixed[EARLY:, columns]))
        shares = jnp.concatenate([weights[p, :, EARLY:FRAMES], weights[p, :, FRAMES + EARLY:]], 1)
        delta = jnp.sum(shares * grad_weights, 0, keepdims=True)
        scores = (shares * (grad_weights - delta)).astype(BF16)
        grad_query[EARLY:, columns] = (merge(tn(scores, keys)) * (1.0 / math.sqrt(HEAD))).astype(BF16)
        pieces = []
        for c in range(2):
            pieces.append(low_early[p, :, c * EARLY:(c + 1) * EARLY])
            pieces.append(scores[:, c * LATE:(c + 1) * LATE])
        grad_key[:, columns] = nn(jnp.concatenate(pieces, 1), spread(query[:, columns])).astype(BF16)

    lefts = [grad_query, grad_key, grad_value, dy]
    rights = [normed, normed, normed, mixed]

    def core_copy(w, h, r):
        rows = pl.ds(r, 2)
        return remote(
            part.at[w, rows, h, :, 1 - core], pair.at[w, rows, h],
            core_send.at[w, h, r // 2], core_recv.at[w, h, r // 2], partner,
        )

    def product(w, h):
        left = lefts[w]
        for r in (0, 2):
            rows = [left[:, (r + j) * 256 + h * 128:(r + j) * 256 + h * 128 + 128] for j in range(2)]
            total = tn(jnp.concatenate(rows, 1), rights[w][...]).astype(BF16).reshape(2, 4, 2, 16, D)
            for j in range(2):
                part[w, r + j, h] = total[j]
            core_copy(w, h, r).start()

    def first_axis(w, h):
        return (x, x_next, x_prev) if X_FIRST[w][h] else (y, y_next, y_prev)

    def held(w, h, i, s):
        return pair.at[w, pl.ds(2 * s, 2), h, i] if X_FIRST[w][h] else pair.at[w, i, h, pl.ds(2 * s, 2)]

    def start_unit(w, h):
        for half in (0, 2):
            core_copy(w, h, half).wait_recv()

            def add(n):
                r, c = half + n // 4, n % 4
                pair[w, r, h, c] = (part[w, r, h, c, core].astype(F32) + pair[w, r, h, c].astype(F32)).astype(BF16)

            loop(8, add, 4)
        for k in range(4):
            first_ring(w, h, k).start()

    def ring(axis, source, inbox, forwarded, send, recv, k):
        at, after, before = axis
        to, d, slot = (after, before)[k % 2], k % 2, k // 2
        if slot == 0:
            block = source((at + 2) % 4, d)
        elif slot == 1:
            block = source((at + (1, 3)[d]) % 4, 1 - d)
        else:
            block = forwarded.at[d]
        return remote(block, inbox.at[d, slot], send.at[d, slot], recv.at[d, slot], to)

    def first_ring(w, h, k):
        return ring(
            first_axis(w, h), lambda i, s: held(w, h, i, s), first_in.at[w, h], first_fwd.at[w, h],
            first_send.at[w, h], first_recv.at[w, h], k,
        )

    def second_copy(w, h, o):
        at = (y if X_FIRST[w][h] else x) + o
        to = device(z, at % 4, x, core) if X_FIRST[w][h] else device(z, y, at % 4, core)
        return remote(
            mid.at[w, h, at % 4], second_in.at[w, h, o - 1], second_send.at[w, h, o - 1], second_recv.at[w, h, o - 1], to
        )

    def forward_first(w, h):
        at = first_axis(w, h)[0]
        for d in range(2):
            first_ring(w, h, d).wait_recv()
            own = held(w, h, (at + (1, 3)[d]) % 4, d)[...]
            first_fwd[w, h, d] = (first_in[w, h, d, 0].astype(F32) + own.astype(F32)).astype(BF16)
            first_ring(w, h, 4 + d).start()

    def finish_first(w, h):
        at = first_axis(w, h)[0]
        for k in range(2, 6):
            first_ring(w, h, k).wait_recv()
        for s in range(2):
            mid[w, h, 2 * s:2 * s + 2] = (
                held(w, h, at, s)[...].astype(F32)
                + first_in[w, h, s, 2].astype(F32) + first_in[w, h, 1 - s, 1].astype(F32)
            ).astype(BF16)
        for o in (2, 1, 3):
            second_copy(w, h, o).start()

    def z_copy(w, h):
        to = 2 * w + h
        slot = (to + 8 - z) % 8
        return remote(
            last.at[to], last_in.at[slot], z_send.at[to], z_recv.at[slot], device(to, y, x, core)
        )

    def finish_second(w, h):
        total = mid[w, h, y if X_FIRST[w][h] else x].astype(F32)
        for o in range(1, 4):
            second_copy(w, h, o).wait_recv()
            total = total + second_in[w, h, o - 1].astype(F32)
        last[2 * w + h] = total.astype(BF16)

        @pl.when(z != 2 * w + h)
        def _():
            z_copy(w, h).start()

    def unproject(start, count):
        def block(n):
            columns = pl.ds(pl.multiple_of(n * 256, 256), 256)
            total = nt(grad_query[start:start + count, :], wq[columns, :])
            total = total + nt(grad_key[start:start + count, :], wk[columns, :])
            total = total + nt(grad_value[start:start + count, :], wv[columns, :])
            total = total * gain[:, columns]
            for t in range(2):
                row = pl.multiple_of((2 * n + t) * FRAMES + start, 8)
                turn[pl.ds(row, count), :] = total[:, t * 128:(t + 1) * 128]

        loop(4, block, 4)

    def rows_back(i):
        mean = stats[0, i][:, :1]
        inv_scale = stats[1, i][:, :1]
        standard = (x_in[i].astype(F32) - mean) * inv_scale
        tiles = [turn[pl.ds(t * FRAMES + i * LOCAL, LOCAL), :] for t in range(TILES)]
        grad_standard = jnp.concatenate(tiles, 1)
        grad = dy_in[i].astype(F32) + inv_scale * (
            grad_standard
            - jnp.mean(grad_standard, -1, keepdims=True)
            - standard * jnp.mean(grad_standard * standard, -1, keepdims=True)
        )
        back_out[i] = grad.astype(BF16)

    def back_copy(i):
        _, peer = member(i, -1)
        return remote(back_out.at[i], back_in.at[me], back_send.at[i], back_recv.at[i], peer)

    def send_back(i):
        rows_back(i)
        back_copy(i).start()

    firsts, evens, odds = ((3, 0), (3, 1), (2, 0), (2, 1)), ((1, 0), (0, 0)), ((1, 1), (0, 1))
    for unit in firsts[:2]:
        product(*unit)
    project_back(EARLY, LATE)
    loop(PAIRS, backward_value, 8)
    for unit in firsts[2:]:
        product(*unit)
    for unit in firsts[:2]:
        start_unit(*unit)
    loop(PAIRS // 2, lambda i: backward_late(2 * i), 4)
    for unit in firsts[2:]:
        start_unit(*unit)
    for unit in evens:
        product(*unit)
    for unit in firsts[:2]:
        forward_first(*unit)
    loop(PAIRS // 2, lambda i: backward_late(2 * i + 1), 4)
    for unit in evens:
        start_unit(*unit)
    for unit in odds:
        product(*unit)
    for unit in firsts[2:]:
        forward_first(*unit)
    unproject(FRAMES // 2, FRAMES // 2)
    for unit in odds:
        start_unit(*unit)
    for i in range(GROUP // 2, GROUP):
        send_back(i)
    for unit in evens:
        forward_first(*unit)
    for unit in firsts[:2]:
        finish_first(*unit)
    unproject(0, FRAMES // 2)
    for i in list(range(4, GROUP // 2)) + [1, 2, 3]:
        send_back(i)
    rows_back(0)
    for unit in firsts[2:]:
        finish_first(*unit)
    for unit in firsts[:2]:
        finish_second(*unit)
    forward_first(*odds[0])
    for unit in evens:
        finish_first(*unit)
    forward_first(*odds[1])
    for unit in firsts[2:]:
        finish_second(*unit)
    finish_first(*odds[0])
    for unit in evens:
        finish_second(*unit)
    finish_first(*odds[1])
    for unit in odds:
        finish_second(*unit)

    back_in[me] = back_out[0]
    for i in range(1, GROUP):
        back_copy(i).wait_recv()

    def position_out(p):
        rows = back_in[p].astype(F32)
        for t in range(TILES):
            turn[pl.ds(t * FRAMES + p, LOCAL, stride=GROUP), :] = rows[:, t * 128:(t + 1) * 128]

    loop(GROUP, position_out, 4)

    def frame_out(f):
        rows = [turn[pl.ds(pl.multiple_of(t * FRAMES + f * GROUP, 16), GROUP), :] for t in range(TILES)]
        result[f] = jnp.concatenate(rows, 1).astype(BF16)

    loop(LOCAL, frame_out, 4)
    store = pltpu.make_async_copy(result, grad_ref, load_sem.at[0])
    store.start()

    total = last[z].astype(F32)
    for o in range(1, 8):
        remote(
            last.at[0], last_in.at[o], z_send.at[0], z_recv.at[o], device((z + o) % 8, y, x, core)
        ).wait_recv()
        total = total + last_in[o].astype(F32)
    sums_ref[...] = total * scale
    store.wait()

    for i in range(1, GROUP):
        in_copy(0, i).wait_send()
        in_copy(1, i).wait_send()
        back_copy(i).wait_send()
    for w in range(4):
        for h in range(2):
            core_copy(w, h, 0).wait_send()
            core_copy(w, h, 2).wait_send()
            for k in range(6):
                first_ring(w, h, k).wait_send()
            for o in range(1, 4):
                second_copy(w, h, o).wait_send()

            @pl.when(z != 2 * w + h)
            def _():
                z_copy(w, h).wait_send()


def hand_over(grad, sums, grad_out, sums_out, held, held_sums, sem):
    steps = [(grad.at[pl.ds(6 * i, 6)], held.at[pl.ds(6 * i, 6)], grad_out.at[pl.ds(6 * i, 6)]) for i in range(4)]
    steps.append((sums, held_sums, sums_out))
    inward = [pltpu.make_async_copy(step[0], step[1], sem.at[0, i]) for i, step in enumerate(steps)]
    outward = [pltpu.make_async_copy(step[1], step[2], sem.at[1, i]) for i, step in enumerate(steps)]
    for copy in inward:
        copy.start()
    for copy, onward in zip(inward, outward):
        copy.wait()
        onward.start()
    for onward in outward:
        onward.wait()


def shards(tokens, cotangent, norm_gain, query_weight, key_weight, value_weight, out_weight):
    total_rows = FRAMES * lax.axis_size("tm") * lax.axis_size("space")
    anywhere = pl.BlockSpec(memory_space=pl.ANY)
    vmem = pl.BlockSpec(memory_space=pltpu.VMEM)
    dma = pltpu.SemaphoreType.DMA
    rows = pltpu.VMEM((FRAMES, D), BF16)
    block = pltpu.VMEM((GROUP, LOCAL, D), BF16)
    weight = pltpu.VMEM((D, D), BF16)
    grad, sums = pl.pallas_call(
        functools.partial(kernel, 1.0 / math.sqrt(total_rows)),
        out_shape=(
            jax.ShapeDtypeStruct((LOCAL, GROUP, D), BF16),
            jax.ShapeDtypeStruct((16, D), F32),
        ),
        in_specs=[anywhere, anywhere, vmem] + [anywhere] * 4,
        out_specs=(anywhere, vmem),
        scratch_shapes=[
            pltpu.VMEM((2, LOCAL, GROUP, D), BF16),
            pltpu.VMEM((TILES * FRAMES, 128), F32),
            block, block, block, block, block, block,
            pltpu.VMEM((LOCAL, GROUP, D), BF16),
            pltpu.VMEM((2, GROUP, LOCAL, 128), F32),
            weight, weight, weight, weight,
            rows, rows, rows, rows, rows, rows, rows, rows, rows, rows,
            pltpu.VMEM((PAIRS, FRAMES, 2 * FRAMES), F32),
            pltpu.VMEM((PAIRS, FRAMES, 2 * FRAMES), BF16),
            pltpu.VMEM((PAIRS, FRAMES, 2 * EARLY), BF16),
            pltpu.VMEM((4, 4, 2, 4, 2, 16, D), BF16),
            pltpu.VMEM((4, 4, 2, 4, 16, D), BF16),
            pltpu.VMEM((4, 2, 2, 3, 2, 16, D), BF16),
            pltpu.VMEM((4, 2, 2, 2, 16, D), BF16),
            pltpu.VMEM((4, 2, 4, 16, D), BF16),
            pltpu.VMEM((4, 2, 3, 16, D), BF16),
            pltpu.VMEM((8, 16, D), BF16),
            pltpu.VMEM((8, 16, D), BF16),
            dma((6,)), dma((2, 16)), dma((2, 16)), dma((16,)), dma((16,)),
            dma((4, 2, 2)), dma((4, 2, 2)),
            dma((4, 2, 2, 3)), dma((4, 2, 2, 3)),
            dma((4, 2, 3)), dma((4, 2, 3)),
            dma((8,)), dma((8,)),
        ],
        compiler_params=pltpu.CompilerParams(
            collective_id=0, has_side_effects=True, vmem_limit_bytes=63 * 1024 * 1024
        ),
    )(tokens, cotangent, norm_gain.reshape(1, D), query_weight, key_weight, value_weight, out_weight)
    grad, sums = pl.pallas_call(
        hand_over,
        out_shape=(
            jax.ShapeDtypeStruct((LOCAL, GROUP, D), BF16),
            jax.ShapeDtypeStruct((16, D), F32),
        ),
        in_specs=[anywhere, anywhere],
        out_specs=(anywhere, anywhere),
        scratch_shapes=[pltpu.VMEM((LOCAL, GROUP, D), BF16), pltpu.VMEM((16, D), F32), dma((2, 5))],
        compiler_params=pltpu.CompilerParams(vmem_limit_bytes=62 * 1024 * 1024),
    )(grad, sums)
    return grad, sums.T


def solution(mesh):
    in_specs = (P("tm", "space", None), P("tm", "space", None), P(), P(), P(), P(), P())
    out_specs = (P("tm", "space", None), P(None, ("tm", "space")))
    return jax.shard_map(shards, mesh=mesh, in_specs=in_specs, out_specs=out_specs, check_vma=False)
```
